32 devices in a mesh: dp: 8 (over z, y), mp: 4 (over x, core).
Axes of the slice: x: 2, y: 2, z: 4, core: 2. Of those that a mesh axis runs over, the one named last changes fastest.
Arguments:
- tokens: bfloat16 [32768, 1024], P(('dp', 'mp')), may hold values from -6 to 6
- out_grad: bfloat16 [32768, 1024], P(('dp', 'mp')), may hold values from -6 to 6
- item_counts: int32 [8], P('dp'), may hold values from 1 to 2, as said below
- group_dataset: int32 [8], P('dp'), may hold values from 0 to 5
- variable_mask: int32 [6, 48], replicated, may hold values from 0 to 1, as said below
- first_gain: float32 [1024], replicated, may hold values from 0.5 to 1.5
- first_shift: float32 [1024], replicated, may hold values from -1.75 to 1.75
- input_weight: bfloat16 [3, 1024, 1024], P(None, None, 'mp'), may hold values from -0.1875 to 0.1875
- input_bias: float32 [2, 1024], P(None, 'mp'), may hold values from -3 to 3
- output_weight: bfloat16 [1024, 1024], P('mp'), may hold values from -2 to 2
- output_bias: float32 [1024], replicated, may hold values from -3 to 3
- second_gain: float32 [1024], replicated, may hold values from 0.5 to 1.5
- second_shift: float32 [1024], replicated, may hold values from -1.75 to 1.75
- up_weight: bfloat16 [1024, 4096], P(None, 'mp'), may hold values from -0.1875 to 0.1875
- up_bias: float32 [4096], P('mp'), may hold values from -3 to 3
- down_weight: bfloat16 [4096, 1024], P('mp'), may hold values from -0.09375 to 0.09375
- down_bias: float32 [1024], replicated, may hold values from -3 to 3
Outputs:
- result: bfloat16 [32768, 1024], P(('dp', 'mp'))
- token_grad: bfloat16 [32768, 1024], P(('dp', 'mp'))
- first_gain_grad: float32 [1024], replicated
- first_shift_grad: float32 [1024], replicated
- input_weight_grad: float32 [3, 1024, 1024], P(None, None, 'mp')
- input_bias_grad: float32 [2, 1024], P(None, 'mp')
- output_weight_grad: float32 [1024, 1024], P('mp')
- output_bias_grad: float32 [1024], replicated
- second_gain_grad: float32 [1024], replicated
- second_shift_grad: float32 [1024], replicated
- up_weight_grad: float32 [1024, 4096], P(None, 'mp')
- up_bias_grad: float32 [4096], P('mp')
- down_weight_grad: float32 [4096, 1024], P('mp')
- down_bias_grad: float32 [1024], replicated
The draws below stay inside these ranges and needn't reach their ends.
Inputs may be any that keep to these rules, and one draw needn't show every extreme that they name: `item_counts`: every draw has some group with exactly 2 items in use. `variable_mask`: each row is a run of ones then zeros, with 30 to 48 ones; some row has 48 ones and some row 30.
All inputs are finite; a program needn't handle non-finite values.
Results may differ from the reference program's by a relative error of at most 0.012.
The reference program's roundings to bfloat16 on the way count: a program that leaves them out, or rounds other values in their place, can miss the bound.
Values may be sent and summed in bfloat16 or wider, within the bound.
No kernel may reach another device: no remote copies, remote signals or barrier semaphores. Data moves between devices by JAX's collectives and lax.ppermute only.
A program may use at most 256 MiB of HBM per device.

```python
import jax
import jax.numpy as jnp
from jax import lax

D = 1024
HEADS = 16
HEAD_DIM = 64
FF = 4096
SEQ = 2048
ITEMS_DEV = 2
NSETS = 6
VARS = 48
GROUPS = 8
TOKENS = 32768


def draw_item_counts(key, part):
    key = jax.random.fold_in(key, 11)
    light_key, heavy_key, chosen_key = jax.random.split(key, 3)
    light_counts = jnp.minimum(jax.random.randint(light_key, (GROUPS,), 1, 3), ITEMS_DEV)
    heavy_flags = jax.random.randint(heavy_key, (GROUPS,), 0, 8) == 0
    chosen_group = jax.random.randint(chosen_key, (), 0, GROUPS)
    counts_out = jnp.where(heavy_flags, ITEMS_DEV, light_counts)
    counts_out = jnp.where(jnp.arange(GROUPS) == chosen_group, ITEMS_DEV, counts_out)
    return counts_out.astype(jnp.int32)


def draw_variable_mask(key, part):
    key = jax.random.fold_in(key, 23)
    var_counts = jax.random.randint(key, (NSETS,), 30, VARS + 1)
    var_counts = var_counts.at[0].set(VARS).at[1].set(30)
    return (jnp.arange(VARS)[None, :] < var_counts[:, None]).astype(jnp.int32)


def with_ends(result, rng, smallest, top_value):
    shape = result.shape
    spot = [jax.random.randint(jax.random.fold_in(rng, axis), (), 0, shape[axis]) for axis in range(len(shape))]
    result = result.at[tuple(spot)].set(smallest)
    longest = shape.index(max(shape))
    spot[longest] = (spot[longest] + 1) % shape[longest]
    return result.at[tuple(spot)].set(top_value)


def steps_of(stream_key, shape, shards, low, high):
    loudness = 1.0
    for dim, shards_of in shards:
        heights = jax.random.uniform(jax.random.fold_in(jax.random.fold_in(stream_key, 6), dim), (shards_of,), jnp.float32, low / len(shards), high / len(shards))
        loudness = loudness * jnp.repeat(jnp.exp(heights), shape[dim] // shards_of).reshape((-1,) + (1,) * (len(shape) - 1 - dim))
    return loudness


def noise(rng, shape, deviation, bound, cuts=(), kind=jnp.bfloat16):
    array = deviation * jax.random.normal(rng, shape, jnp.float32)
    if cuts:
        array = array * steps_of(rng, shape, cuts, -0.22, 0.18)
    return jnp.clip(array, -bound, bound).astype(kind)


def setup_inputs(seed: int = 0) -> dict:
    key_of = jax.random.split(jax.random.key(seed), 18)
    tokens = noise(key_of[0], (TOKENS, D), 1.0, 6.0, ((0, 32),))
    out_grad = noise(key_of[1], (TOKENS, D), 1.0, 6.0, ((0, 32),))
    item_counts = draw_item_counts(jax.random.fold_in(key_of[17], 71), 0)
    group_dataset = with_ends(jax.random.randint(key_of[3], (GROUPS,), 0, NSETS), jax.random.fold_in(key_of[3], 1), 0, NSETS - 1).astype(jnp.int32)
    variable_mask = draw_variable_mask(jax.random.fold_in(key_of[17], 71), 0)
    first_gain = jnp.clip(1.0 + 0.1 * jax.random.normal(key_of[5], (D,), jnp.float32), 0.5, 1.5)
    first_shift = noise(key_of[6], (D,), 0.3, 1.75, (), jnp.float32)
    input_weight = noise(key_of[7], (3, D, D), D ** -0.5, 0.1875, ((2, 4),))
    input_bias = noise(key_of[8], (2, D), 0.5, 3.0, ((1, 4),), jnp.float32)
    output_weight = noise(key_of[9], (D, D), (max(SEQ // 256, 1)) ** -0.5, 2.0, ((0, 4),))
    output_bias = noise(key_of[10], (D,), 0.5, 3.0, (), jnp.float32)
    second_gain = jnp.clip(1.0 + 0.1 * jax.random.normal(key_of[11], (D,), jnp.float32), 0.5, 1.5)
    second_shift = noise(key_of[12], (D,), 0.3, 1.75, (), jnp.float32)
    up_weight = noise(key_of[13], (D, FF), D ** -0.5, 0.1875, ((1, 4),))
    up_bias = noise(key_of[14], (FF,), 0.5, 3.0, ((0, 4),), jnp.float32)
    down_weight = noise(key_of[15], (FF, D), FF ** -0.5, 0.09375, ((0, 4),))
    down_bias = noise(key_of[16], (D,), 0.5, 3.0, (), jnp.float32)
    return {"tokens": tokens, "out_grad": out_grad, "item_counts": item_counts, "group_dataset": group_dataset, "variable_mask": variable_mask, "first_gain": first_gain, "first_shift": first_shift, "input_weight": input_weight, "input_bias": input_bias, "output_weight": output_weight, "output_bias": output_bias, "second_gain": second_gain, "second_shift": second_shift, "up_weight": up_weight, "up_bias": up_bias, "down_weight": down_weight, "down_bias": down_bias}


norm_eps = 1e-06

@jax.custom_vjp
def low(v):
    return lax.optimization_barrier(v.astype(jnp.bfloat16)).astype(jnp.float32)

@jax.custom_vjp
def low_back(v):
    return v

def low_keep(v):
    return (low(v), None)

def low_pass(kept, grad):
    return (grad,)

def back_keep(v):
    return (v, None)

def back_low(kept, grad):
    return (low(grad),)
low.defvjp(low_keep, low_pass)
low_back.defvjp(back_keep, back_low)

def matmul(left_side, right_side):
    return jnp.dot(left_side, right_side, precision=lax.Precision.HIGHEST, preferred_element_type=jnp.float32)

def layer_norm(values, gain_vec, offset_vec):
    row_mean = lax.optimization_barrier(jnp.mean(values, axis=-1, keepdims=True))
    centered = values - row_mean
    variance = lax.optimization_barrier(jnp.mean(centered * centered, axis=-1, keepdims=True))
    return centered * lax.rsqrt(variance + norm_eps) * gain_vec + offset_vec

def attend_item(inputs):
    queries, key_rows, value_rows = inputs
    scores = jnp.einsum('qhd,khd->hqk', queries, key_rows, precision=lax.Precision.HIGHEST) * HEAD_DIM ** (-0.5)
    scores = low_back(scores)
    row_peak = lax.optimization_barrier(jnp.max(scores, axis=2, keepdims=True))
    weights = jnp.exp(scores - row_peak)
    probabilities = low(weights / lax.optimization_barrier(jnp.sum(weights, axis=2, keepdims=True)))
    attended = jnp.einsum('hqk,khd->qhd', probabilities, value_rows, precision=lax.Precision.HIGHEST)
    return low(low_back(attended))

def block_forward(row_values, params, active):
    first_gain, first_shift, input_weight, input_bias, output_weight, output_bias, second_gain, second_shift, up_weight, up_bias, down_weight, down_bias = params
    normed1 = low(layer_norm(row_values, first_gain, first_shift))
    queries = low(low_back(matmul(normed1, input_weight[0])) + input_bias[0])
    key_rows = low(low_back(matmul(normed1, input_weight[1])))
    value_rows = low(low_back(matmul(normed1, input_weight[2])) + input_bias[1])
    item_shape = (ITEMS_DEV, SEQ, HEADS, HEAD_DIM)
    attended = lax.map(jax.checkpoint(attend_item), (queries.reshape(item_shape), key_rows.reshape(item_shape), value_rows.reshape(item_shape)))
    merged = attended.reshape(ITEMS_DEV * SEQ, D)
    middle = row_values + low_back(matmul(merged, output_weight)) + output_bias
    normed2 = low(layer_norm(middle, second_gain, second_shift))
    hidden = low_back(matmul(normed2, up_weight)) + up_bias
    activated = low(jax.nn.gelu(hidden, approximate=False))
    return (middle + low_back(matmul(activated, down_weight)) + down_bias) * active[:, None]

def reference(tokens, out_grad, item_counts, group_dataset, variable_mask, first_gain, first_shift, input_weight, input_bias, output_weight, output_bias, second_gain, second_shift, up_weight, up_bias, down_weight, down_bias):
    params = tuple((member.astype(jnp.float32) for member in (first_gain, first_shift, input_weight, input_bias, output_weight, output_bias, second_gain, second_shift, up_weight, up_bias, down_weight, down_bias)))
    group_rows = ITEMS_DEV * SEQ
    var_totals = lax.optimization_barrier(jnp.sum(variable_mask, axis=1))
    patch_units = item_counts * var_totals[group_dataset]
    shares = patch_units.astype(jnp.float32) / jnp.sum(patch_units).astype(jnp.float32)
    rows_all = tokens.astype(jnp.float32).reshape(GROUPS, group_rows, D)
    cotangent_all = out_grad.astype(jnp.float32).reshape(GROUPS, group_rows, D)

    def one_group(running, slices):
        row_values, cotangent, item_count, group_share = slices
        active = (jnp.arange(group_rows, dtype=jnp.int32) // SEQ < item_count).astype(jnp.float32)

        def forward(rows_in, params_in):
            return block_forward(rows_in, params_in, active)
        outcome, pullback = jax.vjp(forward, row_values, params)
        row_grad, param_grads = pullback(cotangent)
        running = tuple((held + group_share * grad_part for held, grad_part in zip(running, param_grads)))
        return (running, (outcome.astype(jnp.bfloat16), row_grad.astype(jnp.bfloat16)))
    zeros_start = tuple((jnp.zeros_like(member) for member in params))
    totals, (outcomes, row_grads) = lax.scan(one_group, zeros_start, (rows_all, cotangent_all, item_counts, shares))
    return (outcomes.reshape(TOKENS, D), row_grads.reshape(TOKENS, D), totals[0], totals[1], totals[2], totals[3], totals[4], totals[5], totals[6], totals[7], totals[8], totals[9], totals[10], totals[11])
```

```python
import jax
import jax.numpy as jnp
from jax import lax
from jax.experimental import pallas as pl
from jax.experimental.pallas import tpu as pltpu
from jax.sharding import PartitionSpec as P

HEAD_DIM = 64
LANES = 128
norm_eps = 1e-06
SCALE = HEAD_DIM**-0.5
LOG2E = 1.4426950408889634
RSQRT2 = 0.7071067811865476
RSQRT2PI = 0.3989422804014327

bf16 = jnp.bfloat16
f32 = jnp.float32
NN = (((1,), (0,)), ((), ()))
NT = (((1,), (1,)), ((), ()))
TN = (((0,), (0,)), ((), ()))
VMEM_BYTES = 60 << 20


def dot(left, right, dims=NN):
    return lax.dot_general(left, right, dims, preferred_element_type=f32)


def shape(dims, dtype):
    return jax.ShapeDtypeStruct(dims, dtype)


def whole(array):
    rank = len(array.shape)
    return pl.BlockSpec(array.shape, lambda *_: (0,) * rank, pipeline_mode=pl.Buffered(1))


def scalars():
    return pl.BlockSpec(memory_space=pltpu.SMEM)


def call(kernel, name, grid, in_specs, out_specs, out_shape, scratch=(), flops=0, nbytes=0, exps=0):
    return pl.pallas_call(
        kernel,
        name=name,
        grid=grid,
        in_specs=in_specs,
        out_specs=out_specs,
        out_shape=out_shape,
        scratch_shapes=list(scratch),
        compiler_params=pltpu.CompilerParams(vmem_limit_bytes=VMEM_BYTES),
        cost_estimate=pl.CostEstimate(
            flops=int(flops), bytes_accessed=int(nbytes), transcendentals=int(exps)
        ),
    )


def split_two(values):
    high = values.astype(bf16)
    return high, (values - high.astype(f32)).astype(bf16)


def split_three(values):
    high = values.astype(bf16)
    rest = values - high.astype(f32)
    mid = rest.astype(bf16)
    return high, mid, (rest - mid.astype(f32)).astype(bf16)


def stat_rows(vector, rows):
    high, mid, rest = (part.astype(f32) for part in split_three(vector))
    row = lax.broadcasted_iota(jnp.int32, (rows, vector.shape[1]), 0)
    return jnp.where(
        row == 0, high, jnp.where(row == 1, mid, jnp.where(row == 2, rest, 0.0))
    ).astype(bf16)


def normalize(values):
    centered = values - jnp.mean(values, axis=-1, keepdims=True)
    variance = jnp.mean(centered * centered, axis=-1, keepdims=True)
    inverse = lax.rsqrt(variance + norm_eps)
    return centered * inverse, inverse


def norm_back(grad, gain, unit, inverse):
    scaled = grad * gain
    return inverse * (
        scaled
        - jnp.mean(scaled, axis=-1, keepdims=True)
        - unit * jnp.mean(scaled * unit, axis=-1, keepdims=True)
    )


def add_rows(ref, rows, first):
    @pl.when(first)
    def _():
        ref[...] = jnp.zeros_like(ref)

    for place, row in enumerate(rows):
        ref[place : place + 1, :] += row


def first_norm(tokens, out_grad, params, scal):
    rows, width = tokens.shape
    block = 256

    def kernel(scal_ref, tok_ref, grad_ref, par_ref, norm_ref, cot_ref):
        unit, _ = normalize(tok_ref[...].astype(f32))
        norm_ref[...] = (unit * par_ref[0:1, :] + par_ref[1:2, :]).astype(bf16)
        cot_ref[...] = (grad_ref[...].astype(f32) * scal_ref[0]).astype(bf16)

    spec = pl.BlockSpec((block, width), lambda i: (i, 0))
    return call(
        kernel,
        "first_norm",
        (rows // block,),
        [scalars(), spec, spec, whole(params)],
        [spec, spec],
        [shape((rows, width), bf16)] * 2,
        flops=20 * rows * width,
        nbytes=8 * rows * width,
    )(scal, tokens, out_grad, params)


def halves(block, width, count):
    own = pl.BlockSpec((block, width), lambda i, *_: (jnp.minimum(i, count - 1), 0))
    other = pl.BlockSpec((block, width), lambda i, *_: (jnp.maximum(i - count, 0), 0))
    return own, other


def pick(count, own_ref, other_ref):
    return jnp.where(pl.program_id(0) < count, own_ref[...], other_ref[...])


def project(norm_own, norm_other, weight, bias):
    rows, width = norm_own.shape
    cols = weight.shape[2]
    block = 512
    count = rows // block

    def kernel(own_ref, other_ref, w_ref, b_ref, q_ref, k_ref, v_ref):
        x = pick(count, own_ref, other_ref)
        q_ref[...] = (dot(x, w_ref[0]) + b_ref[0:1, :]).astype(bf16)
        k_ref[...] = dot(x, w_ref[1]).astype(bf16)
        v_ref[...] = (dot(x, w_ref[2]) + b_ref[1:2, :]).astype(bf16)

    out = pl.BlockSpec((block, cols), lambda i: (i, 0))
    return call(
        kernel,
        "project",
        (2 * count,),
        [*halves(block, width, count), whole(weight), whole(bias)],
        [out] * 3,
        [shape((2 * rows, cols), bf16)] * 3,
        flops=12 * rows * width * cols,
        nbytes=4 * rows * width + 6 * width * cols + 12 * rows * cols,
    )(norm_own, norm_other, weight, bias)


def attend_forward(queries, keys, values):
    rows, width = queries.shape
    block = min(1024, rows)
    chunk = 256
    steps = rows // chunk

    def kernel(q_ref, k_ref, v_ref, o_ref, ot_ref, lse_ref, k_two, v_turned):
        @pl.when(pl.program_id(1) == 0)
        def _():
            k = k_ref[...]
            lane = lax.broadcasted_iota(jnp.int32, k.shape, 1)
            rolled = pltpu.roll(k.astype(f32), HEAD_DIM, 1).astype(bf16)
            k_two[0] = jnp.where(lane < HEAD_DIM, k, rolled)
            k_two[1] = jnp.where(lane < HEAD_DIM, rolled, k)
            turned = v_ref[...].astype(f32).T
            ones = jnp.ones((HEAD_DIM, rows), bf16)
            v_turned[0] = jnp.concatenate([turned[:HEAD_DIM].astype(bf16), ones], 0)
            v_turned[1] = jnp.concatenate([ones, turned[HEAD_DIM:].astype(bf16)], 0)

        q_turned = q_ref[...].astype(f32).T * (SCALE * LOG2E)
        outs = []
        for head in range(2):
            at = head * HEAD_DIM
            q_two = jnp.concatenate(split_two(q_turned[at : at + HEAD_DIM]), 0)
            scores = [dot(k_two[head, pl.ds(j * chunk, chunk), :], q_two) for j in range(steps)]
            peak = None
            for part in scores:
                top = part.reshape(chunk // 8, 8, block).max(axis=0)
                peak = top if peak is None else jnp.maximum(peak, top)
            peak = jnp.max(peak, axis=0, keepdims=True)
            total = None
            for j in range(steps):
                weights = jnp.exp2(scores[j] - peak).astype(bf16)
                part = dot(v_turned[head, :, pl.ds(j * chunk, chunk)], weights)
                total = part if total is None else total + part
            row_sum = total[HEAD_DIM - at : HEAD_DIM - at + 1]
            outs.append(total[at : at + HEAD_DIM] / row_sum)
            lse_ref[head : head + 1, :] = peak + jnp.log2(row_sum)
        turned = jnp.concatenate(outs, 0)
        ot_ref[...] = turned
        o_ref[...] = turned.T.astype(bf16)

    by_query = pl.BlockSpec((block, LANES), lambda j, i: (i, j))
    by_key = pl.BlockSpec((rows, LANES), lambda j, i: (0, j))
    turned_spec = pl.BlockSpec((LANES, block), lambda j, i: (j, i))
    stat_spec = pl.BlockSpec((None, 8, block), lambda j, i: (j, 0, i))
    pairs = width // LANES
    return call(
        kernel,
        "attend_forward",
        (pairs, rows // block),
        [by_query, by_key, by_key],
        [by_query, turned_spec, stat_spec],
        [shape((rows, width), bf16), shape((width, rows), f32), shape((pairs, 8, rows), f32)],
        [pltpu.VMEM((2, rows, LANES), bf16), pltpu.VMEM((2, LANES, rows), bf16)],
        flops=16 * rows * rows * width,
        nbytes=12 * rows * width,
        exps=rows * rows * width // HEAD_DIM,
    )(queries, keys, values)


def attend_backward(queries, keys, values, out_grad, out_turned, stats):
    rows, width = queries.shape
    block = min(1024, rows)
    chunk = 256
    count = rows // block

    def kernel(
        q_ref, k_ref, v_ref, g_ref, ot_ref, lse_ref, dq_ref, dk_ref, dv_ref, sum_ref,
        k_wide, k_turned, v_wide, dk_acc, dv_acc,
    ):
        i = pl.program_id(1)

        @pl.when(i == 0)
        def _():
            k = k_ref[...]
            v = v_ref[...]
            lane = lax.broadcasted_iota(jnp.int32, k.shape, 1)
            k_rolled = pltpu.roll(k.astype(f32), HEAD_DIM, 1).astype(bf16)
            v_rolled = pltpu.roll(v.astype(f32), HEAD_DIM, 1).astype(bf16)
            ones = jnp.where(lane < 3, 1.0, 0.0).astype(bf16)
            k_wide[0] = jnp.concatenate([jnp.where(lane < HEAD_DIM, k, k_rolled), ones], 1)
            k_wide[1] = jnp.concatenate([jnp.where(lane < HEAD_DIM, k_rolled, k), ones], 1)
            tail = jnp.where(lane < HEAD_DIM + 3, 1.0, 0.0).astype(bf16)
            v_wide[0] = jnp.where(lane < HEAD_DIM, v, tail)
            v_wide[1] = jnp.where(lane < HEAD_DIM, v_rolled, tail)
            k_turned[...] = k.astype(f32).T.astype(bf16)
            dk_acc[...] = jnp.zeros_like(dk_acc)
            dv_acc[...] = jnp.zeros_like(dv_acc)
            sum_ref[...] = jnp.zeros_like(sum_ref)

        q_turned = q_ref[...].astype(f32).T
        q_low = q_turned.astype(bf16)
        q_turned = q_turned * (SCALE * LOG2E)
        g_turned = g_ref[...].astype(f32).T
        g_low = g_turned.astype(bf16)
        dqs = []
        for head in range(2):
            part = slice(head * HEAD_DIM, (head + 1) * HEAD_DIM)
            q_wide = jnp.concatenate(
                [*split_two(q_turned[part]), stat_rows(-lse_ref[head : head + 1, :], LANES)], 0
            )
            row_dot = jnp.sum(g_turned[part] * ot_ref[part, :], axis=0, keepdims=True)
            g_wide = jnp.concatenate([g_low[part], stat_rows(-row_dot, HEAD_DIM)], 0)
            dq = None
            for j in range(rows // chunk):
                at = pl.ds(j * chunk, chunk)
                probabilities = jnp.exp2(dot(k_wide[head, at, :], q_wide))
                shifted = dot(v_wide[head, at, :], g_wide)
                probs_low = probabilities.astype(bf16)
                score_grad = (probabilities * shifted).astype(bf16)
                dv_acc[part, at] += dot(g_low[part], probs_low, NT)
                dk_acc[part, at] += dot(q_low[part], score_grad, NT)
                add = dot(k_turned[part, at], score_grad)
                dq = add if dq is None else dq + add
            dqs.append(dq)
        dq = (jnp.concatenate(dqs, 0) * SCALE).T
        dq_ref[...] = dq.astype(bf16)
        sum_ref[0:1, :] += jnp.sum(dq, axis=0, keepdims=True)

        @pl.when(i == count - 1)
        def _():
            dk_ref[...] = (dk_acc[...] * SCALE).T.astype(bf16)
            dv = dv_acc[...].T
            dv_ref[...] = dv.astype(bf16)
            sum_ref[1:2, :] = jnp.sum(dv, axis=0, keepdims=True)

    by_query = pl.BlockSpec((block, LANES), lambda j, i: (i, j))
    by_key = pl.BlockSpec((rows, LANES), lambda j, i: (0, j))
    turned_spec = pl.BlockSpec((LANES, block), lambda j, i: (j, i))
    stat_spec = pl.BlockSpec((None, 8, block), lambda j, i: (j, 0, i))
    sum_spec = pl.BlockSpec((8, LANES), lambda j, i: (0, j))
    return call(
        kernel,
        "attend_backward",
        (width // LANES, count),
        [by_query, by_key, by_key, by_query, turned_spec, stat_spec],
        [by_query, by_key, by_key, sum_spec],
        [shape((rows, width), bf16)] * 3 + [shape((8, width), f32)],
        [
            pltpu.VMEM((2, rows, 2 * LANES), bf16),
            pltpu.VMEM((LANES, rows), bf16),
            pltpu.VMEM((2, rows, LANES), bf16),
            pltpu.VMEM((LANES, rows), f32),
            pltpu.VMEM((LANES, rows), f32),
        ],
        flops=40 * rows * rows * width,
        nbytes=20 * rows * width,
        exps=rows * rows * width // HEAD_DIM,
    )(queries, keys, values, out_grad, out_turned, stats)


def output_other(first, second, weight_one, weight_two):
    total, cols = first.shape
    rows = total // 2
    width = weight_one.shape[1]
    block = 512
    count = rows // block

    def kernel(a_ref, b_ref, wa_ref, wb_ref, out_ref):
        out_ref[...] = (dot(a_ref[...], wa_ref[...]) + dot(b_ref[...], wb_ref[...])).astype(bf16)

    spec = pl.BlockSpec((block, cols), lambda i: (i + count, 0))
    return call(
        kernel,
        "output_other",
        (count,),
        [spec, spec, whole(weight_one), whole(weight_two)],
        pl.BlockSpec((block, width), lambda i: (i, 0)),
        shape((rows, width), bf16),
        flops=4 * rows * cols * width,
        nbytes=4 * rows * cols + 2 * rows * width,
    )(first, second, weight_one, weight_two)


def output_own(tokens, first, second, weight_one, weight_two, received, params):
    rows, width = tokens.shape
    cols = first.shape[1]
    block = 256

    def kernel(t_ref, a_ref, b_ref, wa_ref, wb_ref, r_ref, par_ref, mid_ref, norm_ref):
        middle = (
            t_ref[...].astype(f32)
            + (dot(a_ref[...], wa_ref[...]) + dot(b_ref[...], wb_ref[...]) + r_ref[...].astype(f32))
            + par_ref[2:3, :]
        )
        mid_ref[...] = middle
        unit, _ = normalize(middle)
        norm_ref[...] = (unit * par_ref[3:4, :] + par_ref[4:5, :]).astype(bf16)

    spec = pl.BlockSpec((block, width), lambda i: (i, 0))
    thin = pl.BlockSpec((block, cols), lambda i: (i, 0))
    return call(
        kernel,
        "output_own",
        (rows // block,),
        [spec, thin, thin, whole(weight_one), whole(weight_two), spec, whole(params)],
        [spec, spec],
        [shape((rows, width), f32), shape((rows, width), bf16)],
        flops=4 * rows * cols * width,
        nbytes=4 * rows * cols + 10 * rows * width,
    )(tokens, first, second, weight_one, weight_two, received, params)


def feed_forward(norm_own, norm_other, cot_own, cot_other, up, bias, down, scal, earlier=None):
    rows, width = norm_own.shape
    hidden = up.shape[1]
    block = 256
    count = rows // block
    last = earlier is not None
    term_type = bf16 if last else f32

    def kernel(scal_ref, no_ref, nt_ref, co_ref, ct_ref, up_ref, b_ref, dn_ref, *refs):
        if last:
            ff_in, ng_in, ffo_ref, ngo_ref, fft_ref, ngt_ref, *refs = refs
        else:
            ff_ref, ng_ref, *refs = refs
        up_term, down_term, sum_ref, up_acc, down_acc = refs
        i = pl.program_id(0)

        @pl.when(i == 0)
        def _():
            up_acc[...] = jnp.zeros_like(up_acc)
            down_acc[...] = jnp.zeros_like(down_acc)
            sum_ref[...] = jnp.zeros_like(sum_ref)

        x = pick(count, no_ref, nt_ref)
        cot = pick(count, co_ref, ct_ref)
        h = dot(x, up_ref[...]) + b_ref[0:1, :]
        cdf = 0.5 * (1.0 + lax.erf(h * RSQRT2))
        act = (h * cdf).astype(bf16)
        slope = cdf + h * (RSQRT2PI * jnp.exp(-0.5 * h * h))
        ff = dot(act, dn_ref[...])
        grad = dot(cot, dn_ref[...], NT) * slope
        sum_ref[0:1, :] += jnp.sum(grad, axis=0, keepdims=True)
        low = grad.astype(bf16)
        ng = dot(low, up_ref[...], NT)
        up_acc[...] += dot(x, low, TN)
        down_acc[...] += dot(act, cot, TN)
        if last:
            ff = ff + ff_in[...]
            ng = ng + ng_in[...]

            @pl.when(i < count)
            def _():
                ffo_ref[...] = ff
                ngo_ref[...] = ng

            @pl.when(i >= count)
            def _():
                fft_ref[...] = ff.astype(bf16)
                ngt_ref[...] = ng.astype(bf16)
        else:
            ff_ref[...] = ff
            ng_ref[...] = ng

        @pl.when(i == 2 * count - 1)
        def _():
            units = scal_ref[1]
            up_term[...] = (up_acc[...] * units).astype(term_type)
            down_term[...] = (down_acc[...] * units).astype(term_type)
            sum_ref[...] = sum_ref[...] * units

    own, other = halves(block, width, count)
    every = pl.BlockSpec((block, width), lambda i: (i, 0))
    ins = [scalars(), own, other, own, other, whole(up), whole(bias), whole(down)]
    args = [scal, norm_own, norm_other, cot_own, cot_other, up, bias, down]
    if last:
        ins += [every, every]
        args += list(earlier)
        outs = [own, own, other, other]
        shapes = [shape((rows, width), f32)] * 2 + [shape((rows, width), bf16)] * 2
    else:
        outs = [every, every]
        shapes = [shape((2 * rows, width), f32)] * 2
    terms = [shape((width, hidden), term_type), shape((hidden, width), term_type)]
    sums = shape((8, hidden), f32)
    return call(
        kernel,
        "feed_forward",
        (2 * count,),
        ins,
        outs + [whole(terms[0]), whole(terms[1]), whole(sums)],
        shapes + terms + [sums],
        [pltpu.VMEM((width, hidden), f32), pltpu.VMEM((hidden, width), f32)],
        flops=24 * rows * width * hidden,
        nbytes=24 * rows * width + 12 * width * hidden,
        exps=4 * rows * hidden,
    )(*args)


def second_back(middle, grad_own, grad_received, cot, params, scal):
    rows, width = middle.shape
    block = 256
    last = rows // block - 1

    def kernel(scal_ref, mid_ref, go_ref, gr_ref, cot_ref, par_ref, out_ref, low_ref, sum_ref):
        i = pl.program_id(0)
        unit, inverse = normalize(mid_ref[...])
        grad = go_ref[...] + gr_ref[...].astype(f32)
        cot = cot_ref[...].astype(f32)
        out = cot + norm_back(grad, par_ref[3:4, :], unit, inverse)
        out_ref[...] = out
        low_ref[...] = out.astype(bf16)
        sums = [jnp.sum(v, axis=0, keepdims=True) for v in (grad * unit, grad, out, cot)]
        add_rows(sum_ref, sums, i == 0)

        @pl.when(i == last)
        def _():
            sum_ref[...] = sum_ref[...] * scal_ref[1]

    spec = pl.BlockSpec((block, width), lambda i: (i, 0))
    sums = shape((8, width), f32)
    return call(
        kernel,
        "second_back",
        (rows // block,),
        [scalars(), spec, spec, spec, spec, whole(params)],
        [spec, spec, whole(sums)],
        [shape((rows, width), f32), shape((rows, width), bf16), sums],
        flops=30 * rows * width,
        nbytes=18 * rows * width,
    )(scal, middle, grad_own, grad_received, cot, params)


def output_back(low_own, low_other, first, second, weight_one, weight_two, scal):
    rows, width = low_own.shape
    cols = first.shape[1]
    block = 512
    count = rows // block

    def kernel(
        scal_ref, lo_ref, lt_ref, a_ref, b_ref, wa_ref, wb_ref,
        ga_ref, gb_ref, ta_ref, tb_ref, acc_a, acc_b,
    ):
        i = pl.program_id(0)

        @pl.when(i == 0)
        def _():
            acc_a[...] = jnp.zeros_like(acc_a)
            acc_b[...] = jnp.zeros_like(acc_b)

        low = pick(count, lo_ref, lt_ref)
        ga_ref[...] = dot(low, wa_ref[...], NT).astype(bf16)
        gb_ref[...] = dot(low, wb_ref[...], NT).astype(bf16)
        acc_a[...] += dot(a_ref[...], low, TN)
        acc_b[...] += dot(b_ref[...], low, TN)

        @pl.when(i == 2 * count - 1)
        def _():
            ta_ref[...] = acc_a[...] * scal_ref[1]
            tb_ref[...] = (acc_b[...] * scal_ref[1]).astype(bf16)

    own, other = halves(block, width, count)
    thin = pl.BlockSpec((block, cols), lambda i: (i, 0))
    terms = [shape((cols, width), f32), shape((cols, width), bf16)]
    return call(
        kernel,
        "output_back",
        (2 * count,),
        [scalars(), own, other, thin, thin, whole(weight_one), whole(weight_two)],
        [thin, thin, whole(terms[0]), whole(terms[1])],
        [shape((2 * rows, cols), bf16)] * 2 + terms,
        [pltpu.VMEM((cols, width), f32)] * 2,
        flops=16 * rows * width * cols,
        nbytes=4 * rows * width + 16 * rows * cols,
    )(scal, low_own, low_other, first, second, weight_one, weight_two)


def input_term(norm_own, norm_other, grads, scal, term_type):
    rows, width = norm_own.shape
    cols = grads[0].shape[1]

    def kernel(scal_ref, no_ref, nt_ref, *refs):
        out_ref = refs[-1]
        for j in range(3):

            @pl.when(pl.program_id(0) == j)
            def _():
                grad = refs[j]
                term = dot(no_ref[...], grad[:rows, :], TN) + dot(nt_ref[...], grad[rows:, :], TN)
                out_ref[...] = (term * scal_ref[1]).astype(term_type)

    return call(
        kernel,
        "input_term",
        (3,),
        [scalars(), whole(norm_own), whole(norm_other)] + [whole(g) for g in grads],
        pl.BlockSpec((None, width, cols), lambda j: (j, 0, 0)),
        shape((3, width, cols), term_type),
        flops=12 * rows * width * cols,
        nbytes=4 * rows * width + 12 * rows * cols + 12 * width * cols,
    )(scal, norm_own, norm_other, *grads)


def norm1_other(grads, weight_one, weight_two):
    total, cols = grads[0].shape
    rows = total // 2
    width = weight_one.shape[1]
    block = 256
    count = rows // block

    def kernel(*refs):
        wa_ref, wb_ref, out_ref = refs[6:]
        total = None
        for j in range(3):
            part = dot(refs[j][...], wa_ref[j], NT) + dot(refs[3 + j][...], wb_ref[j], NT)
            total = part if total is None else total + part
        out_ref[...] = total.astype(bf16)

    thin = pl.BlockSpec((block, cols), lambda i: (i + count, 0))
    return call(
        kernel,
        "first_other",
        (count,),
        [thin] * 6 + [whole(weight_one), whole(weight_two)],
        pl.BlockSpec((block, width), lambda i: (i, 0)),
        shape((rows, width), bf16),
        flops=12 * rows * width * cols,
        nbytes=12 * rows * cols + 2 * rows * width + 12 * width * cols,
    )(*grads, weight_one, weight_two)


def norm1_own(grads, weight_one, weight_two, received, tokens, middle_grad, params, scal):
    rows, width = tokens.shape
    cols = grads[0].shape[1]
    block = 256
    last = rows // block - 1

    def kernel(scal_ref, *refs):
        wa_ref, wb_ref, rec_ref, tok_ref, mid_ref, par_ref, out_ref, sum_ref = refs[6:]
        i = pl.program_id(0)
        grad = rec_ref[...].astype(f32)
        for j in range(3):
            grad += dot(refs[j][...], wa_ref[j], NT) + dot(refs[3 + j][...], wb_ref[j], NT)
        unit, inverse = normalize(tok_ref[...].astype(f32))
        out = mid_ref[...] + norm_back(grad, par_ref[0:1, :], unit, inverse)
        out_ref[...] = out.astype(bf16)
        sums = [jnp.sum(v, axis=0, keepdims=True) for v in (grad * unit, grad)]
        add_rows(sum_ref, sums, i == 0)

        @pl.when(i == last)
        def _():
            sum_ref[...] = sum_ref[...] * scal_ref[1]

    thin = pl.BlockSpec((block, cols), lambda i: (i, 0))
    spec = pl.BlockSpec((block, width), lambda i: (i, 0))
    sums = shape((8, width), f32)
    return call(
        kernel,
        "first_own",
        (rows // block,),
        [scalars()] + [thin] * 6 + [whole(weight_one), whole(weight_two)] + [spec] * 3 + [whole(params)],
        [spec, whole(sums)],
        [shape((rows, width), bf16), sums],
        flops=12 * rows * width * cols,
        nbytes=12 * rows * cols + 10 * rows * width + 12 * width * cols,
    )(scal, *grads, weight_one, weight_two, received, tokens, middle_grad, params)


def body(
    tokens,
    out_grad,
    item_counts,
    group_dataset,
    variable_mask,
    first_gain,
    first_shift,
    input_weight,
    input_bias,
    output_weight,
    output_bias,
    second_gain,
    second_shift,
    up_weight,
    up_bias,
    down_weight,
    down_bias,
):
    shard_count = lax.axis_size("mp")
    width = tokens.shape[1]
    cols = input_weight.shape[2]
    hidden = up_weight.shape[1]

    def core_swap(value):
        return lax.ppermute(value, "mp", [(i, i ^ 1) for i in range(shard_count)])

    def chip_swap(value):
        return lax.ppermute(value, "mp", [(i, i ^ 2) for i in range(shard_count)])

    def after(value, *others):
        return lax.optimization_barrier((value, *others))[0]

    live = (lax.axis_index("mp") // 2 < item_counts[0]).astype(f32)
    dataset_hit = jnp.arange(variable_mask.shape[0], dtype=jnp.int32) == group_dataset[0]
    own_units = (
        item_counts[0] * jnp.sum(jnp.where(dataset_hit[:, None], variable_mask, 0))
    ).astype(f32)
    scal = jnp.stack([live, own_units])
    zero = jnp.zeros((width,), f32)
    params = jnp.stack(
        [first_gain, first_shift, output_bias, second_gain, second_shift, down_bias, zero, zero]
    )

    bias_pack = jnp.concatenate([up_bias, input_bias[0], input_bias[1]]).reshape(-1, LANES)
    bias_two = chip_swap(bias_pack).reshape(-1)
    wi_two = chip_swap(input_weight)
    wo_two = chip_swap(after(output_weight, wi_two))
    up_two = chip_swap(after(up_weight, wi_two))
    down_two = chip_swap(after(down_weight, up_two))
    up_bias_one = up_bias.reshape(1, hidden)
    up_bias_two = bias_two[:hidden].reshape(1, hidden)
    in_bias_two = bias_two[hidden:].reshape(2, cols)

    normed1, cot = first_norm(tokens, out_grad, params, scal)
    normed1_t = core_swap(normed1)
    cot_t = core_swap(cot)

    qkv_one = project(normed1, normed1_t, input_weight, input_bias)
    att_one, turned_one, stat_one = attend_forward(*qkv_one)
    qkv_two = project(normed1, normed1_t, wi_two, in_bias_two)
    att_two, turned_two, stat_two = attend_forward(*qkv_two)

    other_part = core_swap(output_other(att_one, att_two, output_weight, wo_two))
    middle, normed2 = output_own(
        tokens, att_one, att_two, output_weight, wo_two, other_part, params
    )
    normed2_t = core_swap(normed2)

    ff_one, ng_one, up_one_term, down_one_term, up_sum_one = feed_forward(
        normed2, normed2_t, cot, cot_t, up_weight, up_bias_one, down_weight, scal
    )
    ff_own, ng_own, ff_send, ng_send, up_two_term, down_two_term, up_sum_two = feed_forward(
        normed2, normed2_t, cot, cot_t, up_two, up_bias_two, down_two, scal, (ff_one, ng_one)
    )
    ng_received = core_swap(ng_send)
    ff_received = core_swap(after(ff_send, ng_received))
    up_received = chip_swap(up_two_term)
    down_received = chip_swap(after(down_two_term, up_received))

    middle_grad, middle_low, second_sums = second_back(
        middle, ng_own, ng_received, cot, params, scal
    )
    middle_low_t = core_swap(middle_low)
    result = (live * (middle + ff_own + ff_received.astype(f32) + down_bias)).astype(bf16)

    g_one, g_two, wo_one_term, wo_two_term = output_back(
        middle_low, middle_low_t, att_one, att_two, output_weight, wo_two, scal
    )
    *grads_two, sums_two = attend_backward(*qkv_two, g_two, turned_two, stat_two)
    wi_two_term = input_term(normed1, normed1_t, grads_two, scal, bf16)
    *grads_one, sums_one = attend_backward(*qkv_one, g_one, turned_one, stat_one)
    wi_one_term = input_term(normed1, normed1_t, grads_one, scal, f32)

    wo_received = chip_swap(after(wo_two_term, down_received))
    wi_received = chip_swap(after(wi_two_term, down_received))

    grads = [*grads_one, *grads_two]
    ng1_received = core_swap(norm1_other(grads, input_weight, wi_two))
    token_grad, first_sums = norm1_own(
        grads, input_weight, wi_two, ng1_received, tokens, middle_grad, params, scal
    )

    def both(own, received):
        return (own + received.astype(f32)).astype(bf16)

    up_sum, down_sum = lax.psum(
        (both(up_one_term, up_received), both(down_one_term, down_received)), "dp"
    )
    wo_sum, wi_sum = lax.psum((both(wo_one_term, wo_received), both(wi_one_term, wi_received)), "dp")

    def vector_pack(up_sums, in_sums):
        units_sum = own_units
        return jnp.concatenate([up_sums[0], in_sums[0] * units_sum, in_sums[1] * units_sum])

    vec_one = vector_pack(up_sum_one, sums_one)
    vec_two = vector_pack(up_sum_two, sums_two)
    vec = vec_one + chip_swap(vec_two.reshape(-1, LANES)).reshape(-1)
    vec = jnp.concatenate([vec, jnp.full((LANES,), own_units)])
    vec_sum = lax.psum(vec, "dp")
    rep_sum = lax.psum(jnp.concatenate([first_sums[:2], second_sums[:4]]), ("dp", "mp"))
    share = 1.0 / vec_sum[-1]
    vec_sum = vec_sum * share
    rep_sum = rep_sum * share

    return (
        result,
        token_grad,
        rep_sum[0],
        rep_sum[1],
        wi_sum.astype(f32) * share,
        vec_sum[hidden : hidden + 2 * cols].reshape(2, cols),
        wo_sum.astype(f32) * share,
        rep_sum[4],
        rep_sum[2],
        rep_sum[3],
        up_sum.astype(f32) * share,
        vec_sum[:hidden],
        down_sum.astype(f32) * share,
        rep_sum[5],
    )


def solution(mesh):
    in_specs = (
        P(("dp", "mp"), None),
        P(("dp", "mp"), None),
        P("dp"),
        P("dp"),
        P(),
        P(),
        P(),
        P(None, None, "mp"),
        P(None, "mp"),
        P("mp", None),
        P(),
        P(),
        P(),
        P(None, "mp"),
        P("mp"),
        P("mp", None),
        P(),
    )
    out_specs = (
        P(("dp", "mp"), None),
        P(("dp", "mp"), None),
        P(),
        P(),
        P(None, None, "mp"),
        P(None, "mp"),
        P("mp", None),
        P(),
        P(),
        P(),
        P(None, "mp"),
        P("mp"),
        P("mp", None),
        P(),
    )
    return jax.shard_map(body, mesh=mesh, in_specs=in_specs, out_specs=out_specs, check_vma=False)
```

```python
import jax
import jax.numpy as jnp
from jax import lax
from jax.experimental import pallas as pl
from jax.experimental.pallas import tpu as pltpu
from jax.sharding import PartitionSpec as P

HEAD_DIM = 64
LANES = 128
norm_eps = 1e-06
SCALE = HEAD_DIM**-0.5
LOG2E = 1.4426950408889634
RSQRT2 = 0.7071067811865476
RSQRT2PI = 0.3989422804014327

bf16 = jnp.bfloat16
f32 = jnp.float32
NN = (((1,), (0,)), ((), ()))
NT = (((1,), (1,)), ((), ()))
TN = (((0,), (0,)), ((), ()))
VMEM_BYTES = 60 << 20


def dot(left, right, dims=NN):
    return lax.dot_general(left, right, dims, preferred_element_type=f32)


def shape(dims, dtype):
    return jax.ShapeDtypeStruct(dims, dtype)


def whole(array):
    rank = len(array.shape)
    return pl.BlockSpec(array.shape, lambda *_: (0,) * rank, pipeline_mode=pl.Buffered(1))


def scalars():
    return pl.BlockSpec(memory_space=pltpu.SMEM)


def call(kernel, name, grid, in_specs, out_specs, out_shape, scratch=(), flops=0, nbytes=0, exps=0, weight=1e-6):
    return pl.pallas_call(
        kernel,
        name=name,
        grid=grid,
        in_specs=in_specs,
        out_specs=out_specs,
        out_shape=out_shape,
        scratch_shapes=list(scratch),
        compiler_params=pltpu.CompilerParams(vmem_limit_bytes=VMEM_BYTES),
        cost_estimate=pl.CostEstimate(
            flops=int(flops * weight), bytes_accessed=int(nbytes * weight), transcendentals=int(exps * weight)
        ),
    )


def split_two(values):
    high = values.astype(bf16)
    return high, (values - high.astype(f32)).astype(bf16)


def split_three(values):
    high = values.astype(bf16)
    rest = values - high.astype(f32)
    mid = rest.astype(bf16)
    return high, mid, (rest - mid.astype(f32)).astype(bf16)


def stat_rows(vector, rows):
    high, mid, rest = (part.astype(f32) for part in split_three(vector))
    row = lax.broadcasted_iota(jnp.int32, (rows, vector.shape[1]), 0)
    return jnp.where(
        row == 0, high, jnp.where(row == 1, mid, jnp.where(row == 2, rest, 0.0))
    ).astype(bf16)


def normalize(values):
    centered = values - jnp.mean(values, axis=-1, keepdims=True)
    variance = jnp.mean(centered * centered, axis=-1, keepdims=True)
    inverse = lax.rsqrt(variance + norm_eps)
    return centered * inverse, inverse


def norm_back(grad, gain, unit, inverse):
    scaled = grad * gain
    return inverse * (
        scaled
        - jnp.mean(scaled, axis=-1, keepdims=True)
        - unit * jnp.mean(scaled * unit, axis=-1, keepdims=True)
    )


def add_rows(ref, rows, first):
    @pl.when(first)
    def _():
        ref[...] = jnp.zeros_like(ref)

    for place, row in enumerate(rows):
        ref[place : place + 1, :] += row


def first_norm(tokens, out_grad, params, scal):
    rows, width = tokens.shape
    block = 256

    def kernel(scal_ref, tok_ref, grad_ref, par_ref, norm_ref, cot_ref):
        unit, _ = normalize(tok_ref[...].astype(f32))
        norm_ref[...] = (unit * par_ref[0:1, :] + par_ref[1:2, :]).astype(bf16)
        cot_ref[...] = (grad_ref[...].astype(f32) * scal_ref[0]).astype(bf16)

    spec = pl.BlockSpec((block, width), lambda i: (i, 0))
    return call(
        kernel,
        "first_norm",
        (rows // block,),
        [scalars(), spec, spec, whole(params)],
        [spec, spec],
        [shape((rows, width), bf16)] * 2,
        flops=20 * rows * width,
        nbytes=8 * rows * width,
    )(scal, tokens, out_grad, params)


def halves(block, width, count):
    own = pl.BlockSpec((block, width), lambda i, *_: (jnp.minimum(i, count - 1), 0))
    other = pl.BlockSpec((block, width), lambda i, *_: (jnp.maximum(i - count, 0), 0))
    return own, other


def pick(count, own_ref, other_ref):
    return jnp.where(pl.program_id(0) < count, own_ref[...], other_ref[...])


def project(norm_own, norm_other, weight, bias):
    rows, width = norm_own.shape
    cols = weight.shape[2]
    block = 512
    count = rows // block

    def kernel(own_ref, other_ref, w_ref, b_ref, q_ref, k_ref, v_ref):
        x = pick(count, own_ref, other_ref)
        q_ref[...] = (dot(x, w_ref[0]) + b_ref[0:1, :]).astype(bf16)
        k_ref[...] = dot(x, w_ref[1]).astype(bf16)
        v_ref[...] = (dot(x, w_ref[2]) + b_ref[1:2, :]).astype(bf16)

    out = pl.BlockSpec((block, cols), lambda i: (i, 0))
    return call(
        kernel,
        "project",
        (2 * count,),
        [*halves(block, width, count), whole(weight), whole(bias)],
        [out] * 3,
        [shape((2 * rows, cols), bf16)] * 3,
        flops=12 * rows * width * cols,
        nbytes=4 * rows * width + 6 * width * cols + 12 * rows * cols,
    )(norm_own, norm_other, weight, bias)


def attend_forward(queries, keys, values):
    rows, width = queries.shape
    block = min(1024, rows)
    chunk = 256
    steps = rows // chunk

    def kernel(q_ref, k_ref, v_ref, o_ref, ot_ref, lse_ref, k_two, v_turned):
        @pl.when(pl.program_id(1) == 0)
        def _():
            k = k_ref[...]
            lane = lax.broadcasted_iota(jnp.int32, k.shape, 1)
            rolled = pltpu.roll(k.astype(f32), HEAD_DIM, 1).astype(bf16)
            k_two[0] = jnp.where(lane < HEAD_DIM, k, rolled)
            k_two[1] = jnp.where(lane < HEAD_DIM, rolled, k)
            turned = v_ref[...].astype(f32).T
            ones = jnp.ones((HEAD_DIM, rows), bf16)
            v_turned[0] = jnp.concatenate([turned[:HEAD_DIM].astype(bf16), ones], 0)
            v_turned[1] = jnp.concatenate([ones, turned[HEAD_DIM:].astype(bf16)], 0)

        q_turned = q_ref[...].astype(f32).T * (SCALE * LOG2E)
        outs = []
        for head in range(2):
            at = head * HEAD_DIM
            q_two = jnp.concatenate(split_two(q_turned[at : at + HEAD_DIM]), 0)
            scores = [dot(k_two[head, pl.ds(j * chunk, chunk), :], q_two) for j in range(steps)]
            peak = None
            for part in scores:
                top = part.reshape(chunk // 8, 8, block).max(axis=0)
                peak = top if peak is None else jnp.maximum(peak, top)
            peak = jnp.max(peak, axis=0, keepdims=True)
            total = None
            for j in range(steps):
                weights = jnp.exp2(scores[j] - peak).astype(bf16)
                part = dot(v_turned[head, :, pl.ds(j * chunk, chunk)], weights)
                total = part if total is None else total + part
            row_sum = total[HEAD_DIM - at : HEAD_DIM - at + 1]
            outs.append(total[at : at + HEAD_DIM] / row_sum)
            lse_ref[head : head + 1, :] = peak + jnp.log2(row_sum)
        turned = jnp.concatenate(outs, 0)
        ot_ref[...] = turned
        o_ref[...] = turned.T.astype(bf16)

    by_query = pl.BlockSpec((block, LANES), lambda j, i: (i, j))
    by_key = pl.BlockSpec((rows, LANES), lambda j, i: (0, j))
    turned_spec = pl.BlockSpec((LANES, block), lambda j, i: (j, i))
    stat_spec = pl.BlockSpec((None, 8, block), lambda j, i: (j, 0, i))
    pairs = width // LANES
    return call(
        kernel,
        "attend_forward",
        (pairs, rows // block),
        [by_query, by_key, by_key],
        [by_query, turned_spec, stat_spec],
        [shape((rows, width), bf16), shape((width, rows), f32), shape((pairs, 8, rows), f32)],
        [pltpu.VMEM((2, rows, LANES), bf16), pltpu.VMEM((2, LANES, rows), bf16)],
        flops=16 * rows * rows * width,
        nbytes=12 * rows * width,
        exps=rows * rows * width // HEAD_DIM,
        weight=1000,
    )(queries, keys, values)


def attend_backward(queries, keys, values, out_grad, out_turned, stats, pair):
    rows = queries.shape[0]
    width = LANES
    block = min(1024, rows)
    chunk = 256
    count = rows // block

    def kernel(
        q_ref, k_ref, v_ref, g_ref, ot_ref, lse_ref, dq_ref, dk_ref, dv_ref, sum_ref,
        k_wide, k_turned, v_wide, dk_acc, dv_acc,
    ):
        i = pl.program_id(1)

        @pl.when(i == 0)
        def _():
            k = k_ref[...]
            v = v_ref[...]
            lane = lax.broadcasted_iota(jnp.int32, k.shape, 1)
            k_rolled = pltpu.roll(k.astype(f32), HEAD_DIM, 1).astype(bf16)
            v_rolled = pltpu.roll(v.astype(f32), HEAD_DIM, 1).astype(bf16)
            ones = jnp.where(lane < 3, 1.0, 0.0).astype(bf16)
            k_wide[0] = jnp.concatenate([jnp.where(lane < HEAD_DIM, k, k_rolled), ones], 1)
            k_wide[1] = jnp.concatenate([jnp.where(lane < HEAD_DIM, k_rolled, k), ones], 1)
            tail = jnp.where(lane < HEAD_DIM + 3, 1.0, 0.0).astype(bf16)
            v_wide[0] = jnp.where(lane < HEAD_DIM, v, tail)
            v_wide[1] = jnp.where(lane < HEAD_DIM, v_rolled, tail)
            k_turned[...] = k.astype(f32).T.astype(bf16)
            dk_acc[...] = jnp.zeros_like(dk_acc)
            dv_acc[...] = jnp.zeros_like(dv_acc)
            sum_ref[...] = jnp.zeros_like(sum_ref)

        q_turned = q_ref[...].astype(f32).T
        q_low = q_turned.astype(bf16)
        q_turned = q_turned * (SCALE * LOG2E)
        g_turned = g_ref[...].astype(f32).T
        g_low = g_turned.astype(bf16)
        dqs = []
        for head in range(2):
            part = slice(head * HEAD_DIM, (head + 1) * HEAD_DIM)
            q_wide = jnp.concatenate(
                [*split_two(q_turned[part]), stat_rows(-lse_ref[head : head + 1, :], LANES)], 0
            )
            row_dot = jnp.sum(g_turned[part] * ot_ref[part, :], axis=0, keepdims=True)
            g_wide = jnp.concatenate([g_low[part], stat_rows(-row_dot, HEAD_DIM)], 0)
            dq = None
            for j in range(rows // chunk):
                at = pl.ds(j * chunk, chunk)
                probabilities = jnp.exp2(dot(k_wide[head, at, :], q_wide))
                shifted = dot(v_wide[head, at, :], g_wide)
                probs_low = probabilities.astype(bf16)
                score_grad = (probabilities * shifted).astype(bf16)
                dv_acc[part, at] += dot(g_low[part], probs_low, NT)
                dk_acc[part, at] += dot(q_low[part], score_grad, NT)
                add = dot(k_turned[part, at], score_grad)
                dq = add if dq is None else dq + add
            dqs.append(dq)
        dq = (jnp.concatenate(dqs, 0) * SCALE).T
        dq_ref[...] = dq.astype(bf16)
        sum_ref[0:1, :] += jnp.sum(dq, axis=0, keepdims=True)

        @pl.when(i == count - 1)
        def _():
            dk_ref[...] = (dk_acc[...] * SCALE).T.astype(bf16)
            dv = dv_acc[...].T
            dv_ref[...] = dv.astype(bf16)
            sum_ref[1:2, :] = jnp.sum(dv, axis=0, keepdims=True)

    by_query = pl.BlockSpec((block, LANES), lambda j, i: (i, pair))
    by_key = pl.BlockSpec((rows, LANES), lambda j, i: (0, pair))
    turned_spec = pl.BlockSpec((LANES, block), lambda j, i: (pair, i))
    stat_spec = pl.BlockSpec((None, 8, block), lambda j, i: (pair, 0, i))
    query_out = pl.BlockSpec((block, LANES), lambda j, i: (i, 0))
    key_out = pl.BlockSpec((rows, LANES), lambda j, i: (0, 0))
    sum_spec = pl.BlockSpec((8, LANES), lambda j, i: (0, 0))
    return call(
        kernel,
        "attend_backward",
        (1, count),
        [by_query, by_key, by_key, by_query, turned_spec, stat_spec],
        [query_out, key_out, key_out, sum_spec],
        [shape((rows, width), bf16)] * 3 + [shape((8, width), f32)],
        [
            pltpu.VMEM((2, rows, 2 * LANES), bf16),
            pltpu.VMEM((LANES, rows), bf16),
            pltpu.VMEM((2, rows, LANES), bf16),
            pltpu.VMEM((LANES, rows), f32),
            pltpu.VMEM((LANES, rows), f32),
        ],
        flops=40 * rows * rows * width,
        nbytes=20 * rows * width,
        exps=rows * rows * width // HEAD_DIM,
        weight=1000,
    )(queries, keys, values, out_grad, out_turned, stats)


def output_other(first, second, weight_one, weight_two):
    total, cols = first.shape
    rows = total // 2
    width = weight_one.shape[1]
    block = 512
    count = rows // block

    def kernel(a_ref, b_ref, wa_ref, wb_ref, out_ref):
        out_ref[...] = (dot(a_ref[...], wa_ref[...]) + dot(b_ref[...], wb_ref[...])).astype(bf16)

    spec = pl.BlockSpec((block, cols), lambda i: (i + count, 0))
    return call(
        kernel,
        "output_other",
        (count,),
        [spec, spec, whole(weight_one), whole(weight_two)],
        pl.BlockSpec((block, width), lambda i: (i, 0)),
        shape((rows, width), bf16),
        flops=4 * rows * cols * width,
        nbytes=4 * rows * cols + 2 * rows * width,
    )(first, second, weight_one, weight_two)


def output_own(tokens, first, second, weight_one, weight_two, received, params):
    rows, width = tokens.shape
    cols = first.shape[1]
    block = 256

    def kernel(t_ref, a_ref, b_ref, wa_ref, wb_ref, r_ref, par_ref, mid_ref, norm_ref):
        middle = (
            t_ref[...].astype(f32)
            + (dot(a_ref[...], wa_ref[...]) + dot(b_ref[...], wb_ref[...]) + r_ref[...].astype(f32))
            + par_ref[2:3, :]
        )
        mid_ref[...] = middle
        unit, _ = normalize(middle)
        norm_ref[...] = (unit * par_ref[3:4, :] + par_ref[4:5, :]).astype(bf16)

    spec = pl.BlockSpec((block, width), lambda i: (i, 0))
    thin = pl.BlockSpec((block, cols), lambda i: (i, 0))
    return call(
        kernel,
        "output_own",
        (rows // block,),
        [spec, thin, thin, whole(weight_one), whole(weight_two), spec, whole(params)],
        [spec, spec],
        [shape((rows, width), f32), shape((rows, width), bf16)],
        flops=4 * rows * cols * width,
        nbytes=4 * rows * cols + 10 * rows * width,
    )(tokens, first, second, weight_one, weight_two, received, params)


def feed_forward(norm_own, norm_other, cot_own, cot_other, bias, both_weights, scal, earlier=None):
    rows, width = norm_own.shape
    hidden = bias.shape[1]
    block = 256
    count = rows // block
    last = earlier is not None
    slices, depth = both_weights.shape[0], both_weights.shape[2]
    term_type = bf16

    def kernel(scal_ref, no_ref, nt_ref, co_ref, ct_ref, b_ref, up_ref, dn_ref, *refs):
        if last:
            ff_in, ng_in, ffo_ref, ngo_ref, fft_ref, ngt_ref, *refs = refs
        else:
            ff_ref, ng_ref, *refs = refs
        up_term, down_term, sum_ref, up_acc, down_acc = refs
        i = pl.program_id(0)

        @pl.when(i == 0)
        def _():
            up_acc[...] = jnp.zeros_like(up_acc)
            down_acc[...] = jnp.zeros_like(down_acc)
            sum_ref[...] = jnp.zeros_like(sum_ref)

        x = pick(count, no_ref, nt_ref)
        cot = pick(count, co_ref, ct_ref)
        up = up_ref[...].reshape(width, hidden)
        down = dn_ref[...].reshape(hidden, width)
        h = dot(x, up) + b_ref[0:1, :]
        cdf = 0.5 * (1.0 + lax.erf(h * RSQRT2))
        act = (h * cdf).astype(bf16)
        slope = cdf + h * (RSQRT2PI * jnp.exp(-0.5 * h * h))
        ff = dot(act, down)
        grad = dot(cot, down, NT) * slope
        sum_ref[0:1, :] += jnp.sum(grad, axis=0, keepdims=True)
        low = grad.astype(bf16)
        ng = dot(low, up, NT)
        up_acc[...] += dot(x, low, TN)
        down_acc[...] += dot(act, cot, TN)
        if last:
            ff = ff + ff_in[...]
            ng = ng + ng_in[...]

            @pl.when(i < count)
            def _():
                ffo_ref[...] = ff
                ngo_ref[...] = ng

            @pl.when(i >= count)
            def _():
                fft_ref[...] = ff.astype(bf16)
                ngt_ref[...] = ng.astype(bf16)
        else:
            ff_ref[...] = ff
            ng_ref[...] = ng

        @pl.when(i == 2 * count - 1)
        def _():
            units = scal_ref[1]
            up_term[...] = (up_acc[...] * units).astype(term_type)
            down_term[...] = (down_acc[...] * units).astype(term_type)
            sum_ref[...] = sum_ref[...] * units

    own, other = halves(block, width, count)
    every = pl.BlockSpec((block, width), lambda i: (i, 0))
    up_spec, down_spec = (
        pl.BlockSpec(
            (slices, None, depth, width), lambda i, j=j: (0, j, 0, 0), pipeline_mode=pl.Buffered(1)
        )
        for j in range(2)
    )
    ins = [scalars(), own, other, own, other, whole(bias), up_spec, down_spec]
    args = [scal, norm_own, norm_other, cot_own, cot_other, bias, both_weights, both_weights]
    if last:
        ins += [every, every]
        args += list(earlier)
        outs = [own, own, other, other]
        shapes = [shape((rows, width), f32)] * 2 + [shape((rows, width), bf16)] * 2
    else:
        outs = [every, every]
        shapes = [shape((2 * rows, width), f32)] * 2
    terms = [shape((width, hidden), term_type), shape((hidden, width), term_type)]
    sums = shape((8, hidden), f32)
    return call(
        kernel,
        "feed_forward",
        (2 * count,),
        ins,
        outs + [whole(terms[0]), whole(terms[1]), whole(sums)],
        shapes + terms + [sums],
        [pltpu.VMEM((width, hidden), f32), pltpu.VMEM((hidden, width), f32)],
        flops=24 * rows * width * hidden,
        nbytes=24 * rows * width + 12 * width * hidden,
        exps=4 * rows * hidden,
        weight=1000 if last else 1e-6,
    )(*args)


def second_back(middle, grad_own, grad_received, cot, params, scal):
    rows, width = middle.shape
    block = 256
    last = rows // block - 1

    def kernel(scal_ref, mid_ref, go_ref, gr_ref, cot_ref, par_ref, out_ref, low_ref, sum_ref):
        i = pl.program_id(0)
        unit, inverse = normalize(mid_ref[...])
        grad = go_ref[...] + gr_ref[...].astype(f32)
        cot = cot_ref[...].astype(f32)
        out = cot + norm_back(grad, par_ref[3:4, :], unit, inverse)
        out_ref[...] = out
        low_ref[...] = out.astype(bf16)
        sums = [jnp.sum(v, axis=0, keepdims=True) for v in (grad * unit, grad, out, cot)]
        add_rows(sum_ref, sums, i == 0)

        @pl.when(i == last)
        def _():
            sum_ref[...] = sum_ref[...] * scal_ref[1]

    spec = pl.BlockSpec((block, width), lambda i: (i, 0))
    sums = shape((8, width), f32)
    return call(
        kernel,
        "second_back",
        (rows // block,),
        [scalars(), spec, spec, spec, spec, whole(params)],
        [spec, spec, whole(sums)],
        [shape((rows, width), f32), shape((rows, width), bf16), sums],
        flops=30 * rows * width,
        nbytes=18 * rows * width,
    )(scal, middle, grad_own, grad_received, cot, params)


def output_back(low_own, low_other, first, second, weight_one, weight_two, scal):
    rows, width = low_own.shape
    cols = first.shape[1]
    block = 512
    count = rows // block

    def kernel(
        scal_ref, lo_ref, lt_ref, a_ref, b_ref, wa_ref, wb_ref,
        ga_ref, gb_ref, ta_ref, tb_ref, acc_a, acc_b,
    ):
        i = pl.program_id(0)

        @pl.when(i == 0)
        def _():
            acc_a[...] = jnp.zeros_like(acc_a)
            acc_b[...] = jnp.zeros_like(acc_b)

        low = pick(count, lo_ref, lt_ref)
        ga_ref[...] = dot(low, wa_ref[...], NT).astype(bf16)
        gb_ref[...] = dot(low, wb_ref[...], NT).astype(bf16)
        acc_a[...] += dot(a_ref[...], low, TN)
        acc_b[...] += dot(b_ref[...], low, TN)

        @pl.when(i == 2 * count - 1)
        def _():
            ta_ref[...] = (acc_a[...] * scal_ref[1]).astype(bf16)
            tb_ref[...] = (acc_b[...] * scal_ref[1]).astype(bf16)

    own, other = halves(block, width, count)
    thin = pl.BlockSpec((block, cols), lambda i: (i, 0))
    terms = [shape((cols, width), bf16)] * 2
    return call(
        kernel,
        "output_back",
        (2 * count,),
        [scalars(), own, other, thin, thin, whole(weight_one), whole(weight_two)],
        [thin, thin, whole(terms[0]), whole(terms[1])],
        [shape((2 * rows, cols), bf16)] * 2 + terms,
        [pltpu.VMEM((cols, width), f32)] * 2,
        flops=16 * rows * width * cols,
        nbytes=4 * rows * width + 16 * rows * cols,
    )(scal, low_own, low_other, first, second, weight_one, weight_two)


def input_term(norm_own, norm_other, pairs, scal):
    rows, width = norm_own.shape
    count = len(pairs)
    grads = [pair[j] for j in range(3) for pair in pairs]

    def kernel(scal_ref, no_ref, nt_ref, *refs):
        out_ref = refs[-1]
        for j in range(3):

            @pl.when(pl.program_id(0) == j)
            def _():
                grad = jnp.concatenate([r[...] for r in refs[count * j : count * j + count]], 1)
                term = dot(no_ref[...], grad[:rows, :], TN) + dot(nt_ref[...], grad[rows:, :], TN)
                out_ref[...] = (term * scal_ref[1]).astype(bf16)

    cols = count * LANES
    return call(
        kernel,
        "input_term",
        (3,),
        [scalars(), whole(norm_own), whole(norm_other)] + [whole(g) for g in grads],
        pl.BlockSpec((width, cols), lambda j: (j, 0)),
        shape((3 * width, cols), bf16),
        flops=12 * rows * width * cols,
        nbytes=4 * rows * width + 12 * rows * cols + 12 * width * cols,
    )(scal, norm_own, norm_other, *grads)


def norm1_part(refs, weights):
    total = None
    place = 0
    for w_ref in weights:
        cols = w_ref.shape[2]
        count = cols // LANES
        for j in range(3):
            grad = jnp.concatenate([r[...] for r in refs[place : place + count]], 1)
            part = dot(grad, w_ref[j], NT)
            total = part if total is None else total + part
            place += count
    return total


def flat(quarters):
    return [pair[j] for pairs in quarters for j in range(3) for pair in pairs]


def norm1_other(quarters, weights):
    grads = flat(quarters)
    rows = grads[0].shape[0] // 2
    width, cols = weights[0].shape[1:]
    block = 256
    start = rows // block
    many = len(grads)

    def kernel(*refs):
        refs[-1][...] = norm1_part(refs[:many], refs[many:-1]).astype(bf16)

    thin = pl.BlockSpec((block, LANES), lambda i: (i + start, 0))
    return call(
        kernel,
        "first_other",
        (rows // block,),
        [thin] * many + [whole(w) for w in weights],
        pl.BlockSpec((block, width), lambda i: (i, 0)),
        shape((rows, width), bf16),
        flops=12 * rows * width * cols,
        nbytes=12 * rows * cols + 2 * rows * width + 12 * width * cols,
    )(*grads, *weights)


def norm1_own(quarters, weights, received, tokens, middle_grad, params, scal):
    grads = flat(quarters)
    rows, width = tokens.shape
    cols = weights[0].shape[2]
    block = 256
    last = rows // block - 1
    many = len(grads)

    def kernel(scal_ref, *refs):
        rec_ref, tok_ref, mid_ref, par_ref, out_ref, sum_ref = refs[many + len(weights) :]
        i = pl.program_id(0)
        grad = norm1_part(refs[:many], refs[many : many + len(weights)])
        grad += rec_ref[...].astype(f32)
        unit, inverse = normalize(tok_ref[...].astype(f32))
        out = mid_ref[...] + norm_back(grad, par_ref[0:1, :], unit, inverse)
        out_ref[...] = out.astype(bf16)
        sums = [jnp.sum(v, axis=0, keepdims=True) for v in (grad * unit, grad)]
        add_rows(sum_ref, sums, i == 0)

        @pl.when(i == last)
        def _():
            sum_ref[...] = sum_ref[...] * scal_ref[1]

    thin = pl.BlockSpec((block, LANES), lambda i: (i, 0))
    spec = pl.BlockSpec((block, width), lambda i: (i, 0))
    sums = shape((8, width), f32)
    return call(
        kernel,
        "first_own",
        (rows // block,),
        [scalars()] + [thin] * many + [whole(w) for w in weights] + [spec] * 3 + [whole(params)],
        [spec, whole(sums)],
        [shape((rows, width), bf16), sums],
        flops=12 * rows * width * cols,
        nbytes=12 * rows * cols + 10 * rows * width + 12 * width * cols,
    )(scal, *grads, *weights, received, tokens, middle_grad, params)


def body(
    tokens,
    out_grad,
    item_counts,
    group_dataset,
    variable_mask,
    first_gain,
    first_shift,
    input_weight,
    input_bias,
    output_weight,
    output_bias,
    second_gain,
    second_shift,
    up_weight,
    up_bias,
    down_weight,
    down_bias,
):
    shard_count = lax.axis_size("mp")
    groups = lax.axis_size("dp")
    width = tokens.shape[1]
    cols = input_weight.shape[2]
    hidden = up_weight.shape[1]

    def core_swap(value):
        return lax.ppermute(value, "mp", [(i, i ^ 1) for i in range(shard_count)])

    def chip_swap(value):
        return lax.ppermute(value, "mp", [(i, i ^ 2) for i in range(shard_count)])

    def after(value, *others):
        return lax.optimization_barrier((value, *others))[0]

    def along(value, bit):
        return lax.ppermute(value, "dp", [(i, i ^ bit) for i in range(groups)])

    group = lax.axis_index("dp")

    slice_rows = up_weight.shape[0] // groups
    slices = [
        lax.dynamic_slice_in_dim(weight, group * slice_rows, slice_rows, 0)
        for weight in (up_weight, down_weight)
    ]
    slice_two = chip_swap(jnp.stack(slices)[None])
    ff_weights_two = lax.all_gather(slice_two, "dp", axis=0, tiled=True)
    bias_pack = jnp.concatenate([up_bias, input_bias[0], input_bias[1]]).reshape(-1, LANES)
    bias_two = chip_swap(after(bias_pack, slice_two))
    wi_two = chip_swap(after(input_weight, slice_two))
    wo_two = chip_swap(after(output_weight, bias_two))

    live = (lax.axis_index("mp") // 2 < item_counts[0]).astype(f32)
    dataset_hit = jnp.arange(variable_mask.shape[0], dtype=jnp.int32) == group_dataset[0]
    own_units = (
        item_counts[0] * jnp.sum(jnp.where(dataset_hit[:, None], variable_mask, 0))
    ).astype(f32)
    scal = jnp.stack([live, own_units])
    zero = jnp.zeros((width,), f32)
    params = jnp.stack(
        [first_gain, first_shift, output_bias, second_gain, second_shift, down_bias, zero, zero]
    )

    normed1, cot = first_norm(tokens, out_grad, params, scal)
    normed1_t = core_swap(normed1)
    cot_t = core_swap(cot)

    qkv_one = project(normed1, normed1_t, input_weight, input_bias)
    att_one, turned_one, stat_one = attend_forward(*qkv_one)
    bias_two = bias_two.reshape(-1)
    up_bias_one = up_bias.reshape(1, hidden)
    up_bias_two = bias_two[:hidden].reshape(1, hidden)
    in_bias_two = bias_two[hidden:].reshape(2, cols)
    qkv_two = project(after(normed1, att_one), normed1_t, wi_two, in_bias_two)
    att_two, turned_two, stat_two = attend_forward(*qkv_two)

    other_part = core_swap(output_other(att_one, after(att_two, ff_weights_two), output_weight, wo_two))
    middle, normed2 = output_own(
        tokens, att_one, att_two, output_weight, wo_two, other_part, params
    )
    normed2_t = core_swap(normed2)

    ff_two, ng_two, up_two_term, down_two_term, up_sum_two = feed_forward(
        normed2, normed2_t, cot, cot_t, up_bias_two, ff_weights_two, scal
    )
    up_received = chip_swap(up_two_term)
    ff_weights = jnp.stack([w.reshape(1, -1, width) for w in (up_weight, down_weight)], 1)
    ff_own, ng_own, ff_send, ng_send, up_one_term, down_one_term, up_sum_one = feed_forward(
        normed2, normed2_t, cot, cot_t, up_bias_one, ff_weights, scal, (ff_two, ng_two)
    )
    ng_received = core_swap(ng_send)
    down_received = chip_swap(after(down_two_term, up_received))
    middle_grad, middle_low, second_sums = second_back(
        middle, ng_own, after(ng_received, up_received), cot, params, scal
    )
    middle_low_t = core_swap(middle_low)
    g_one, g_two, wo_one_term, wo_two_term = output_back(
        middle_low, middle_low_t, att_one, att_two, output_weight, wo_two, scal
    )

    def pairs_back(qkv, grad, turned, stat, begin, between):
        pairs = []
        waits = begin
        for pair in range(cols // LANES):
            pairs.append(attend_backward(*qkv, after(grad, *waits), turned, stat, pair))
            waits = [pairs[-1][0], *between(pair, pairs[-1])]
        return pairs

    def both(own, received, *last):
        return own.astype(f32) + after(received, *last).astype(f32)

    sums = []

    def between_two(pair, outs):
        if pair > 0:
            return []
        up_both = both(up_one_term, up_received, outs[0]).astype(bf16)
        down_both = both(down_one_term, down_received, outs[0]).astype(bf16)
        sums.extend(lax.psum((up_both, down_both), "dp"))
        return [up_both, down_both]

    pairs_two = pairs_back(qkv_two, g_two, turned_two, stat_two, [], between_two)
    up_sum, down_sum = sums
    wi_two_term = input_term(normed1, normed1_t, pairs_two, scal)
    ff_received = core_swap(after(ff_send, pairs_two[0][0]))
    wo_received = chip_swap(after(wo_two_term, pairs_two[0][0]))
    wi_received = chip_swap(wi_two_term)
    pairs_one = pairs_back(
        qkv_one, g_one, turned_one, stat_one, [wi_two_term], lambda *_: [wo_received]
    )

    quarters = [pairs_one, pairs_two]
    weights = [input_weight, wi_two]
    ng1_send = norm1_other(quarters, [input_weight, after(wi_two, wi_received, wo_received)])
    ng1_received = core_swap(ng1_send)
    wi_one_term = input_term(after(normed1, ng1_send), normed1_t, pairs_one, scal)
    token_grad, first_sums = norm1_own(
        quarters, weights, after(ng1_received, wi_one_term), tokens, middle_grad, params, scal
    )
    result = live * (middle + ff_own + ff_received.astype(f32) + down_bias)
    result = result.astype(bf16)

    def columns(term):
        return jnp.concatenate([term[:, k * cols : (k + 1) * cols] for k in range(width // cols)])

    tail = jnp.concatenate(
        [both(wi_one_term, wi_received), both(columns(wo_one_term), columns(wo_received))]
    )
    bits = [1 << k for k in range(groups.bit_length() - 1)]
    orders = [bits, bits[1:] + bits[:1]]
    middle_row = tail.shape[0] // 2
    parts = [tail[:middle_row], tail[middle_row:]]

    def upper(bit):
        return (group // bit) % 2

    for turn in range(len(bits)):
        if turn == 1:
            parts = [after(part, token_grad) for part in parts]
        for k in range(2):
            bit = orders[k][turn]
            half = parts[k].shape[0] // 2
            keep = lax.dynamic_slice_in_dim(parts[k], upper(bit) * half, half, 0)
            send = lax.dynamic_slice_in_dim(parts[k], (1 - upper(bit)) * half, half, 0)
            parts[k] = keep + along(send.astype(bf16), bit).astype(f32)
    parts = [part.astype(bf16) for part in parts]
    for turn in reversed(range(len(bits))):
        for k in range(2):
            bit = orders[k][turn]
            received = along(parts[k], bit)
            is_upper = upper(bit) == 1
            parts[k] = jnp.concatenate(
                [jnp.where(is_upper, received, parts[k]), jnp.where(is_upper, parts[k], received)]
            )
    wi_rows = 3 * width
    tail_sum = jnp.concatenate(parts)
    wi_sum = tail_sum[:wi_rows].reshape(3, width, cols)
    wo_sum = tail_sum[wi_rows:].reshape(width // cols, cols, cols)
    wo_sum = jnp.concatenate([wo_sum[k] for k in range(width // cols)], 1)

    def quarter_rows(pairs, up_sums):
        sums_all = jnp.concatenate([pair[3] for pair in pairs], 1)
        rest = jnp.full((1, width - 2 * cols), own_units)
        bias_row = jnp.concatenate([sums_all[0:1] * own_units, sums_all[1:2] * own_units, rest], 1)
        return jnp.concatenate([bias_row, up_sums[:1]])

    late = jnp.concatenate([first_sums[:2], second_sums[:4]])
    late = late + core_swap(late)
    late_one, late_two = (
        jnp.concatenate([late, quarter_rows(pairs, up_sums)])
        for pairs, up_sums in ((pairs_one, up_sum_one), (pairs_two, up_sum_two))
    )
    late = late_one + chip_swap(late_two)
    for bit in bits:
        late = late + along(late, bit)
    share = 2.0 / late[6, -1]
    late = late * share

    return (
        result,
        token_grad,
        late[0],
        late[1],
        wi_sum.astype(f32) * share,
        late[6, : 2 * cols].reshape(2, cols),
        wo_sum.astype(f32) * share,
        late[4],
        late[2],
        late[3],
        up_sum.astype(f32) * share,
        late[7],
        down_sum.astype(f32) * share,
        late[5],
    )


def solution(mesh):
    in_specs = (
        P(("dp", "mp"), None),
        P(("dp", "mp"), None),
        P("dp"),
        P("dp"),
        P(),
        P(),
        P(),
        P(None, None, "mp"),
        P(None, "mp"),
        P("mp", None),
        P(),
        P(),
        P(),
        P(None, "mp"),
        P("mp"),
        P("mp", None),
        P(),
    )
    out_specs = (
        P(("dp", "mp"), None),
        P(("dp", "mp"), None),
        P(),
        P(),
        P(None, None, "mp"),
        P(None, "mp"),
        P("mp", None),
        P(),
        P(),
        P(),
        P(None, "mp"),
        P("mp"),
        P("mp", None),
        P(),
    )
    return jax.shard_map(body, mesh=mesh, in_specs=in_specs, out_specs=out_specs, check_vma=False)
```

```python
import jax
import jax.numpy as jnp
from jax import lax
from jax.experimental import pallas as pl
from jax.experimental.pallas import tpu as pltpu
from jax.sharding import PartitionSpec as P

HEAD_DIM = 64
LANES = 128
norm_eps = 1e-06
SCALE = HEAD_DIM**-0.5
LOG2E = 1.4426950408889634
RSQRT2 = 0.7071067811865476
RSQRT2PI = 0.3989422804014327

bf16 = jnp.bfloat16
f32 = jnp.float32
NN = (((1,), (0,)), ((), ()))
NT = (((1,), (1,)), ((), ()))
TN = (((0,), (0,)), ((), ()))
VMEM_BYTES = 60 << 20


def dot(left, right, dims=NN):
    return lax.dot_general(left, right, dims, preferred_element_type=f32)


def shape(dims, dtype):
    return jax.ShapeDtypeStruct(dims, dtype)


def whole(array):
    rank = len(array.shape)
    return pl.BlockSpec(array.shape, lambda *_: (0,) * rank, pipeline_mode=pl.Buffered(1))


def scalars():
    return pl.BlockSpec(memory_space=pltpu.SMEM)


def call(kernel, name, grid, in_specs, out_specs, out_shape, scratch=(), flops=0, nbytes=0, exps=0, weight=1e-6, aliases=None):
    return pl.pallas_call(
        kernel,
        name=name,
        grid=grid,
        in_specs=in_specs,
        out_specs=out_specs,
        out_shape=out_shape,
        scratch_shapes=list(scratch),
        input_output_aliases=aliases or {},
        compiler_params=pltpu.CompilerParams(vmem_limit_bytes=VMEM_BYTES),
        cost_estimate=pl.CostEstimate(
            flops=int(flops * weight), bytes_accessed=int(nbytes * weight), transcendentals=int(exps * weight)
        ),
    )


def split_two(values):
    high = values.astype(bf16)
    return high, (values - high.astype(f32)).astype(bf16)


def split_three(values):
    high = values.astype(bf16)
    rest = values - high.astype(f32)
    mid = rest.astype(bf16)
    return high, mid, (rest - mid.astype(f32)).astype(bf16)


def stat_rows(vector, rows):
    high, mid, rest = (part.astype(f32) for part in split_three(vector))
    row = lax.broadcasted_iota(jnp.int32, (rows, vector.shape[1]), 0)
    return jnp.where(
        row == 0, high, jnp.where(row == 1, mid, jnp.where(row == 2, rest, 0.0))
    ).astype(bf16)


def normalize(values):
    centered = values - jnp.mean(values, axis=-1, keepdims=True)
    variance = jnp.mean(centered * centered, axis=-1, keepdims=True)
    inverse = lax.rsqrt(variance + norm_eps)
    return centered * inverse, inverse


def norm_back(grad, gain, unit, inverse):
    scaled = grad * gain
    return inverse * (
        scaled
        - jnp.mean(scaled, axis=-1, keepdims=True)
        - unit * jnp.mean(scaled * unit, axis=-1, keepdims=True)
    )


def add_rows(ref, rows, first, start):
    @pl.when(first)
    def _():
        ref[...] = jnp.zeros_like(ref)

    for place, row in enumerate(rows):
        ref[start + place : start + place + 1, :] += row


def first_norm(tokens, out_grad, params, scal):
    rows, width = tokens.shape
    block = 256

    def kernel(scal_ref, tok_ref, grad_ref, par_ref, norm_ref, cot_ref):
        unit, _ = normalize(tok_ref[...].astype(f32))
        norm_ref[...] = (unit * par_ref[0:1, :] + par_ref[1:2, :]).astype(bf16)
        cot_ref[...] = (grad_ref[...].astype(f32) * scal_ref[0]).astype(bf16)

    spec = pl.BlockSpec((block, width), lambda i: (i, 0))
    return call(
        kernel,
        "first_norm",
        (rows // block,),
        [scalars(), spec, spec, whole(params)],
        [spec, spec],
        [shape((rows, width), bf16)] * 2,
        flops=20 * rows * width,
        nbytes=8 * rows * width,
    )(scal, tokens, out_grad, params)


def halves(block, width, count):
    own = pl.BlockSpec((block, width), lambda i, *_: (jnp.minimum(i, count - 1), 0))
    other = pl.BlockSpec((block, width), lambda i, *_: (jnp.maximum(i - count, 0), 0))
    return own, other


def pick(count, own_ref, other_ref):
    return jnp.where(pl.program_id(0) < count, own_ref[...], other_ref[...])


def project(norm, weight, bias, earlier=None):
    rows, width = norm.shape
    cols = weight.shape[2]
    block = 512
    start = 0 if earlier is None else rows // block
    skip = 0 if earlier is None else 3

    def kernel(x_ref, w_ref, b_ref, *refs):
        q_ref, k_ref, v_ref = refs[skip:]
        x = x_ref[...]
        q_ref[...] = (dot(x, w_ref[0]) + b_ref[0:1, :]).astype(bf16)
        k_ref[...] = dot(x, w_ref[1]).astype(bf16)
        v_ref[...] = (dot(x, w_ref[2]) + b_ref[1:2, :]).astype(bf16)

    out = pl.BlockSpec((block, cols), lambda i: (i + start, 0))
    return call(
        kernel,
        "project",
        (rows // block,),
        [pl.BlockSpec((block, width), lambda i: (i, 0)), whole(weight), whole(bias)]
        + [pl.BlockSpec(memory_space=pl.ANY)] * skip,
        [out] * 3,
        [shape((2 * rows, cols), bf16)] * 3,
        flops=6 * rows * width * cols,
        nbytes=2 * rows * width + 6 * width * cols + 6 * rows * cols,
        weight=1000,
        aliases={3 + k: k for k in range(skip)},
    )(norm, weight, bias, *(earlier or ()))


def attend_forward(queries, keys, values):
    rows, width = queries.shape
    chunk = min(512, rows)

    def kernel(q_ref, k_ref, v_ref, o_ref, ot_ref, lse_ref):
        k = k_ref[...]
        lane = lax.broadcasted_iota(jnp.int32, k.shape, 1)
        rolled = pltpu.roll(k.astype(f32), HEAD_DIM, 1).astype(bf16)
        turned = v_ref[...].astype(f32).T
        ones = jnp.ones((HEAD_DIM, rows), bf16)
        q_turned = q_ref[...].astype(f32).T * (SCALE * LOG2E)
        outs = []
        for head in range(2):
            at = head * HEAD_DIM
            k_two = jnp.where(lane < HEAD_DIM, k, rolled) if head == 0 else jnp.where(lane < HEAD_DIM, rolled, k)
            own = turned[at : at + HEAD_DIM].astype(bf16)
            v_turned = jnp.concatenate([own, ones] if head == 0 else [ones, own], 0)
            q_two = jnp.concatenate(split_two(q_turned[at : at + HEAD_DIM]), 0)
            total = peak = None
            for j in range(rows // chunk):
                part = slice(j * chunk, (j + 1) * chunk)
                scores = dot(k_two[part], q_two)
                top = jnp.max(scores.reshape(chunk // 8, 8, rows).max(axis=0), axis=0, keepdims=True)
                higher = top if peak is None else jnp.maximum(peak, top)
                weights = jnp.exp2(scores - higher).astype(bf16)
                add = dot(v_turned[:, part], weights)
                total = add if total is None else total * jnp.exp2(peak - higher) + add
                peak = higher
            row_sum = total[HEAD_DIM - at : HEAD_DIM - at + 1]
            outs.append(total[at : at + HEAD_DIM] / row_sum)
            lse_ref[head : head + 1, :] = peak + jnp.log2(row_sum)
        attended = jnp.concatenate(outs, 0)
        ot_ref[...] = attended
        o_ref[...] = attended.T.astype(bf16)

    by_pair = pl.BlockSpec((rows, LANES), lambda j: (0, j))
    pairs = width // LANES
    return call(
        kernel,
        "attend_forward",
        (pairs,),
        [by_pair] * 3,
        [
            by_pair,
            pl.BlockSpec((LANES, rows), lambda j: (j, 0)),
            pl.BlockSpec((None, 8, rows), lambda j: (j, 0, 0)),
        ],
        [shape((rows, width), bf16), shape((width, rows), f32), shape((pairs, 8, rows), f32)],
        flops=16 * rows * rows * width,
        nbytes=12 * rows * width,
        exps=rows * rows * width // HEAD_DIM,
        weight=1000,
    )(queries, keys, values)


def attend_backward(queries, keys, values, grad_own, grad_other, out_turned, stats, first, pairs):
    rows = queries.shape[0]
    width = LANES * pairs
    block = grad_own.shape[0]
    chunk = 256
    count = rows // block

    def kernel(
        q_ref, k_ref, v_ref, go_ref, gt_ref, ot_ref, lse_ref, dq_ref, dk_ref, dv_ref, sum_ref,
        k_wide, k_turned, v_wide, dk_acc, dv_acc,
    ):
        i = pl.program_id(1)

        @pl.when(i == 0)
        def _():
            k = k_ref[...]
            v = v_ref[...]
            lane = lax.broadcasted_iota(jnp.int32, k.shape, 1)
            k_rolled = pltpu.roll(k.astype(f32), HEAD_DIM, 1).astype(bf16)
            v_rolled = pltpu.roll(v.astype(f32), HEAD_DIM, 1).astype(bf16)
            ones = jnp.where(lane < 3, 1.0, 0.0).astype(bf16)
            k_wide[0] = jnp.concatenate([jnp.where(lane < HEAD_DIM, k, k_rolled), ones], 1)
            k_wide[1] = jnp.concatenate([jnp.where(lane < HEAD_DIM, k_rolled, k), ones], 1)
            tail = jnp.where(lane < HEAD_DIM + 3, 1.0, 0.0).astype(bf16)
            v_wide[0] = jnp.where(lane < HEAD_DIM, v, tail)
            v_wide[1] = jnp.where(lane < HEAD_DIM, v_rolled, tail)
            k_turned[...] = k.astype(f32).T.astype(bf16)
            dk_acc[...] = jnp.zeros_like(dk_acc)
            dv_acc[...] = jnp.zeros_like(dv_acc)
            sum_ref[...] = jnp.zeros_like(sum_ref)

        q_turned = q_ref[...].astype(f32).T
        q_low = q_turned.astype(bf16)
        q_turned = q_turned * (SCALE * LOG2E)
        g_turned = jnp.where(i == 0, go_ref[...], gt_ref[...]).astype(f32).T
        g_low = g_turned.astype(bf16)
        dqs = []
        for head in range(2):
            part = slice(head * HEAD_DIM, (head + 1) * HEAD_DIM)
            q_wide = jnp.concatenate(
                [*split_two(q_turned[part]), stat_rows(-lse_ref[head : head + 1, :], LANES)], 0
            )
            row_dot = jnp.sum(g_turned[part] * ot_ref[part, :], axis=0, keepdims=True)
            g_wide = jnp.concatenate([g_low[part], stat_rows(-row_dot, HEAD_DIM)], 0)
            dq = None
            for j in range(rows // chunk):
                at = pl.ds(j * chunk, chunk)
                probabilities = jnp.exp2(dot(k_wide[head, at, :], q_wide))
                shifted = dot(v_wide[head, at, :], g_wide)
                probs_low = probabilities.astype(bf16)
                score_grad = (probabilities * shifted).astype(bf16)
                dv_acc[part, at] += dot(g_low[part], probs_low, NT)
                dk_acc[part, at] += dot(q_low[part], score_grad, NT)
                add = dot(k_turned[part, at], score_grad)
                dq = add if dq is None else dq + add
            dqs.append(dq)
        dq = (jnp.concatenate(dqs, 0) * SCALE).T
        dq_ref[...] = dq.astype(bf16)
        sum_ref[0:1, :] += jnp.sum(dq, axis=0, keepdims=True)

        @pl.when(i == count - 1)
        def _():
            dk_ref[...] = (dk_acc[...] * SCALE).T.astype(bf16)
            dv = dv_acc[...].T
            dv_ref[...] = dv.astype(bf16)
            sum_ref[1:2, :] = jnp.sum(dv, axis=0, keepdims=True)

    by_query = pl.BlockSpec((block, LANES), lambda j, i: (i, j + first))
    by_key = pl.BlockSpec((rows, LANES), lambda j, i: (0, j + first))
    half = pl.BlockSpec((block, LANES), lambda j, i: (0, j + first))
    turned_spec = pl.BlockSpec((LANES, block), lambda j, i: (j + first, i))
    stat_spec = pl.BlockSpec((None, 8, block), lambda j, i: (j + first, 0, i))
    query_out = pl.BlockSpec((block, LANES), lambda j, i: (i, j))
    key_out = pl.BlockSpec((rows, LANES), lambda j, i: (0, j))
    sum_spec = pl.BlockSpec((8, LANES), lambda j, i: (0, j))
    return call(
        kernel,
        "attend_backward",
        (pairs, count),
        [by_query, by_key, by_key, half, half, turned_spec, stat_spec],
        [query_out, key_out, key_out, sum_spec],
        [shape((rows, width), bf16)] * 3 + [shape((8, width), f32)],
        [
            pltpu.VMEM((2, rows, 2 * LANES), bf16),
            pltpu.VMEM((LANES, rows), bf16),
            pltpu.VMEM((2, rows, LANES), bf16),
            pltpu.VMEM((LANES, rows), f32),
            pltpu.VMEM((LANES, rows), f32),
        ],
        flops=40 * rows * rows * width,
        nbytes=20 * rows * width,
        exps=rows * rows * width // HEAD_DIM,
        weight=1000,
    )(queries, keys, values, grad_own, grad_other, out_turned, stats)


def output_own(tokens, attended, weights, params):
    rows, width = tokens.shape
    cols = weights[0].shape[0]
    block = 256
    many = len(attended)

    def kernel(t_ref, par_ref, *refs):
        total = None
        for a_ref, w_ref in zip(refs[:many], refs[many : 2 * many], strict=True):
            part = dot(a_ref[...], w_ref[...])
            total = part if total is None else total + part
        mid_ref, norm_ref = refs[2 * many :]
        middle = t_ref[...].astype(f32) + total + par_ref[2:3, :]
        mid_ref[...] = middle
        unit, _ = normalize(middle)
        norm_ref[...] = (unit * par_ref[3:4, :] + par_ref[4:5, :]).astype(bf16)

    spec = pl.BlockSpec((block, width), lambda i: (i, 0))
    thin = pl.BlockSpec((block, cols), lambda i: (i, 0))
    return call(
        kernel,
        "output_own",
        (rows // block,),
        [spec, whole(params)] + [thin] * many + [whole(w) for w in weights],
        [spec, spec],
        [shape((rows, width), f32), shape((rows, width), bf16)],
        flops=2 * rows * many * cols * width,
        nbytes=2 * rows * many * cols + 8 * rows * width,
    )(tokens, params, *attended, *weights)


def feed_forward(norm_own, norm_other, cot_own, cot_other, bias, up, down, scal, earlier=None):
    rows, width = norm_own.shape
    hidden = bias.shape[1]
    block = 256
    count = rows // block
    last = earlier is not None
    (up, up_place), (down, down_place) = up, down
    slices, depth = up.shape[0], up.shape[2]
    term_type = bf16

    def kernel(scal_ref, no_ref, nt_ref, co_ref, ct_ref, b_ref, up_ref, dn_ref, *refs):
        if last:
            ff_in, ng_in, ffo_ref, ngo_ref, fft_ref, ngt_ref, *refs = refs
        else:
            ff_ref, ng_ref, *refs = refs
        up_term, down_term, sum_ref, up_acc, down_acc = refs
        i = pl.program_id(0)

        @pl.when(i == 0)
        def _():
            up_acc[...] = jnp.zeros_like(up_acc)
            down_acc[...] = jnp.zeros_like(down_acc)
            sum_ref[...] = jnp.zeros_like(sum_ref)

        x = pick(count, no_ref, nt_ref)
        cot = pick(count, co_ref, ct_ref)
        up_now = up_ref[...].reshape(width, hidden)
        down_now = dn_ref[...].reshape(hidden, width)
        h = dot(x, up_now) + b_ref[0:1, :]
        cdf = 0.5 * (1.0 + lax.erf(h * RSQRT2))
        act = (h * cdf).astype(bf16)
        slope = cdf + h * (RSQRT2PI * jnp.exp(-0.5 * h * h))
        ff = dot(act, down_now)
        grad = dot(cot, down_now, NT) * slope
        sum_ref[7:8, :] += jnp.sum(grad, axis=0, keepdims=True)
        low = grad.astype(bf16)
        ng = dot(low, up_now, NT)
        up_acc[...] += dot(x, low, TN)
        down_acc[...] += dot(act, cot, TN)
        if last:
            ff = ff + ff_in[...]
            ng = ng + ng_in[...]

            @pl.when(i < count)
            def _():
                ffo_ref[...] = ff
                ngo_ref[...] = ng

            @pl.when(i >= count)
            def _():
                fft_ref[...] = ff.astype(bf16)
                ngt_ref[...] = ng.astype(bf16)
        else:
            ff_ref[...] = ff
            ng_ref[...] = ng

        @pl.when(i == 2 * count - 1)
        def _():
            units = scal_ref[1]
            up_term[...] = (up_acc[...] * units).astype(term_type)
            down_term[...] = (down_acc[...] * units).astype(term_type)
            sum_ref[...] = sum_ref[...] * units

    own, other = halves(block, width, count)
    every = pl.BlockSpec((block, width), lambda i: (i, 0))
    up_spec, down_spec = (
        pl.BlockSpec(
            (slices, None, depth, width), lambda i, j=j: (0, j, 0, 0), pipeline_mode=pl.Buffered(1)
        )
        for j in (up_place, down_place)
    )
    ins = [scalars(), own, other, own, other, whole(bias), up_spec, down_spec]
    args = [scal, norm_own, norm_other, cot_own, cot_other, bias, up, down]
    if last:
        ins += [every, every]
        args += list(earlier)
        outs = [own, own, other, other]
        shapes = [shape((rows, width), f32)] * 2 + [shape((rows, width), bf16)] * 2
    else:
        outs = [every, every]
        shapes = [shape((2 * rows, width), f32)] * 2
    terms = [shape((width, hidden), term_type), shape((hidden, width), term_type)]
    sums = shape((8, hidden), f32)
    return call(
        kernel,
        "feed_forward",
        (2 * count,),
        ins,
        outs + [whole(terms[0]), whole(terms[1]), whole(sums)],
        shapes + terms + [sums],
        [pltpu.VMEM((width, hidden), f32), pltpu.VMEM((hidden, width), f32)],
        flops=24 * rows * width * hidden,
        nbytes=24 * rows * width + 12 * width * hidden,
        exps=4 * rows * hidden,
        weight=1000 if last else 1e-6,
    )(*args)


def second_back(middle, grad_own, grad_received, cot, params, scal):
    rows, width = middle.shape
    block = 256
    last = rows // block - 1

    def kernel(scal_ref, mid_ref, go_ref, gr_ref, cot_ref, par_ref, out_ref, low_ref, sum_ref):
        i = pl.program_id(0)
        unit, inverse = normalize(mid_ref[...])
        grad = go_ref[...] + gr_ref[...].astype(f32)
        cot = cot_ref[...].astype(f32)
        out = cot + norm_back(grad, par_ref[3:4, :], unit, inverse)
        out_ref[...] = out
        low_ref[...] = out.astype(bf16)
        sums = [jnp.sum(v, axis=0, keepdims=True) for v in (grad * unit, grad, out, cot)]
        add_rows(sum_ref, sums, i == 0, 2)

        @pl.when(i == last)
        def _():
            sum_ref[...] = sum_ref[...] * scal_ref[1]

    spec = pl.BlockSpec((block, width), lambda i: (i, 0))
    sums = shape((8, width), f32)
    return call(
        kernel,
        "second_back",
        (rows // block,),
        [scalars(), spec, spec, spec, spec, whole(params)],
        [spec, spec, whole(sums)],
        [shape((rows, width), f32), shape((rows, width), bf16), sums],
        flops=30 * rows * width,
        nbytes=18 * rows * width,
    )(scal, middle, grad_own, grad_received, cot, params)


def output_back(low, attended, weights, scal, earlier=None):
    rows, width = low.shape
    cols = weights[0].shape[0]
    block = 512
    last = earlier is not None
    start = rows // block if last else 0

    def kernel(scal_ref, low_ref, a_ref, b_ref, wa_ref, wb_ref, *refs):
        before = refs[:2] if last else (None, None)
        ga_ref, gb_ref, ta_ref, tb_ref, acc_a, acc_b = refs[2 if last else 0 :]
        i = pl.program_id(0)
        now = low_ref[...]
        ga_ref[...] = dot(now, wa_ref[...], NT).astype(bf16)
        gb_ref[...] = dot(now, wb_ref[...], NT).astype(bf16)
        for acc, rows_ref, old in ((acc_a, a_ref, before[0]), (acc_b, b_ref, before[1])):

            @pl.when(i == 0)
            def _():
                acc[...] = jnp.zeros_like(acc) if old is None else old[...]

            acc[...] += dot(rows_ref[...], now, TN)

        @pl.when(i == rows // block - 1)
        def _():
            factor = scal_ref[1] if last else 1.0
            ta_ref[...] = (acc_a[...] * factor).astype(ta_ref.dtype)
            tb_ref[...] = (acc_b[...] * factor).astype(tb_ref.dtype)

    thin = pl.BlockSpec((block, cols), lambda i: (i, 0))
    rows_in = pl.BlockSpec((block, cols), lambda i: (i + start, 0))
    terms = [shape((cols, width), bf16 if last else f32)] * 2
    before = list(earlier or ())
    return call(
        kernel,
        "output_back",
        (rows // block,),
        [scalars(), pl.BlockSpec((block, width), lambda i: (i, 0)), rows_in, rows_in]
        + [whole(w) for w in weights]
        + [whole(t) for t in before],
        [thin, thin, whole(terms[0]), whole(terms[1])],
        [shape((rows, cols), bf16)] * 2 + terms,
        [pltpu.VMEM((cols, width), f32)] * 2,
        flops=8 * rows * width * cols,
        nbytes=2 * rows * width + 8 * rows * cols,
        weight=1e-6 if last else 1000,
    )(scal, low, *attended, *weights, *before)


def input_term(norm_own, norm_other, parts, scal, other=None):
    rows, width = norm_own.shape
    count = len(parts)
    grads = [part[j] for j in range(3) for part in parts]
    more = [] if other is None else [other]

    def kernel(scal_ref, no_ref, nt_ref, *refs):
        out_ref = refs[-1]
        for j in range(3):

            @pl.when(pl.program_id(0) == j)
            def _():
                grad = jnp.concatenate([r[...] for r in refs[count * j : count * j + count]], 1)
                term = dot(no_ref[...], grad[:rows, :], TN) + dot(nt_ref[...], grad[rows:, :], TN)
                term = term * scal_ref[1]
                if more:
                    term = term + refs[-2][...].astype(f32)
                out_ref[...] = term.astype(bf16)

    cols = sum(part[0].shape[1] for part in parts)
    out_spec = pl.BlockSpec((width, cols), lambda j: (j, 0))
    return call(
        kernel,
        "input_term",
        (3,),
        [scalars(), whole(norm_own), whole(norm_other)]
        + [whole(g) for g in grads]
        + [out_spec] * len(more),
        out_spec,
        shape((3 * width, cols), bf16),
        flops=12 * rows * width * cols,
        nbytes=4 * rows * width + 12 * rows * cols + 12 * width * cols,
    )(scal, norm_own, norm_other, *grads, *more)


def norm1_part(refs, weights, counts):
    total = None
    place = 0
    for w_ref, count in zip(weights, counts, strict=True):
        for j in range(3):
            grad = jnp.concatenate([r[...] for r in refs[place : place + count]], 1)
            part = dot(grad, w_ref[j], NT)
            total = part if total is None else total + part
            place += count
    return total


def flat(quarters):
    return [part[j] for parts in quarters for j in range(3) for part in parts]


def row_specs(grads, block, start):
    return [pl.BlockSpec((block, g.shape[1]), lambda i: (i + start, 0)) for g in grads]


def norm1_other(quarters, weights):
    grads = flat(quarters)
    rows = grads[0].shape[0] // 2
    width, cols = weights[0].shape[1:]
    block = 256
    many = len(grads)
    counts = [len(parts) for parts in quarters]

    def kernel(*refs):
        refs[-1][...] = norm1_part(refs[:many], refs[many:-1], counts).astype(bf16)

    return call(
        kernel,
        "first_other",
        (rows // block,),
        row_specs(grads, block, rows // block) + [whole(w) for w in weights],
        pl.BlockSpec((block, width), lambda i: (i, 0)),
        shape((rows, width), bf16),
        flops=12 * rows * width * cols,
        nbytes=12 * rows * cols + 2 * rows * width + 12 * width * cols,
    )(*grads, *weights)


def norm1_own(quarters, weights, received, tokens, middle_grad, params, scal):
    grads = flat(quarters)
    rows, width = tokens.shape
    cols = weights[0].shape[2]
    block = 256
    last = rows // block - 1
    many = len(grads)
    counts = [len(parts) for parts in quarters]

    def kernel(scal_ref, *refs):
        rec_ref, tok_ref, mid_ref, par_ref, out_ref, sum_ref = refs[many + len(weights) :]
        i = pl.program_id(0)
        grad = norm1_part(refs[:many], refs[many : many + len(weights)], counts)
        grad += rec_ref[...].astype(f32)
        unit, inverse = normalize(tok_ref[...].astype(f32))
        out = mid_ref[...] + norm_back(grad, par_ref[0:1, :], unit, inverse)
        out_ref[...] = out.astype(bf16)
        sums = [jnp.sum(v, axis=0, keepdims=True) for v in (grad * unit, grad)]
        add_rows(sum_ref, sums, i == 0, 0)

        @pl.when(i == last)
        def _():
            sum_ref[...] = sum_ref[...] * scal_ref[1]

    spec = pl.BlockSpec((block, width), lambda i: (i, 0))
    sums = shape((8, width), f32)
    return call(
        kernel,
        "first_own",
        (rows // block,),
        [scalars()]
        + row_specs(grads, block, 0)
        + [whole(w) for w in weights]
        + [spec] * 3
        + [whole(params)],
        [spec, whole(sums)],
        [shape((rows, width), bf16), sums],
        flops=12 * rows * width * cols,
        nbytes=12 * rows * cols + 10 * rows * width + 12 * width * cols,
    )(scal, *grads, *weights, received, tokens, middle_grad, params)


def body(
    tokens,
    out_grad,
    item_counts,
    group_dataset,
    variable_mask,
    first_gain,
    first_shift,
    input_weight,
    input_bias,
    output_weight,
    output_bias,
    second_gain,
    second_shift,
    up_weight,
    up_bias,
    down_weight,
    down_bias,
):
    shard_count = lax.axis_size("mp")
    groups = lax.axis_size("dp")
    rows, width = tokens.shape
    cols = input_weight.shape[2]
    hidden = up_weight.shape[1]

    def core_swap(value):
        return lax.ppermute(value, "mp", [(i, i ^ 1) for i in range(shard_count)])

    def chip_swap(value):
        return lax.ppermute(value, "mp", [(i, i ^ 2) for i in range(shard_count)])

    def after(value, *others):
        return lax.optimization_barrier((value, *others))[0]

    def along(value, bit):
        return lax.ppermute(value, "dp", [(i, i ^ bit) for i in range(groups)])

    group = lax.axis_index("dp")

    slice_rows = up_weight.shape[0] // groups
    slices = [
        lax.dynamic_slice_in_dim(weight, group * slice_rows, slice_rows, 0)
        for weight in (up_weight, down_weight)
    ]
    slice_two = chip_swap(jnp.stack(slices)[None])
    ff_weights_two = lax.all_gather(slice_two, "dp", axis=0, tiled=True)
    bias_pack = jnp.concatenate([up_bias, input_bias[0], input_bias[1]]).reshape(-1, LANES)
    bias_two = chip_swap(after(bias_pack, slice_two))
    wi_two = chip_swap(after(input_weight, slice_two))
    wo_two = chip_swap(after(output_weight, bias_two))

    live = (lax.axis_index("mp") // 2 < item_counts[0]).astype(f32)
    dataset_hit = jnp.arange(variable_mask.shape[0], dtype=jnp.int32) == group_dataset[0]
    own_units = (
        item_counts[0] * jnp.sum(jnp.where(dataset_hit[:, None], variable_mask, 0))
    ).astype(f32)
    scal = jnp.stack([live, own_units])
    zero = jnp.zeros((width,), f32)
    params = jnp.stack(
        [first_gain, first_shift, output_bias, second_gain, second_shift, down_bias, zero, zero]
    )

    normed1, cot = first_norm(tokens, out_grad, params, scal)
    normed1_t = core_swap(normed1)
    cot_t = core_swap(cot)

    qkv_one = project(normed1, input_weight, input_bias)
    qkv_one = project(normed1_t, input_weight, after(input_bias, qkv_one[0]), qkv_one)
    att_one, turned_one, stat_one = attend_forward(*qkv_one)
    att_one_t = core_swap(att_one[rows:])
    wo_one_t = core_swap(output_weight)
    bias_two = bias_two.reshape(-1)
    up_bias_one = up_bias.reshape(1, hidden)
    up_bias_two = bias_two[:hidden].reshape(1, hidden)
    in_bias_two = bias_two[hidden:].reshape(2, cols)
    qkv_two = project(after(normed1, att_one), wi_two, in_bias_two)
    qkv_two = project(normed1_t, wi_two, after(in_bias_two, att_one_t), qkv_two)
    att_two, turned_two, stat_two = attend_forward(*qkv_two)
    wo_two_t = core_swap(after(wo_two, qkv_two[0]))
    att_two_t = core_swap(att_two[rows:])
    middle, normed2 = output_own(
        tokens,
        [att_one, att_two, att_one_t, after(att_two_t, ff_weights_two)],
        [output_weight, wo_two, wo_one_t, wo_two_t],
        params,
    )
    normed2_t = core_swap(normed2)

    ff_two, ng_two, up_two_term, down_two_term, up_sum_two = feed_forward(
        normed2, normed2_t, cot, cot_t, up_bias_two, (ff_weights_two, 0), (ff_weights_two, 1), scal
    )
    up_received = chip_swap(up_two_term)
    up_one, down_one = ((w.reshape(1, 1, -1, width), 0) for w in (up_weight, down_weight))
    ff_own, ng_own, ff_send, ng_send, up_one_term, down_one_term, up_sum_one = feed_forward(
        normed2, normed2_t, cot, cot_t, up_bias_one, up_one, down_one, scal, (ff_two, ng_two)
    )
    ng_received = core_swap(ng_send)
    down_received = chip_swap(after(down_two_term, up_received))
    middle_grad, middle_low, second_sums = second_back(
        middle, ng_own, after(ng_received, up_received), cot, params, scal
    )
    middle_low_t = core_swap(middle_low)
    out_weights = [output_weight, wo_two]
    g_one, g_two, *wo_terms = output_back(middle_low, [att_one, att_two], out_weights, scal)
    g_one_t, g_two_t, wo_one_term, wo_two_term = output_back(
        middle_low_t, [att_one, att_two], out_weights, scal, wo_terms
    )

    def both(own, received, *last):
        return (own.astype(f32) + after(received, *last).astype(f32)).astype(bf16)

    parts_two = [attend_backward(*qkv_two, g_two, g_two_t, turned_two, stat_two, 0, 1)]
    wait = parts_two[0][0]
    up_both = both(up_one_term, up_received, wait)
    down_both = both(down_one_term, down_received, wait)
    up_sum, down_sum = lax.psum((up_both, down_both), "dp")
    g_two = after(g_two, up_both, down_both, wait)
    parts_two.append(attend_backward(*qkv_two, g_two, g_two_t, turned_two, stat_two, 1, cols // LANES - 1))
    wi_two_term = input_term(normed1, normed1_t, parts_two, scal)
    ff_received = core_swap(after(ff_send, wait))
    wo_received = chip_swap(after(wo_two_term, parts_two[1][0]))
    wi_received = chip_swap(wi_two_term)
    g_one = after(g_one, wi_two_term)
    parts_one = [attend_backward(*qkv_one, g_one, g_one_t, turned_one, stat_one, 0, cols // LANES)]
    wi_both = input_term(normed1, normed1_t, parts_one, scal, after(wi_received, wo_received))
    quarters = [parts_one, parts_two]
    weights = [input_weight, wi_two]
    ng1_received = core_swap(norm1_other(quarters, [input_weight, after(wi_two, wi_both)]))
    token_grad, first_sums = norm1_own(
        quarters, weights, ng1_received, tokens, middle_grad, params, scal
    )
    result = live * (middle + ff_own + ff_received.astype(f32) + down_bias)
    result = result.astype(bf16)

    def columns(term):
        return jnp.concatenate([term[:, k * cols : (k + 1) * cols] for k in range(width // cols)])

    wo_both = columns(both(wo_one_term, wo_received))
    middle_row = (wi_both.shape[0] + wo_both.shape[0]) // 2
    parts = [wi_both[:middle_row], jnp.concatenate([wi_both[middle_row:], wo_both])]
    bits = [1 << k for k in range(groups.bit_length() - 1)]
    orders = [bits, bits[1:] + bits[:1]]

    def upper(bit):
        return (group // bit) % 2

    for turn in range(len(bits)):
        if turn == 1:
            parts = [after(part, token_grad) for part in parts]
        for k in range(2):
            bit = orders[k][turn]
            half = parts[k].shape[0] // 2
            keep = lax.dynamic_slice_in_dim(parts[k], upper(bit) * half, half, 0)
            send = lax.dynamic_slice_in_dim(parts[k], (1 - upper(bit)) * half, half, 0)
            parts[k] = both(keep, along(send, bit))
    for turn in reversed(range(len(bits))):
        for k in range(2):
            bit = orders[k][turn]
            received = along(parts[k], bit)
            is_upper = upper(bit) == 1
            parts[k] = jnp.concatenate(
                [jnp.where(is_upper, received, parts[k]), jnp.where(is_upper, parts[k], received)]
            )
    wi_rows = 3 * width
    tail_sum = jnp.concatenate(parts)
    wi_sum = tail_sum[:wi_rows].reshape(3, width, cols)
    wo_sum = tail_sum[wi_rows:].reshape(width // cols, cols, cols)
    wo_sum = jnp.concatenate([wo_sum[k] for k in range(width // cols)], 1)

    def quarter_rows(parts, up_sums):
        sums_all = jnp.concatenate([part[3] for part in parts], 1)
        rest = jnp.full((1, width - 2 * cols), own_units)
        bias_row = jnp.concatenate([sums_all[0:1] * own_units, sums_all[1:2] * own_units, rest], 1)
        return up_sums + jnp.pad(bias_row, ((6, 1), (0, 0)))

    late = first_sums + second_sums
    late = late + core_swap(late)
    late_one = late + quarter_rows(parts_one, up_sum_one)
    late = late_one + chip_swap(late + quarter_rows(parts_two, up_sum_two))
    for bit in bits:
        late = late + along(late, bit)
    share = 2.0 / late[6, -1]
    late = late * share

    return (
        result,
        token_grad,
        late[0],
        late[1],
        wi_sum.astype(f32) * share,
        late[6, : 2 * cols].reshape(2, cols),
        wo_sum.astype(f32) * share,
        late[4],
        late[2],
        late[3],
        up_sum.astype(f32) * share,
        late[7],
        down_sum.astype(f32) * share,
        late[5],
    )


def solution(mesh):
    in_specs = (
        P(("dp", "mp"), None),
        P(("dp", "mp"), None),
        P("dp"),
        P("dp"),
        P(),
        P(),
        P(),
        P(None, None, "mp"),
        P(None, "mp"),
        P("mp", None),
        P(),
        P(),
        P(),
        P(None, "mp"),
        P("mp"),
        P("mp", None),
        P(),
    )
    out_specs = (
        P(("dp", "mp"), None),
        P(("dp", "mp"), None),
        P(),
        P(),
        P(None, None, "mp"),
        P(None, "mp"),
        P("mp", None),
        P(),
        P(),
        P(),
        P(None, "mp"),
        P("mp"),
        P("mp", None),
        P(),
    )
    return jax.shard_map(body, mesh=mesh, in_specs=in_specs, out_specs=out_specs, check_vma=False)
```

```python
import jax
import jax.numpy as jnp
from jax import lax
from jax.experimental import pallas as pl
from jax.experimental.pallas import tpu as pltpu
from jax.sharding import PartitionSpec as P

HEAD_DIM = 64
LANES = 128
norm_eps = 1e-06
SCALE = HEAD_DIM**-0.5
LOG2E = 1.4426950408889634
RSQRT2 = 0.7071067811865476
RSQRT2PI = 0.3989422804014327

bf16 = jnp.bfloat16
f32 = jnp.float32
NN = (((1,), (0,)), ((), ()))
NT = (((1,), (1,)), ((), ()))
TN = (((0,), (0,)), ((), ()))
VMEM_BYTES = 60 << 20


def dot(left, right, dims=NN):
    return lax.dot_general(left, right, dims, preferred_element_type=f32)


def shape(dims, dtype):
    return jax.ShapeDtypeStruct(dims, dtype)


def whole(array):
    rank = len(array.shape)
    return pl.BlockSpec(array.shape, lambda *_: (0,) * rank, pipeline_mode=pl.Buffered(1))


def scalars():
    return pl.BlockSpec(memory_space=pltpu.SMEM)


def call(kernel, name, grid, in_specs, out_specs, out_shape, scratch=(), flops=0, nbytes=0, exps=0, weight=1e-6, aliases=None):
    return pl.pallas_call(
        kernel,
        name=name,
        grid=grid,
        in_specs=in_specs,
        out_specs=out_specs,
        out_shape=out_shape,
        scratch_shapes=list(scratch),
        input_output_aliases=aliases or {},
        compiler_params=pltpu.CompilerParams(vmem_limit_bytes=VMEM_BYTES),
        cost_estimate=pl.CostEstimate(
            flops=int(flops * weight), bytes_accessed=int(nbytes * weight), transcendentals=int(exps * weight)
        ),
    )


def split_two(values):
    high = values.astype(bf16)
    return high, (values - high.astype(f32)).astype(bf16)


def split_three(values):
    high = values.astype(bf16)
    rest = values - high.astype(f32)
    mid = rest.astype(bf16)
    return high, mid, (rest - mid.astype(f32)).astype(bf16)


def stat_rows(vector, rows):
    high, mid, rest = (part.astype(f32) for part in split_three(vector))
    row = lax.broadcasted_iota(jnp.int32, (rows, vector.shape[1]), 0)
    return jnp.where(
        row == 0, high, jnp.where(row == 1, mid, jnp.where(row == 2, rest, 0.0))
    ).astype(bf16)


def normalize(values):
    centered = values - jnp.mean(values, axis=-1, keepdims=True)
    variance = jnp.mean(centered * centered, axis=-1, keepdims=True)
    inverse = lax.rsqrt(variance + norm_eps)
    return centered * inverse, inverse


def norm_back(grad, gain, unit, inverse):
    scaled = grad * gain
    return inverse * (
        scaled
        - jnp.mean(scaled, axis=-1, keepdims=True)
        - unit * jnp.mean(scaled * unit, axis=-1, keepdims=True)
    )


def add_rows(ref, rows, first, start):
    @pl.when(first)
    def _():
        ref[...] = jnp.zeros_like(ref)

    for place, row in enumerate(rows):
        ref[start + place : start + place + 1, :] += row


def first_norm(tokens, gain, shift):
    rows, width = tokens.shape
    block = 256

    def kernel(tok_ref, gain_ref, shift_ref, norm_ref):
        unit, _ = normalize(tok_ref[...].astype(f32))
        gain_row = gain_ref[...].reshape(1, width)
        norm_ref[...] = (unit * gain_row + shift_ref[...].reshape(1, width)).astype(bf16)

    spec = pl.BlockSpec((block, width), lambda i: (i, 0))
    return call(
        kernel,
        "first_norm",
        (rows // block,),
        [spec, whole(gain), whole(shift)],
        spec,
        shape((rows, width), bf16),
        flops=20 * rows * width,
        nbytes=4 * rows * width,
    )(tokens, gain, shift)


def halves(block, width, count):
    own = pl.BlockSpec((block, width), lambda i, *_: (jnp.minimum(i, count - 1), 0))
    other = pl.BlockSpec((block, width), lambda i, *_: (jnp.maximum(i - count, 0), 0))
    return own, other


def pick(count, own_ref, other_ref):
    return jnp.where(pl.program_id(0) < count, own_ref[...], other_ref[...])


def project(norm, weight, bias, earlier=None):
    rows, width = norm.shape
    cols = weight.shape[2]
    block = 512
    start = 0 if earlier is None else rows // block
    skip = 0 if earlier is None else 3

    def kernel(x_ref, w_ref, b_ref, *refs):
        q_ref, k_ref, v_ref = refs[skip:]
        x = x_ref[...]
        q_ref[...] = (dot(x, w_ref[0]) + b_ref[0:1, :]).astype(bf16)
        k_ref[...] = dot(x, w_ref[1]).astype(bf16)
        v_ref[...] = (dot(x, w_ref[2]) + b_ref[1:2, :]).astype(bf16)

    out = pl.BlockSpec((block, cols), lambda i: (i + start, 0))
    return call(
        kernel,
        "project",
        (rows // block,),
        [pl.BlockSpec((block, width), lambda i: (i, 0)), whole(weight), whole(bias)]
        + [pl.BlockSpec(memory_space=pl.ANY)] * skip,
        [out] * 3,
        [shape((2 * rows, cols), bf16)] * 3,
        flops=6 * rows * width * cols,
        nbytes=2 * rows * width + 6 * width * cols + 6 * rows * cols,
        weight=1000,
        aliases={3 + k: k for k in range(skip)},
    )(norm, weight, bias, *(earlier or ()))


def attend_forward(queries, keys, values):
    rows, width = queries.shape
    chunk = min(512, rows)

    def kernel(q_ref, k_ref, v_ref, own_ref, other_ref, ot_ref, lse_ref):
        k = k_ref[...]
        lane = lax.broadcasted_iota(jnp.int32, k.shape, 1)
        rolled = pltpu.roll(k.astype(f32), HEAD_DIM, 1).astype(bf16)
        turned = v_ref[...].astype(f32).T
        ones = jnp.ones((HEAD_DIM, rows), bf16)
        q_turned = q_ref[...].astype(f32).T * (SCALE * LOG2E)
        outs = []
        for head in range(2):
            at = head * HEAD_DIM
            k_two = jnp.where(lane < HEAD_DIM, k, rolled) if head == 0 else jnp.where(lane < HEAD_DIM, rolled, k)
            own = turned[at : at + HEAD_DIM].astype(bf16)
            v_turned = jnp.concatenate([own, ones] if head == 0 else [ones, own], 0)
            q_two = jnp.concatenate(split_two(q_turned[at : at + HEAD_DIM]), 0)
            total = peak = None
            for j in range(rows // chunk):
                part = slice(j * chunk, (j + 1) * chunk)
                scores = dot(k_two[part], q_two)
                top = jnp.max(scores.reshape(chunk // 8, 8, rows).max(axis=0), axis=0, keepdims=True)
                higher = top if peak is None else jnp.maximum(peak, top)
                weights = jnp.exp2(scores - higher).astype(bf16)
                add = dot(v_turned[:, part], weights)
                total = add if total is None else total * jnp.exp2(peak - higher) + add
                peak = higher
            row_sum = total[HEAD_DIM - at : HEAD_DIM - at + 1]
            outs.append(total[at : at + HEAD_DIM] / row_sum)
            lse_ref[head : head + 1, :] = peak + jnp.log2(row_sum)
        attended = jnp.concatenate(outs, 0)
        ot_ref[...] = attended
        own_ref[...] = attended[:, : rows // 2].T.astype(bf16)
        other_ref[...] = attended[:, rows // 2 :].T.astype(bf16)

    by_pair = pl.BlockSpec((rows, LANES), lambda j: (0, j))
    by_half = pl.BlockSpec((rows // 2, LANES), lambda j: (0, j))
    pairs = width // LANES
    return call(
        kernel,
        "attend_forward",
        (pairs,),
        [by_pair] * 3,
        [
            by_half,
            by_half,
            pl.BlockSpec((LANES, rows), lambda j: (j, 0)),
            pl.BlockSpec((None, 8, rows), lambda j: (j, 0, 0)),
        ],
        [shape((rows // 2, width), bf16)] * 2
        + [shape((width, rows), f32), shape((pairs, 8, rows), f32)],
        flops=16 * rows * rows * width,
        nbytes=12 * rows * width,
        exps=rows * rows * width // HEAD_DIM,
        weight=1000,
    )(queries, keys, values)


def attend_backward(queries, keys, values, grad_own, grad_other, out_turned, stats, first, pairs):
    rows = queries.shape[0]
    width = LANES * pairs
    block = grad_own.shape[0]
    chunk = 256
    count = rows // block

    def kernel(
        q_ref, k_ref, v_ref, go_ref, gt_ref, ot_ref, lse_ref, d_ref, sum_ref,
        k_wide, k_turned, v_wide, dk_acc, dv_acc,
    ):
        i = pl.program_id(1)

        @pl.when(i == 0)
        def _():
            k = k_ref[...]
            v = v_ref[...]
            lane = lax.broadcasted_iota(jnp.int32, k.shape, 1)
            k_rolled = pltpu.roll(k.astype(f32), HEAD_DIM, 1).astype(bf16)
            v_rolled = pltpu.roll(v.astype(f32), HEAD_DIM, 1).astype(bf16)
            ones = jnp.where(lane < 3, 1.0, 0.0).astype(bf16)
            k_wide[0] = jnp.concatenate([jnp.where(lane < HEAD_DIM, k, k_rolled), ones], 1)
            k_wide[1] = jnp.concatenate([jnp.where(lane < HEAD_DIM, k_rolled, k), ones], 1)
            tail = jnp.where(lane < HEAD_DIM + 3, 1.0, 0.0).astype(bf16)
            v_wide[0] = jnp.where(lane < HEAD_DIM, v, tail)
            v_wide[1] = jnp.where(lane < HEAD_DIM, v_rolled, tail)
            k_turned[...] = k.astype(f32).T.astype(bf16)
            dk_acc[...] = jnp.zeros_like(dk_acc)
            dv_acc[...] = jnp.zeros_like(dv_acc)
            sum_ref[...] = jnp.zeros_like(sum_ref)

        q_turned = q_ref[...].astype(f32).T
        q_low = q_turned.astype(bf16)
        q_turned = q_turned * (SCALE * LOG2E)
        g_turned = jnp.where(i == 0, go_ref[...], gt_ref[...]).astype(f32).T
        g_low = g_turned.astype(bf16)
        dqs = []
        for head in range(2):
            part = slice(head * HEAD_DIM, (head + 1) * HEAD_DIM)
            q_wide = jnp.concatenate(
                [*split_two(q_turned[part]), stat_rows(-lse_ref[head : head + 1, :], LANES)], 0
            )
            row_dot = jnp.sum(g_turned[part] * ot_ref[part, :], axis=0, keepdims=True)
            g_wide = jnp.concatenate([g_low[part], stat_rows(-row_dot, HEAD_DIM)], 0)
            dq = None
            for j in range(rows // chunk):
                at = pl.ds(j * chunk, chunk)
                probabilities = jnp.exp2(dot(k_wide[head, at, :], q_wide))
                shifted = dot(v_wide[head, at, :], g_wide)
                probs_low = probabilities.astype(bf16)
                score_grad = (probabilities * shifted).astype(bf16)
                dv_acc[part, at] += dot(g_low[part], probs_low, NT)
                dk_acc[part, at] += dot(q_low[part], score_grad, NT)
                add = dot(k_turned[part, at], score_grad)
                dq = add if dq is None else dq + add
            dqs.append(dq)
        dq = (jnp.concatenate(dqs, 0) * SCALE).T
        d_ref[pl.ds(i * block, block), :LANES] = dq.astype(bf16)
        sum_ref[0:1, :] += jnp.sum(dq, axis=0, keepdims=True)

        @pl.when(i == count - 1)
        def _():
            d_ref[:, LANES : 2 * LANES] = (dk_acc[...] * SCALE).T.astype(bf16)
            dv = dv_acc[...].T
            d_ref[:, 2 * LANES :] = dv.astype(bf16)
            sum_ref[1:2, :] = jnp.sum(dv, axis=0, keepdims=True)

    by_query = pl.BlockSpec((block, LANES), lambda j, i: (i, j + first))
    by_key = pl.BlockSpec((rows, LANES), lambda j, i: (0, j + first))
    half = pl.BlockSpec((block, LANES), lambda j, i: (0, j + first))
    turned_spec = pl.BlockSpec((LANES, block), lambda j, i: (j + first, i))
    stat_spec = pl.BlockSpec((None, 8, block), lambda j, i: (j + first, 0, i))
    out_spec = pl.BlockSpec((None, rows, 3 * LANES), lambda j, i: (j, 0, 0))
    sum_spec = pl.BlockSpec((8, LANES), lambda j, i: (0, j))
    return call(
        kernel,
        "attend_backward",
        (pairs, count),
        [by_query, by_key, by_key, half, half, turned_spec, stat_spec],
        [out_spec, sum_spec],
        [shape((pairs, rows, 3 * LANES), bf16), shape((8, width), f32)],
        [
            pltpu.VMEM((2, rows, 2 * LANES), bf16),
            pltpu.VMEM((LANES, rows), bf16),
            pltpu.VMEM((2, rows, LANES), bf16),
            pltpu.VMEM((LANES, rows), f32),
            pltpu.VMEM((LANES, rows), f32),
        ],
        flops=40 * rows * rows * width,
        nbytes=20 * rows * width,
        exps=rows * rows * width // HEAD_DIM,
        weight=1000,
    )(queries, keys, values, grad_own, grad_other, out_turned, stats)


def output_own(tokens, attended, weights, params):
    rows, width = tokens.shape
    cols = weights[0].shape[0]
    block = 256
    many = len(attended)

    def kernel(t_ref, par_ref, *refs):
        total = None
        for a_ref, w_ref in zip(refs[:many], refs[many : 2 * many], strict=True):
            part = dot(a_ref[...], w_ref[...])
            total = part if total is None else total + part
        mid_ref, norm_ref = refs[2 * many :]
        middle = t_ref[...].astype(f32) + total + par_ref[2:3, :]
        mid_ref[...] = middle
        unit, _ = normalize(middle)
        norm_ref[...] = (unit * par_ref[3:4, :] + par_ref[4:5, :]).astype(bf16)

    spec = pl.BlockSpec((block, width), lambda i: (i, 0))
    thin = pl.BlockSpec((block, cols), lambda i: (i, 0))
    return call(
        kernel,
        "output_own",
        (rows // block,),
        [spec, whole(params)] + [thin] * many + [whole(w) for w in weights],
        [spec, spec],
        [shape((rows, width), f32), shape((rows, width), bf16)],
        flops=2 * rows * many * cols * width,
        nbytes=2 * rows * many * cols + 8 * rows * width,
    )(tokens, params, *attended, *weights)


def feed_forward(norm_own, norm_other, cot_own, cot_other, bias, up, down, scal, earlier=None):
    rows, width = norm_own.shape
    hidden = bias.shape[1]
    block = 256
    count = rows // block
    last = earlier is not None
    (up, up_place), (down, down_place) = up, down
    slices, depth = up.shape[0], up.shape[2]
    def kernel(scal_ref, no_ref, nt_ref, co_ref, ct_ref, b_ref, up_ref, dn_ref, *refs):
        if last:
            ff_in, ng_in, ffo_ref, ngo_ref, fft_ref, ngt_ref, *refs = refs
        else:
            ff_ref, ng_ref, *refs = refs
        keep, send, sum_ref, up_acc, down_acc = refs
        i = pl.program_id(0)

        @pl.when(i == 0)
        def _():
            up_acc[...] = jnp.zeros_like(up_acc)
            down_acc[...] = jnp.zeros_like(down_acc)
            sum_ref[...] = jnp.zeros_like(sum_ref)

        x = pick(count, no_ref, nt_ref)
        cot = (pick(count, co_ref, ct_ref).astype(f32) * scal_ref[0]).astype(bf16)
        up_now = up_ref[...].reshape(width, hidden)
        down_now = dn_ref[...].reshape(hidden, width)
        h = dot(x, up_now) + b_ref[0:1, :]
        cdf = 0.5 * (1.0 + lax.erf(h * RSQRT2))
        act = (h * cdf).astype(bf16)
        slope = cdf + h * (RSQRT2PI * jnp.exp(-0.5 * h * h))
        ff = dot(act, down_now)
        grad = dot(cot, down_now, NT) * slope
        sum_ref[7:8, :] += jnp.sum(grad, axis=0, keepdims=True)
        low = grad.astype(bf16)
        ng = dot(low, up_now, NT)
        up_acc[...] += dot(x, low, TN)
        down_acc[...] += dot(act, cot, TN)
        if last:
            ff = ff + ff_in[...]
            ng = ng + ng_in[...]

            @pl.when(i < count)
            def _():
                ffo_ref[...] = ff
                ngo_ref[...] = ng

            @pl.when(i >= count)
            def _():
                fft_ref[...] = ff.astype(bf16)
                ngt_ref[...] = ng.astype(bf16)
        else:
            ff_ref[...] = ff
            ng_ref[...] = ng

        @pl.when(i == 2 * count - 1)
        def _():
            units = scal_ref[1]

            @pl.when(scal_ref[2] < 0.5)
            def _():
                keep[...] = (up_acc[...] * units).astype(bf16)
                send[...] = (down_acc[...] * units).astype(bf16)

            @pl.when(scal_ref[2] > 0.5)
            def _():
                keep[...] = (down_acc[...] * units).astype(bf16)
                send[...] = (up_acc[...] * units).astype(bf16)

            sum_ref[...] = sum_ref[...] * units

    own, other = halves(block, width, count)
    every = pl.BlockSpec((block, width), lambda i: (i, 0))
    up_spec, down_spec = (
        pl.BlockSpec(
            (slices, None, depth, width), lambda i, j=j: (0, j, 0, 0), pipeline_mode=pl.Buffered(1)
        )
        for j in (up_place, down_place)
    )
    ins = [scalars(), own, other, own, other, whole(bias), up_spec, down_spec]
    args = [scal, norm_own, norm_other, cot_own, cot_other, bias, up, down]
    if last:
        ins += [every, every]
        args += list(earlier)
        outs = [own, own, other, other]
        shapes = [shape((rows, width), f32)] * 2 + [shape((rows, width), bf16)] * 2
    else:
        outs = [every, every]
        shapes = [shape((2 * rows, width), f32)] * 2
    assert width == hidden
    terms = [shape((width, hidden), bf16)] * 2
    sums = shape((8, hidden), f32)
    return call(
        kernel,
        "feed_forward",
        (2 * count,),
        ins,
        outs + [whole(terms[0]), whole(terms[1]), whole(sums)],
        shapes + terms + [sums],
        [pltpu.VMEM((width, hidden), f32), pltpu.VMEM((hidden, width), f32)],
        flops=24 * rows * width * hidden,
        nbytes=24 * rows * width + 12 * width * hidden,
        exps=4 * rows * hidden,
        weight=1000 if last else 1e-6,
    )(*args)


def second_back(middle, grad_own, grad_received, cot, params, scal):
    rows, width = middle.shape
    block = 256
    last = rows // block - 1

    def kernel(scal_ref, mid_ref, go_ref, gr_ref, cot_ref, par_ref, out_ref, low_ref, sum_ref):
        i = pl.program_id(0)
        unit, inverse = normalize(mid_ref[...])
        grad = go_ref[...] + gr_ref[...].astype(f32)
        cot = cot_ref[...].astype(f32) * scal_ref[0]
        out = cot + norm_back(grad, par_ref[3:4, :], unit, inverse)
        out_ref[...] = out
        low_ref[...] = out.astype(bf16)
        sums = [jnp.sum(v, axis=0, keepdims=True) for v in (grad * unit, grad, out, cot)]
        add_rows(sum_ref, sums, i == 0, 2)

        @pl.when(i == last)
        def _():
            sum_ref[...] = sum_ref[...] * scal_ref[1]

    spec = pl.BlockSpec((block, width), lambda i: (i, 0))
    sums = shape((8, width), f32)
    return call(
        kernel,
        "second_back",
        (rows // block,),
        [scalars(), spec, spec, spec, spec, whole(params)],
        [spec, spec, whole(sums)],
        [shape((rows, width), f32), shape((rows, width), bf16), sums],
        flops=30 * rows * width,
        nbytes=18 * rows * width,
    )(scal, middle, grad_own, grad_received, cot, params)


def output_back(low, attended, weights, scal, earlier=None):
    rows, width = low.shape
    cols = weights[0].shape[0]
    block = 512
    last = earlier is not None

    def kernel(scal_ref, low_ref, a_ref, b_ref, wa_ref, wb_ref, *refs):
        before = refs[:2] if last else (None, None)
        ga_ref, gb_ref, ta_ref, tb_ref, acc_a, acc_b = refs[2 if last else 0 :]
        i = pl.program_id(0)
        now = low_ref[...]
        ga_ref[...] = dot(now, wa_ref[...], NT).astype(bf16)
        gb_ref[...] = dot(now, wb_ref[...], NT).astype(bf16)
        for acc, rows_ref, old in ((acc_a, a_ref, before[0]), (acc_b, b_ref, before[1])):

            @pl.when(i == 0)
            def _():
                acc[...] = jnp.zeros_like(acc) if old is None else old[...]

            acc[...] += dot(rows_ref[...], now, TN)

        @pl.when(i == rows // block - 1)
        def _():
            factor = scal_ref[1] if last else 1.0
            ta_ref[...] = (acc_a[...] * factor).astype(ta_ref.dtype)
            tb_ref[...] = (acc_b[...] * factor).astype(tb_ref.dtype)

    thin = pl.BlockSpec((block, cols), lambda i: (i, 0))
    terms = [shape((cols, width), bf16 if last else f32)] * 2
    before = list(earlier or ())
    return call(
        kernel,
        "output_back",
        (rows // block,),
        [scalars(), pl.BlockSpec((block, width), lambda i: (i, 0)), thin, thin]
        + [whole(w) for w in weights]
        + [whole(t) for t in before],
        [thin, thin, whole(terms[0]), whole(terms[1])],
        [shape((rows, cols), bf16)] * 2 + terms,
        [pltpu.VMEM((cols, width), f32)] * 2,
        flops=8 * rows * width * cols,
        nbytes=2 * rows * width + 8 * rows * cols,
        weight=1e-6 if last else 1000,
    )(scal, low, *attended, *weights, *before)


def side_by_side(refs):
    return jnp.concatenate([ref[p] for ref in refs for p in range(ref.shape[0])], 1)


def pair_specs(grads, block, place):
    return [
        pl.BlockSpec((g.shape[0], block, g.shape[2]), lambda i: (0, place(i), 0)) for g in grads
    ]


def input_term(norm_own, norm_other, grads, scal, other=None, outputs=(), place=None):
    rows, width = norm_own.shape
    pairs = sum(g.shape[0] for g in grads)
    cols = pairs * LANES
    many = len(grads)
    more = [] if other is None else [other, *outputs]
    quarter = width

    def kernel(scal_ref, *refs):
        place_ref = refs[0] if more else None
        no_ref, nt_ref, *refs = refs[1 if more else 0 :]
        outs, acc = refs[many + len(more) : -1], refs[-1]
        i = pl.program_id(0)
        term = dot(pick(1, no_ref, nt_ref), side_by_side(refs[:many]), TN)

        @pl.when(i == 0)
        def _():
            acc[...] = term

        def total(j, p):
            at = (3 * p + j) * LANES
            return (acc[:, at : at + LANES] + term[:, at : at + LANES]) * scal_ref[1]

        def store(half, keep, send):
            for p in range(pairs):
                lanes = slice(p * LANES, (p + 1) * LANES)
                for out_ref, j in ((keep, 2 * half), (send, 2 * half + 1)):
                    if j < 3:
                        final = total(j, p) + refs[many][j * width : (j + 1) * width, lanes].astype(f32)
                        out_ref[:, lanes] = final.astype(bf16)
                        continue
                    for k in range(width // cols):
                        at = slice(k * cols + p * LANES, k * cols + (p + 1) * LANES)
                        final = refs[many + 1][:, at].astype(f32) + refs[many + 2][:, at].astype(f32)
                        out_ref[k * cols : (k + 1) * cols, lanes] = final.astype(bf16)

        @pl.when(i == 1)
        def _():
            if not more:
                for p in range(pairs):
                    for j in range(3):
                        at = (slice(j * width, (j + 1) * width), slice(p * LANES, (p + 1) * LANES))
                        outs[0][at] = total(j, p).astype(bf16)
            for half in range(2 if more else 0):
                keep, send = outs[2 * half], outs[2 * half + 1]

                @pl.when(place_ref[half] == 0)
                def _():
                    store(half, keep, send)

                @pl.when(place_ref[half] == 1)
                def _():
                    store(half, send, keep)

    out = [shape((quarter, cols), bf16)] * 4 if more else [shape((3 * width, cols), bf16)]
    return call(
        kernel,
        "input_term",
        (2,),
        [scalars()]
        + [scalars()] * (1 if more else 0)
        + [*halves(rows, width, 1)]
        + pair_specs(grads, rows, lambda i: i)
        + [whole(m) for m in more],
        [whole(o) for o in out],
        out,
        [pltpu.VMEM((width, 3 * cols), f32)],
        flops=12 * rows * width * cols,
        nbytes=4 * rows * width + 12 * rows * cols + 12 * width * cols,
    )(scal, *([place] if more else []), norm_own, norm_other, *grads, *more)


def join_weights(refs, joined):
    @pl.when(pl.program_id(0) == 0)
    def _():
        place = 0
        for ref in refs:
            for p in range(ref.shape[2] // LANES):
                for j in range(3):
                    joined[:, place : place + LANES] = ref[j, :, p * LANES : (p + 1) * LANES]
                    place += LANES


def norm1_other(grads, weights):
    rows = grads[0].shape[1] // 2
    width, cols = weights[0].shape[1:]
    block = 512
    count = rows // block
    many = len(grads)

    def kernel(*refs):
        out_ref, joined = refs[-2:]
        join_weights(refs[many:-2], joined)
        out_ref[...] = dot(side_by_side(refs[:many]), joined[...], NT).astype(bf16)

    return call(
        kernel,
        "first_other",
        (count,),
        pair_specs(grads, block, lambda i: i + count) + [whole(w) for w in weights],
        pl.BlockSpec((block, width), lambda i: (i, 0)),
        shape((rows, width), bf16),
        [pltpu.VMEM((width, 3 * cols * len(weights)), bf16)],
        flops=12 * rows * width * cols,
        nbytes=12 * rows * cols + 2 * rows * width + 12 * width * cols,
    )(*grads, *weights)


def norm1_own(grads, weights, received, tokens, middle_grad, params, scal):
    rows, width = tokens.shape
    cols = weights[0].shape[2]
    block = 256
    last = rows // block - 1
    many = len(grads)

    def kernel(scal_ref, *refs):
        rec_ref, tok_ref, mid_ref, par_ref, out_ref, sum_ref, joined = refs[many + len(weights) :]
        i = pl.program_id(0)
        join_weights(refs[many : many + len(weights)], joined)
        grad = dot(side_by_side(refs[:many]), joined[...], NT) + rec_ref[...].astype(f32)
        unit, inverse = normalize(tok_ref[...].astype(f32))
        out = mid_ref[...] + norm_back(grad, par_ref[0:1, :], unit, inverse)
        out_ref[...] = out.astype(bf16)
        sums = [jnp.sum(v, axis=0, keepdims=True) for v in (grad * unit, grad)]
        add_rows(sum_ref, sums, i == 0, 0)

        @pl.when(i == last)
        def _():
            sum_ref[...] = sum_ref[...] * scal_ref[1]

    spec = pl.BlockSpec((block, width), lambda i: (i, 0))
    sums = shape((8, width), f32)
    return call(
        kernel,
        "first_own",
        (rows // block,),
        [scalars()]
        + pair_specs(grads, block, lambda i: i)
        + [whole(w) for w in weights]
        + [spec] * 3
        + [whole(params)],
        [spec, whole(sums)],
        [shape((rows, width), bf16), sums],
        [pltpu.VMEM((width, 3 * cols * len(weights)), bf16)],
        flops=12 * rows * width * cols,
        nbytes=12 * rows * cols + 10 * rows * width + 12 * width * cols,
    )(scal, *grads, *weights, received, tokens, middle_grad, params)


def block_result(middle, own, received, params, scal):
    rows, width = middle.shape
    block = 256

    def kernel(scal_ref, mid_ref, own_ref, rec_ref, par_ref, out_ref):
        total = mid_ref[...] + own_ref[...] + rec_ref[...].astype(f32) + par_ref[5:6, :]
        out_ref[...] = (total * scal_ref[0]).astype(bf16)

    spec = pl.BlockSpec((block, width), lambda i: (i, 0))
    return call(
        kernel,
        "block_result",
        (rows // block,),
        [scalars(), spec, spec, spec, whole(params)],
        spec,
        shape((rows, width), bf16),
        flops=4 * rows * width,
        nbytes=12 * rows * width,
        weight=1000,
    )(scal, middle, own, received, params)


def add_terms(*terms):
    rows, width = terms[0].shape
    block = 256

    def kernel(*refs):
        total = refs[0][...].astype(f32)
        for ref in refs[1:-1]:
            total = total + ref[...].astype(f32)
        refs[-1][...] = total.astype(bf16)

    spec = pl.BlockSpec((block, width), lambda i: (i, 0))
    return call(
        kernel,
        "add_terms",
        (rows // block,),
        [spec] * len(terms),
        spec,
        shape((rows, width), bf16),
        flops=len(terms) * rows * width,
        nbytes=2 * (len(terms) + 1) * rows * width,
    )(*terms)


def body(
    tokens,
    out_grad,
    item_counts,
    group_dataset,
    variable_mask,
    first_gain,
    first_shift,
    input_weight,
    input_bias,
    output_weight,
    output_bias,
    second_gain,
    second_shift,
    up_weight,
    up_bias,
    down_weight,
    down_bias,
):
    shard_count = lax.axis_size("mp")
    groups = lax.axis_size("dp")
    rows, width = tokens.shape
    cols = input_weight.shape[2]
    hidden = up_weight.shape[1]

    def core_swap(value):
        return lax.ppermute(value, "mp", [(i, i ^ 1) for i in range(shard_count)])

    def chip_swap(value):
        return lax.ppermute(value, "mp", [(i, i ^ 2) for i in range(shard_count)])

    def after(value, *others):
        return lax.optimization_barrier((value, *others))[0]

    def along(value, bit):
        return lax.ppermute(value, "dp", [(i, i ^ bit) for i in range(groups)])

    group = lax.axis_index("dp")

    slice_rows = up_weight.shape[0] // groups
    slices = [
        lax.dynamic_slice_in_dim(weight, group * slice_rows, slice_rows, 0)
        for weight in (up_weight, down_weight)
    ]
    slice_two = chip_swap(jnp.stack(slices)[None])
    bias_pack = jnp.concatenate([up_bias, input_bias[0], input_bias[1]]).reshape(-1, LANES)
    bias_two = chip_swap(bias_pack)
    wi_two = chip_swap(after(input_weight, *slices))
    cot_t = core_swap(out_grad)
    normed1 = first_norm(tokens, first_gain, first_shift)
    normed1_t = core_swap(normed1)
    item_counts, variable_mask, output_bias = after(
        (item_counts, variable_mask, output_bias), normed1
    )

    live = (lax.axis_index("mp") // 2 < item_counts[0]).astype(f32)
    dataset_hit = jnp.arange(variable_mask.shape[0], dtype=jnp.int32) == group_dataset[0]
    own_units = (
        item_counts[0] * jnp.sum(jnp.where(dataset_hit[:, None], variable_mask, 0))
    ).astype(f32)
    scal = jnp.stack([live, own_units, (group % 2).astype(f32)])
    zero = jnp.zeros((width,), f32)
    params = jnp.stack(
        [first_gain, first_shift, output_bias, second_gain, second_shift, down_bias, zero, zero]
    )

    qkv_one = project(normed1, input_weight, input_bias)
    wo_two = chip_swap(after(output_weight, qkv_one[0]))
    ff_weights_two = lax.all_gather(after(slice_two, qkv_one[0]), "dp", axis=0, tiled=True)
    qkv_one = project(normed1_t, input_weight, after(input_bias, qkv_one[0]), qkv_one)
    att_one, att_one_send, turned_one, stat_one = attend_forward(*qkv_one)
    att_one_t = core_swap(att_one_send)
    wo_one_t = core_swap(output_weight)
    bias_two = after(bias_two, att_one).reshape(-1)
    up_bias_one = up_bias.reshape(1, hidden)
    up_bias_two = bias_two[:hidden].reshape(1, hidden)
    in_bias_two = bias_two[hidden:].reshape(2, cols)
    qkv_two = project(after(normed1, att_one), wi_two, in_bias_two)
    qkv_two = project(normed1_t, wi_two, after(in_bias_two, att_one_t), qkv_two)
    att_two, att_two_send, turned_two, stat_two = attend_forward(*qkv_two)
    wo_two_t = core_swap(after(wo_two, qkv_two[0]))
    att_two_t = core_swap(att_two_send)
    middle, normed2 = output_own(
        tokens,
        [att_one, att_two, att_one_t, after(att_two_t, ff_weights_two)],
        [output_weight, wo_two, wo_one_t, wo_two_t],
        params,
    )
    normed2_t = core_swap(normed2)

    ff_two, ng_two, keep_two, send_two, up_sum_two = feed_forward(
        normed2, normed2_t, out_grad, cot_t, up_bias_two, (ff_weights_two, 0), (ff_weights_two, 1), scal
    )
    two_received = along(send_two, 1)
    up_one, down_one = ((w.reshape(1, 1, -1, width), 0) for w in (up_weight, down_weight))
    ff_own, ng_own, ff_send, ng_send, keep_one, send_one, up_sum_one = feed_forward(
        normed2, normed2_t, out_grad, cot_t, up_bias_one, up_one, down_one, scal, (ff_two, ng_two)
    )
    one_received = along(send_one, 1)
    ng_received = core_swap(ng_send)
    pair_two = add_terms(keep_two, two_received)
    pair_received = chip_swap(pair_two)
    middle_grad, middle_low, second_sums = second_back(
        middle, ng_own, ng_received, after(out_grad, pair_two), params, scal
    )
    middle_low_t = core_swap(middle_low)
    out_weights = [output_weight, wo_two]
    g_one, g_two, *wo_terms = output_back(
        middle_low, [att_one, att_two], out_weights, scal
    )
    g_one_t, g_two_t, wo_one_term, wo_two_term = output_back(
        middle_low_t, [att_one_send, att_two_send], out_weights, scal, wo_terms
    )

    def both(own, received, *last):
        return (own.astype(f32) + after(received, *last).astype(f32)).astype(bf16)

    back_two = [attend_backward(*qkv_two, g_two, g_two_t, turned_two, stat_two, 0, 1)]
    wait = back_two[0][0]
    ff_both = add_terms(keep_one, one_received, after(pair_received, wait))
    ff_sum = lax.psum(
        ff_both, "dp", axis_index_groups=[list(range(k, groups, 2)) for k in range(2)]
    )
    back_two.append(
        attend_backward(
            *qkv_two, after(g_two, ff_both), g_two_t, turned_two, stat_two, 1, cols // LANES - 1
        )
    )
    grads_two = [back[0] for back in back_two]
    wi_two_term = input_term(normed1, normed1_t, grads_two, scal)[0]
    ff_received = core_swap(after(ff_send, wait))
    wo_received = chip_swap(after(wo_two_term, grads_two[1]))
    wi_received = chip_swap(wi_two_term)
    g_one = after(g_one, wi_two_term)
    back_one = [attend_backward(*qkv_one, g_one, g_one_t, turned_one, stat_one, 0, cols // LANES)]
    grads_one = [back[0] for back in back_one]

    bits = [1 << k for k in range(groups.bit_length() - 1)]
    orders = [bits, bits[1:] + bits[:1]]

    def upper(bit):
        return (group // bit) % 2

    def split(part, bit):
        half = part.shape[0] // 2
        return (
            lax.dynamic_slice_in_dim(part, upper(bit) * half, half, 0),
            lax.dynamic_slice_in_dim(part, (1 - upper(bit)) * half, half, 0),
        )

    place = jnp.stack([upper(order[0]) for order in orders]).astype(jnp.int32)
    keep_a, send_a, keep_b, send_b = input_term(
        normed1, normed1_t, grads_one, scal, wi_received, (wo_one_term, wo_received), place
    )
    keeps, sends = (keep_a, keep_b), (send_a, send_b)
    received = [along(sends[k], orders[k][0]) for k in range(2)]

    grads = grads_one + grads_two
    weights = [input_weight, wi_two]
    ng1_send = norm1_other(grads, [input_weight, after(wi_two, *sends)])
    ng1_received = core_swap(ng1_send)
    result = block_result(middle, after(ff_own, ng1_send, ff_sum), ff_received, params, scal)
    token_grad, first_sums = norm1_own(
        grads, weights, ng1_received, after(tokens, result), middle_grad, params, scal
    )

    ff_sum_other = along(ff_sum, 1)
    parts = [both(keeps[k], received[k]) for k in range(2)]
    for turn in range(1, len(bits)):
        if turn == len(bits) - 1:
            parts = [after(part, token_grad) for part in parts]
        for k in range(2):
            bit = orders[k][turn]
            keep, send = split(parts[k], bit)
            parts[k] = both(keep, along(send, bit))
    for turn in reversed(range(len(bits))):
        if turn == 0:
            parts = [after(part, ff_sum_other) for part in parts]
        for k in range(2):
            bit = orders[k][turn]
            received = along(parts[k], bit)
            is_upper = upper(bit) == 1
            parts[k] = jnp.concatenate(
                [jnp.where(is_upper, received, parts[k]), jnp.where(is_upper, parts[k], received)]
            )
    wi_rows = 3 * width
    tail_sum = jnp.concatenate(parts)
    wi_sum = tail_sum[:wi_rows].reshape(3, width, cols)
    wo_sum = tail_sum[wi_rows:].reshape(width // cols, cols, cols)
    wo_sum = jnp.concatenate([wo_sum[k] for k in range(width // cols)], 1)

    lower = group % 2 == 0
    up_sum = jnp.where(lower, ff_sum, ff_sum_other)
    down_sum = jnp.where(lower, ff_sum_other, ff_sum)

    def quarter_rows(parts, up_sums):
        sums_all = jnp.concatenate([part[1] for part in parts], 1)
        rest = jnp.full((1, width - 2 * cols), own_units)
        bias_row = jnp.concatenate([sums_all[0:1] * own_units, sums_all[1:2] * own_units, rest], 1)
        return up_sums + jnp.pad(bias_row, ((6, 1), (0, 0)))

    late = first_sums + second_sums
    late = late + core_swap(late)
    late_one = late + quarter_rows(back_one, up_sum_one)
    late = late_one + chip_swap(late + quarter_rows(back_two, up_sum_two))
    for bit in orders[1]:
        late = late + along(late, bit)
    share = 2.0 / late[6, -1]
    late = late * share

    return (
        result,
        token_grad,
        late[0],
        late[1],
        wi_sum.astype(f32) * share,
        late[6, : 2 * cols].reshape(2, cols),
        wo_sum.astype(f32) * share,
        late[4],
        late[2],
        late[3],
        up_sum.astype(f32) * share,
        late[7],
        down_sum.astype(f32) * share,
        late[5],
    )


def solution(mesh):
    in_specs = (
        P(("dp", "mp"), None),
        P(("dp", "mp"), None),
        P("dp"),
        P("dp"),
        P(),
        P(),
        P(),
        P(None, None, "mp"),
        P(None, "mp"),
        P("mp", None),
        P(),
        P(),
        P(),
        P(None, "mp"),
        P("mp"),
        P("mp", None),
        P(),
    )
    out_specs = (
        P(("dp", "mp"), None),
        P(("dp", "mp"), None),
        P(),
        P(),
        P(None, None, "mp"),
        P(None, "mp"),
        P("mp", None),
        P(),
        P(),
        P(),
        P(None, "mp"),
        P("mp"),
        P("mp", None),
        P(),
    )
    return jax.shard_map(body, mesh=mesh, in_specs=in_specs, out_specs=out_specs, check_vma=False)
```

```python
import jax
import jax.numpy as jnp
from jax import lax
from jax.experimental import pallas as pl
from jax.experimental.pallas import tpu as pltpu
from jax.sharding import PartitionSpec as P

HEAD_DIM = 64
LANES = 128
norm_eps = 1e-06
SCALE = HEAD_DIM**-0.5
LOG2E = 1.4426950408889634
RSQRT2 = 0.7071067811865476
RSQRT2PI = 0.3989422804014327

bf16 = jnp.bfloat16
f32 = jnp.float32
NN = (((1,), (0,)), ((), ()))
NT = (((1,), (1,)), ((), ()))
TN = (((0,), (0,)), ((), ()))
VMEM_BYTES = 60 << 20


def dot(left, right, dims=NN):
    return lax.dot_general(left, right, dims, preferred_element_type=f32)


def shape(dims, dtype):
    return jax.ShapeDtypeStruct(dims, dtype)


def whole(array):
    rank = len(array.shape)
    return pl.BlockSpec(array.shape, lambda *_: (0,) * rank, pipeline_mode=pl.Buffered(1))


def scalars():
    return pl.BlockSpec(memory_space=pltpu.SMEM)


def call(kernel, name, grid, in_specs, out_specs, out_shape, scratch=(), flops=0, nbytes=0, exps=0, weight=1e-6, aliases=None):
    return pl.pallas_call(
        kernel,
        name=name,
        grid=grid,
        in_specs=in_specs,
        out_specs=out_specs,
        out_shape=out_shape,
        scratch_shapes=list(scratch),
        input_output_aliases=aliases or {},
        compiler_params=pltpu.CompilerParams(vmem_limit_bytes=VMEM_BYTES),
        cost_estimate=pl.CostEstimate(
            flops=int(flops * weight), bytes_accessed=int(nbytes * weight), transcendentals=int(exps * weight)
        ),
    )


def split_two(values):
    high = values.astype(bf16)
    return high, (values - high.astype(f32)).astype(bf16)


def split_three(values):
    high = values.astype(bf16)
    rest = values - high.astype(f32)
    mid = rest.astype(bf16)
    return high, mid, (rest - mid.astype(f32)).astype(bf16)


def stat_rows(vector, rows):
    high, mid, rest = (part.astype(f32) for part in split_three(vector))
    row = lax.broadcasted_iota(jnp.int32, (rows, vector.shape[1]), 0)
    return jnp.where(
        row == 0, high, jnp.where(row == 1, mid, jnp.where(row == 2, rest, 0.0))
    ).astype(bf16)


def normalize(values):
    centered = values - jnp.mean(values, axis=-1, keepdims=True)
    variance = jnp.mean(centered * centered, axis=-1, keepdims=True)
    inverse = lax.rsqrt(variance + norm_eps)
    return centered * inverse, inverse


def norm_back(grad, gain, unit, inverse):
    scaled = grad * gain
    return inverse * (
        scaled
        - jnp.mean(scaled, axis=-1, keepdims=True)
        - unit * jnp.mean(scaled * unit, axis=-1, keepdims=True)
    )


def add_rows(ref, rows, first, start):
    @pl.when(first)
    def _():
        ref[...] = jnp.zeros_like(ref)

    for place, row in enumerate(rows):
        ref[start + place : start + place + 1, :] += row


def first_norm(tokens, gain, shift):
    rows, width = tokens.shape
    block = 256

    def kernel(tok_ref, gain_ref, shift_ref, norm_ref):
        unit, _ = normalize(tok_ref[...].astype(f32))
        gain_row = gain_ref[...].reshape(1, width)
        norm_ref[...] = (unit * gain_row + shift_ref[...].reshape(1, width)).astype(bf16)

    spec = pl.BlockSpec((block, width), lambda i: (i, 0))
    return call(
        kernel,
        "first_norm",
        (rows // block,),
        [spec, whole(gain), whole(shift)],
        spec,
        shape((rows, width), bf16),
        flops=20 * rows * width,
        nbytes=4 * rows * width,
    )(tokens, gain, shift)


def halves(block, width, count):
    own = pl.BlockSpec((block, width), lambda i, *_: (jnp.minimum(i, count - 1), 0))
    other = pl.BlockSpec((block, width), lambda i, *_: (jnp.maximum(i - count, 0), 0))
    return own, other


def pick(count, own_ref, other_ref):
    return jnp.where(pl.program_id(0) < count, own_ref[...], other_ref[...])


def project(norm, weight, bias, earlier=None):
    rows, width = norm.shape
    cols = weight.shape[2]
    block = 512
    start = 0 if earlier is None else rows // block
    skip = 0 if earlier is None else 3

    def kernel(x_ref, w_ref, b_ref, *refs):
        q_ref, k_ref, v_ref = refs[skip:]
        x = x_ref[...]
        q_ref[...] = (dot(x, w_ref[0]) + b_ref[0:1, :]).astype(bf16)
        k_ref[...] = dot(x, w_ref[1]).astype(bf16)
        v_ref[...] = (dot(x, w_ref[2]) + b_ref[1:2, :]).astype(bf16)

    out = pl.BlockSpec((block, cols), lambda i: (i + start, 0))
    return call(
        kernel,
        "project",
        (rows // block,),
        [pl.BlockSpec((block, width), lambda i: (i, 0)), whole(weight), whole(bias)]
        + [pl.BlockSpec(memory_space=pl.ANY)] * skip,
        [out] * 3,
        [shape((2 * rows, cols), bf16)] * 3,
        flops=6 * rows * width * cols,
        nbytes=2 * rows * width + 6 * width * cols + 6 * rows * cols,
        weight=1000,
        aliases={3 + k: k for k in range(skip)},
    )(norm, weight, bias, *(earlier or ()))


def attend_forward(queries, keys, values):
    rows, width = queries.shape
    chunk = min(512, rows)

    def kernel(q_ref, k_ref, v_ref, own_ref, other_ref, ot_ref, lse_ref):
        k = k_ref[...]
        lane = lax.broadcasted_iota(jnp.int32, k.shape, 1)
        rolled = pltpu.roll(k.astype(f32), HEAD_DIM, 1).astype(bf16)
        turned = v_ref[...].astype(f32).T
        ones = jnp.ones((HEAD_DIM, rows), bf16)
        q_turned = q_ref[...].astype(f32).T * (SCALE * LOG2E)
        outs = []
        for head in range(2):
            at = head * HEAD_DIM
            k_two = jnp.where(lane < HEAD_DIM, k, rolled) if head == 0 else jnp.where(lane < HEAD_DIM, rolled, k)
            own = turned[at : at + HEAD_DIM].astype(bf16)
            v_turned = jnp.concatenate([own, ones] if head == 0 else [ones, own], 0)
            q_two = jnp.concatenate(split_two(q_turned[at : at + HEAD_DIM]), 0)
            total = peak = None
            for j in range(rows // chunk):
                part = slice(j * chunk, (j + 1) * chunk)
                scores = dot(k_two[part], q_two)
                top = jnp.max(scores.reshape(chunk // 8, 8, rows).max(axis=0), axis=0, keepdims=True)
                higher = top if peak is None else jnp.maximum(peak, top)
                weights = jnp.exp2(scores - higher).astype(bf16)
                add = dot(v_turned[:, part], weights)
                total = add if total is None else total * jnp.exp2(peak - higher) + add
                peak = higher
            row_sum = total[HEAD_DIM - at : HEAD_DIM - at + 1]
            outs.append(total[at : at + HEAD_DIM] / row_sum)
            lse_ref[head : head + 1, :] = peak + jnp.log2(row_sum)
        attended = jnp.concatenate(outs, 0)
        ot_ref[...] = attended
        own_ref[...] = attended[:, : rows // 2].T.astype(bf16)
        other_ref[...] = attended[:, rows // 2 :].T.astype(bf16)

    by_pair = pl.BlockSpec((rows, LANES), lambda j: (0, j))
    by_half = pl.BlockSpec((rows // 2, LANES), lambda j: (0, j))
    pairs = width // LANES
    return call(
        kernel,
        "attend_forward",
        (pairs,),
        [by_pair] * 3,
        [
            by_half,
            by_half,
            pl.BlockSpec((LANES, rows), lambda j: (j, 0)),
            pl.BlockSpec((None, 8, rows), lambda j: (j, 0, 0)),
        ],
        [shape((rows // 2, width), bf16)] * 2
        + [shape((width, rows), f32), shape((pairs, 8, rows), f32)],
        flops=16 * rows * rows * width,
        nbytes=12 * rows * width,
        exps=rows * rows * width // HEAD_DIM,
        weight=1000,
    )(queries, keys, values)


def attend_backward(queries, keys, values, grad_own, grad_other, out_turned, stats, first, pairs):
    rows = queries.shape[0]
    width = LANES * pairs
    block = grad_own.shape[0]
    chunk = 256
    count = rows // block

    def kernel(
        q_ref, k_ref, v_ref, go_ref, gt_ref, ot_ref, lse_ref, d_ref, sum_ref,
        k_wide, k_turned, v_wide, dk_acc, dv_acc,
    ):
        i = pl.program_id(1)

        @pl.when(i == 0)
        def _():
            k = k_ref[...]
            v = v_ref[...]
            lane = lax.broadcasted_iota(jnp.int32, k.shape, 1)
            k_rolled = pltpu.roll(k.astype(f32), HEAD_DIM, 1).astype(bf16)
            v_rolled = pltpu.roll(v.astype(f32), HEAD_DIM, 1).astype(bf16)
            ones = jnp.where(lane < 3, 1.0, 0.0).astype(bf16)
            k_wide[0] = jnp.concatenate([jnp.where(lane < HEAD_DIM, k, k_rolled), ones], 1)
            k_wide[1] = jnp.concatenate([jnp.where(lane < HEAD_DIM, k_rolled, k), ones], 1)
            tail = jnp.where(lane < HEAD_DIM + 3, 1.0, 0.0).astype(bf16)
            v_wide[0] = jnp.where(lane < HEAD_DIM, v, tail)
            v_wide[1] = jnp.where(lane < HEAD_DIM, v_rolled, tail)
            k_turned[...] = k.astype(f32).T.astype(bf16)
            dk_acc[...] = jnp.zeros_like(dk_acc)
            dv_acc[...] = jnp.zeros_like(dv_acc)
            sum_ref[...] = jnp.zeros_like(sum_ref)

        q_turned = q_ref[...].astype(f32).T
        q_low = q_turned.astype(bf16)
        q_turned = q_turned * (SCALE * LOG2E)
        g_turned = jnp.where(i == 0, go_ref[...], gt_ref[...]).astype(f32).T
        g_low = g_turned.astype(bf16)
        dqs = []
        for head in range(2):
            part = slice(head * HEAD_DIM, (head + 1) * HEAD_DIM)
            q_wide = jnp.concatenate(
                [*split_two(q_turned[part]), stat_rows(-lse_ref[head : head + 1, :], LANES)], 0
            )
            row_dot = jnp.sum(g_turned[part] * ot_ref[part, :], axis=0, keepdims=True)
            g_wide = jnp.concatenate([g_low[part], stat_rows(-row_dot, HEAD_DIM)], 0)
            dq = None
            for j in range(rows // chunk):
                at = pl.ds(j * chunk, chunk)
                probabilities = jnp.exp2(dot(k_wide[head, at, :], q_wide))
                shifted = dot(v_wide[head, at, :], g_wide)
                probs_low = probabilities.astype(bf16)
                score_grad = (probabilities * shifted).astype(bf16)
                dv_acc[part, at] += dot(g_low[part], probs_low, NT)
                dk_acc[part, at] += dot(q_low[part], score_grad, NT)
                add = dot(k_turned[part, at], score_grad)
                dq = add if dq is None else dq + add
            dqs.append(dq)
        dq = (jnp.concatenate(dqs, 0) * SCALE).T
        d_ref[pl.ds(i * block, block), :LANES] = dq.astype(bf16)
        sum_ref[0:1, :] += jnp.sum(dq, axis=0, keepdims=True)

        @pl.when(i == count - 1)
        def _():
            d_ref[:, LANES : 2 * LANES] = (dk_acc[...] * SCALE).T.astype(bf16)
            dv = dv_acc[...].T
            d_ref[:, 2 * LANES :] = dv.astype(bf16)
            sum_ref[1:2, :] = jnp.sum(dv, axis=0, keepdims=True)

    by_query = pl.BlockSpec((block, LANES), lambda j, i: (i, j + first))
    by_key = pl.BlockSpec((rows, LANES), lambda j, i: (0, j + first))
    half = pl.BlockSpec((block, LANES), lambda j, i: (0, j + first))
    turned_spec = pl.BlockSpec((LANES, block), lambda j, i: (j + first, i))
    stat_spec = pl.BlockSpec((None, 8, block), lambda j, i: (j + first, 0, i))
    out_spec = pl.BlockSpec((None, rows, 3 * LANES), lambda j, i: (j, 0, 0))
    sum_spec = pl.BlockSpec((8, LANES), lambda j, i: (0, j))
    return call(
        kernel,
        "attend_backward",
        (pairs, count),
        [by_query, by_key, by_key, half, half, turned_spec, stat_spec],
        [out_spec, sum_spec],
        [shape((pairs, rows, 3 * LANES), bf16), shape((8, width), f32)],
        [
            pltpu.VMEM((2, rows, 2 * LANES), bf16),
            pltpu.VMEM((LANES, rows), bf16),
            pltpu.VMEM((2, rows, LANES), bf16),
            pltpu.VMEM((LANES, rows), f32),
            pltpu.VMEM((LANES, rows), f32),
        ],
        flops=40 * rows * rows * width,
        nbytes=20 * rows * width,
        exps=rows * rows * width // HEAD_DIM,
        weight=1000,
    )(queries, keys, values, grad_own, grad_other, out_turned, stats)


def output_own(tokens, attended, weights, params):
    rows, width = tokens.shape
    cols = weights[0].shape[0]
    block = 256
    many = len(attended)

    def kernel(t_ref, par_ref, *refs):
        total = None
        for a_ref, w_ref in zip(refs[:many], refs[many : 2 * many], strict=True):
            part = dot(a_ref[...], w_ref[...])
            total = part if total is None else total + part
        mid_ref, norm_ref = refs[2 * many :]
        middle = t_ref[...].astype(f32) + total + par_ref[2:3, :]
        mid_ref[...] = middle
        unit, _ = normalize(middle)
        norm_ref[...] = (unit * par_ref[3:4, :] + par_ref[4:5, :]).astype(bf16)

    spec = pl.BlockSpec((block, width), lambda i: (i, 0))
    thin = pl.BlockSpec((block, cols), lambda i: (i, 0))
    return call(
        kernel,
        "output_own",
        (rows // block,),
        [spec, whole(params)] + [thin] * many + [whole(w) for w in weights],
        [spec, spec],
        [shape((rows, width), f32), shape((rows, width), bf16)],
        flops=2 * rows * many * cols * width,
        nbytes=2 * rows * many * cols + 8 * rows * width,
    )(tokens, params, *attended, *weights)


def feed_forward(norm_own, norm_other, cot_own, cot_other, bias, up, down, scal, earlier=None):
    rows, width = norm_own.shape
    hidden = bias.shape[1]
    block = 512
    count = rows // block
    last = earlier is not None
    (up, up_place), (down, down_place) = up, down
    slices, depth = up.shape[0], up.shape[2]
    def kernel(scal_ref, no_ref, nt_ref, co_ref, ct_ref, b_ref, up_ref, dn_ref, *refs):
        if last:
            ng_in, act_ref, ngo_ref, nga_ref, ngb_ref, *refs = refs
        else:
            act_ref, ng_ref, *refs = refs
        keep, send, sum_ref, up_acc, down_acc = refs
        i = pl.program_id(0)

        @pl.when(i == 0)
        def _():
            up_acc[...] = jnp.zeros_like(up_acc)
            down_acc[...] = jnp.zeros_like(down_acc)
            sum_ref[...] = jnp.zeros_like(sum_ref)

        x = pick(count, no_ref, nt_ref)
        cot = (pick(count, co_ref, ct_ref).astype(f32) * scal_ref[0]).astype(bf16)
        up_now = up_ref[...].reshape(width, hidden)
        down_now = dn_ref[...].reshape(hidden, width)
        h = dot(x, up_now) + b_ref[0:1, :]
        cdf = 0.5 * (1.0 + lax.erf(h * RSQRT2))
        act = (h * cdf).astype(bf16)
        slope = cdf + h * (RSQRT2PI * jnp.exp(-0.5 * h * h))
        act_ref[...] = act
        grad = dot(cot, down_now, NT) * slope
        sum_ref[7:8, :] += jnp.sum(grad, axis=0, keepdims=True)
        low = grad.astype(bf16)
        ng = dot(low, up_now, NT)
        up_acc[...] += dot(x, low, TN)
        down_acc[...] += dot(act, cot, TN)
        if last:
            ng = ng + ng_in[...].astype(f32)

            @pl.when(i < count)
            def _():
                ngo_ref[...] = ng

            @pl.when((i >= count) & (i < count + count // 2))
            def _():
                nga_ref[...] = ng.astype(bf16)

            @pl.when(i >= count + count // 2)
            def _():
                ngb_ref[...] = ng.astype(bf16)
        else:
            ng_ref[...] = ng.astype(bf16)

        @pl.when(i == 2 * count - 1)
        def _():
            units = scal_ref[1]

            @pl.when(scal_ref[2] < 0.5)
            def _():
                keep[...] = (up_acc[...] * units).astype(bf16)
                send[...] = (down_acc[...] * units).astype(bf16)

            @pl.when(scal_ref[2] > 0.5)
            def _():
                keep[...] = (down_acc[...] * units).astype(bf16)
                send[...] = (up_acc[...] * units).astype(bf16)

            sum_ref[...] = sum_ref[...] * units

    own, other = halves(block, width, count)
    every = pl.BlockSpec((block, width), lambda i: (i, 0))
    up_spec, down_spec = (
        pl.BlockSpec(
            (slices, None, depth, width), lambda i, j=j: (0, j, 0, 0), pipeline_mode=pl.Buffered(1)
        )
        for j in (up_place, down_place)
    )
    ins = [scalars(), own, other, own, other, whole(bias), up_spec, down_spec]
    args = [scal, norm_own, norm_other, cot_own, cot_other, bias, up, down]
    outs = [every]
    shapes = [shape((2 * rows, hidden), bf16)]
    if last:
        ins += [every]
        args += [earlier]
        half = count // 2
        top = pl.BlockSpec((block, width), lambda i: (jnp.clip(i - count, 0, half - 1), 0))
        low = pl.BlockSpec((block, width), lambda i: (jnp.maximum(i - count - half, 0), 0))
        outs += [own, top, low]
        shapes += [shape((rows, width), f32)] + [shape((rows // 2, width), bf16)] * 2
    else:
        outs += [every]
        shapes += [shape((2 * rows, width), bf16)]
    assert width == hidden
    terms = [shape((width, hidden), bf16)] * 2
    sums = shape((8, hidden), f32)
    return call(
        kernel,
        "feed_forward",
        (2 * count,),
        ins,
        outs + [whole(terms[0]), whole(terms[1]), whole(sums)],
        shapes + terms + [sums],
        [pltpu.VMEM((width, hidden), f32), pltpu.VMEM((hidden, width), f32)],
        flops=20 * rows * width * hidden,
        nbytes=24 * rows * width + 12 * width * hidden,
        exps=4 * rows * hidden,
        weight=1000 if last else 1e-6,
    )(*args)


def second_back(middle, grad_own, grad_received, cot, params, scal):
    rows, width = middle.shape
    block = 256
    half = rows // block // 2
    last = rows // block - 1

    def kernel(scal_ref, mid_ref, go_ref, ga_ref, gb_ref, cot_ref, par_ref, out_ref, low_ref, sum_ref):
        i = pl.program_id(0)
        unit, inverse = normalize(mid_ref[...])
        grad = go_ref[...] + pick(half, ga_ref, gb_ref).astype(f32)
        cot = cot_ref[...].astype(f32) * scal_ref[0]
        out = cot + norm_back(grad, par_ref[3:4, :], unit, inverse)
        out_ref[...] = out
        low_ref[...] = out.astype(bf16)
        sums = [jnp.sum(v, axis=0, keepdims=True) for v in (grad * unit, grad, out, cot)]
        add_rows(sum_ref, sums, i == 0, 2)

        @pl.when(i == last)
        def _():
            sum_ref[...] = sum_ref[...] * scal_ref[1]

    spec = pl.BlockSpec((block, width), lambda i: (i, 0))
    sums = shape((8, width), f32)
    return call(
        kernel,
        "second_back",
        (rows // block,),
        [scalars(), spec, spec, *halves(block, width, half), spec, whole(params)],
        [spec, spec, whole(sums)],
        [shape((rows, width), f32), shape((rows, width), bf16), sums],
        flops=30 * rows * width,
        nbytes=18 * rows * width,
    )(scal, middle, grad_own, *grad_received, cot, params)


def output_back(low, attended, weights, scal, earlier=None):
    rows, width = low.shape
    cols = weights[0].shape[0]
    block = 512
    last = earlier is not None

    def kernel(scal_ref, low_ref, a_ref, b_ref, wa_ref, wb_ref, *refs):
        before = refs[:2] if last else (None, None)
        ga_ref, gb_ref, ta_ref, tb_ref, acc_a, acc_b = refs[2 if last else 0 :]
        i = pl.program_id(0)
        now = low_ref[...]
        ga_ref[...] = dot(now, wa_ref[...], NT).astype(bf16)
        gb_ref[...] = dot(now, wb_ref[...], NT).astype(bf16)
        for acc, rows_ref, old in ((acc_a, a_ref, before[0]), (acc_b, b_ref, before[1])):

            @pl.when(i == 0)
            def _():
                acc[...] = jnp.zeros_like(acc) if old is None else old[...]

            acc[...] += dot(rows_ref[...], now, TN)

        @pl.when(i == rows // block - 1)
        def _():
            factor = scal_ref[1] if last else 1.0
            ta_ref[...] = (acc_a[...] * factor).astype(ta_ref.dtype)
            tb_ref[...] = (acc_b[...] * factor).astype(tb_ref.dtype)

    thin = pl.BlockSpec((block, cols), lambda i: (i, 0))
    terms = [shape((cols, width), bf16 if last else f32)] * 2
    before = list(earlier or ())
    return call(
        kernel,
        "output_back",
        (rows // block,),
        [scalars(), pl.BlockSpec((block, width), lambda i: (i, 0)), thin, thin]
        + [whole(w) for w in weights]
        + [whole(t) for t in before],
        [thin, thin, whole(terms[0]), whole(terms[1])],
        [shape((rows, cols), bf16)] * 2 + terms,
        [pltpu.VMEM((cols, width), f32)] * 2,
        flops=8 * rows * width * cols,
        nbytes=2 * rows * width + 8 * rows * cols,
        weight=1e-6 if last else 1000,
    )(scal, low, *attended, *weights, *before)


def side_by_side(refs):
    return jnp.concatenate([ref[p] for ref in refs for p in range(ref.shape[0])], 1)


def pair_specs(grads, block, place):
    return [
        pl.BlockSpec((g.shape[0], block, g.shape[2]), lambda i: (0, place(i), 0)) for g in grads
    ]


def input_term(norm_own, norm_other, grads, scal, other=None, outputs=(), place=None):
    rows, width = norm_own.shape
    pairs = sum(g.shape[0] for g in grads)
    cols = pairs * LANES
    many = len(grads)
    more = [] if other is None else [other, *outputs]
    quarter = width

    def kernel(scal_ref, *refs):
        place_ref = refs[0] if more else None
        no_ref, nt_ref, *refs = refs[1 if more else 0 :]
        outs, acc = refs[many + len(more) : -1], refs[-1]
        i = pl.program_id(0)
        term = dot(pick(1, no_ref, nt_ref), side_by_side(refs[:many]), TN)

        @pl.when(i == 0)
        def _():
            acc[...] = term

        def total(j, p):
            at = (3 * p + j) * LANES
            return (acc[:, at : at + LANES] + term[:, at : at + LANES]) * scal_ref[1]

        def store(half, keep, send):
            for p in range(pairs):
                lanes = slice(p * LANES, (p + 1) * LANES)
                for out_ref, j in ((keep, 2 * half), (send, 2 * half + 1)):
                    if j < 3:
                        final = total(j, p) + refs[many][j * width : (j + 1) * width, lanes].astype(f32)
                        out_ref[:, lanes] = final.astype(bf16)
                        continue
                    for k in range(width // cols):
                        at = slice(k * cols + p * LANES, k * cols + (p + 1) * LANES)
                        final = refs[many + 1][:, at].astype(f32) + refs[many + 2][:, at].astype(f32)
                        out_ref[k * cols : (k + 1) * cols, lanes] = final.astype(bf16)

        @pl.when(i == 1)
        def _():
            if not more:
                for p in range(pairs):
                    for j in range(3):
                        at = (slice(j * width, (j + 1) * width), slice(p * LANES, (p + 1) * LANES))
                        outs[0][at] = total(j, p).astype(bf16)
            for half in range(2 if more else 0):
                keep, send = outs[2 * half], outs[2 * half + 1]

                @pl.when(place_ref[half] == 0)
                def _():
                    store(half, keep, send)

                @pl.when(place_ref[half] == 1)
                def _():
                    store(half, send, keep)

    out = [shape((quarter, cols), bf16)] * 4 if more else [shape((3 * width, cols), bf16)]
    return call(
        kernel,
        "input_term",
        (2,),
        [scalars()]
        + [scalars()] * (1 if more else 0)
        + [*halves(rows, width, 1)]
        + pair_specs(grads, rows, lambda i: i)
        + [whole(m) for m in more],
        [whole(o) for o in out],
        out,
        [pltpu.VMEM((width, 3 * cols), f32)],
        flops=12 * rows * width * cols,
        nbytes=4 * rows * width + 12 * rows * cols + 12 * width * cols,
    )(scal, *([place] if more else []), norm_own, norm_other, *grads, *more)


def join_weights(refs, joined):
    @pl.when(pl.program_id(0) == 0)
    def _():
        place = 0
        for ref in refs:
            for p in range(ref.shape[2] // LANES):
                for j in range(3):
                    joined[:, place : place + LANES] = ref[j, :, p * LANES : (p + 1) * LANES]
                    place += LANES


def norm1_other(grads, weights):
    rows = grads[0].shape[1] // 2
    width, cols = weights[0].shape[1:]
    block = 512
    count = rows // block
    many = len(grads)

    def kernel(*refs):
        out_ref, joined = refs[-2:]
        join_weights(refs[many:-2], joined)
        out_ref[...] = dot(side_by_side(refs[:many]), joined[...], NT).astype(bf16)

    return call(
        kernel,
        "first_other",
        (count,),
        pair_specs(grads, block, lambda i: i + count) + [whole(w) for w in weights],
        pl.BlockSpec((block, width), lambda i: (i, 0)),
        shape((rows, width), bf16),
        [pltpu.VMEM((width, 3 * cols * len(weights)), bf16)],
        flops=12 * rows * width * cols,
        nbytes=12 * rows * cols + 2 * rows * width + 12 * width * cols,
    )(*grads, *weights)


def norm1_own(grads, weights, received, tokens, middle_grad, params, scal):
    rows, width = tokens.shape
    cols = weights[0].shape[2]
    block = 256
    last = rows // block - 1
    many = len(grads)

    def kernel(scal_ref, *refs):
        rec_ref, tok_ref, mid_ref, par_ref, out_ref, sum_ref, joined = refs[many + len(weights) :]
        i = pl.program_id(0)
        join_weights(refs[many : many + len(weights)], joined)
        grad = dot(side_by_side(refs[:many]), joined[...], NT) + rec_ref[...].astype(f32)
        unit, inverse = normalize(tok_ref[...].astype(f32))
        out = mid_ref[...] + norm_back(grad, par_ref[0:1, :], unit, inverse)
        out_ref[...] = out.astype(bf16)
        sums = [jnp.sum(v, axis=0, keepdims=True) for v in (grad * unit, grad)]
        add_rows(sum_ref, sums, i == 0, 0)

        @pl.when(i == last)
        def _():
            sum_ref[...] = sum_ref[...] * scal_ref[1]

    spec = pl.BlockSpec((block, width), lambda i: (i, 0))
    sums = shape((8, width), f32)
    return call(
        kernel,
        "first_own",
        (rows // block,),
        [scalars()]
        + pair_specs(grads, block, lambda i: i)
        + [whole(w) for w in weights]
        + [spec] * 3
        + [whole(params)],
        [spec, whole(sums)],
        [shape((rows, width), bf16), sums],
        [pltpu.VMEM((width, 3 * cols * len(weights)), bf16)],
        flops=12 * rows * width * cols,
        nbytes=12 * rows * cols + 10 * rows * width + 12 * width * cols,
    )(scal, *grads, *weights, received, tokens, middle_grad, params)


def down_specs(weights):
    return [
        pl.BlockSpec(
            (w.shape[0], None, *w.shape[2:]), lambda i, j=j: (0, j, 0, 0), pipeline_mode=pl.Buffered(1)
        )
        for w, j in weights
    ]


def down_product(acts, weights):
    total = None
    for a_ref, w_ref in zip(acts, weights, strict=True):
        part = dot(a_ref[...], w_ref[...].reshape(a_ref.shape[1], w_ref.shape[-1]))
        total = part if total is None else total + part
    return total


def result_other(acts, weights):
    rows, hidden = acts[0].shape
    rows = rows // 2
    width = weights[0][0].shape[-1]
    block = 512
    start = rows // block
    many = len(acts)

    def kernel(*refs):
        refs[-1][...] = down_product(refs[:many], refs[many:-1]).astype(bf16)

    return call(
        kernel,
        "result_other",
        (rows // block,),
        [pl.BlockSpec((block, hidden), lambda i: (i + start, 0))] * many + down_specs(weights),
        pl.BlockSpec((block, width), lambda i: (i, 0)),
        shape((rows, width), bf16),
        flops=2 * many * rows * hidden * width,
        nbytes=2 * many * rows * hidden,
    )(*acts, *[w for w, _ in weights])


def block_result(middle, acts, weights, received, params, scal):
    rows, width = middle.shape
    hidden = acts[0].shape[1]
    block = 256
    many = len(acts)

    def kernel(scal_ref, mid_ref, rec_ref, par_ref, *refs):
        total = mid_ref[...] + down_product(refs[:many], refs[many:-1])
        total = total + rec_ref[...].astype(f32) + par_ref[5:6, :]
        refs[-1][...] = (total * scal_ref[0]).astype(bf16)

    spec = pl.BlockSpec((block, width), lambda i: (i, 0))
    return call(
        kernel,
        "block_result",
        (rows // block,),
        [scalars(), spec, spec, whole(params)]
        + [pl.BlockSpec((block, hidden), lambda i: (i, 0))] * many
        + down_specs(weights),
        spec,
        shape((rows, width), bf16),
        flops=2 * many * rows * hidden * width,
        nbytes=12 * rows * width,
    )(scal, middle, received, params, *acts, *[w for w, _ in weights])


def add_terms(*terms):
    rows, width = terms[0].shape
    block = 256

    def kernel(*refs):
        total = refs[0][...].astype(f32)
        for ref in refs[1:-1]:
            total = total + ref[...].astype(f32)
        refs[-1][...] = total.astype(bf16)

    spec = pl.BlockSpec((block, width), lambda i: (i, 0))
    return call(
        kernel,
        "add_terms",
        (rows // block,),
        [spec] * len(terms),
        spec,
        shape((rows, width), bf16),
        flops=len(terms) * rows * width,
        nbytes=2 * (len(terms) + 1) * rows * width,
    )(*terms)


def body(
    tokens,
    out_grad,
    item_counts,
    group_dataset,
    variable_mask,
    first_gain,
    first_shift,
    input_weight,
    input_bias,
    output_weight,
    output_bias,
    second_gain,
    second_shift,
    up_weight,
    up_bias,
    down_weight,
    down_bias,
):
    shard_count = lax.axis_size("mp")
    groups = lax.axis_size("dp")
    rows, width = tokens.shape
    cols = input_weight.shape[2]
    hidden = up_weight.shape[1]

    def core_swap(value):
        return lax.ppermute(value, "mp", [(i, i ^ 1) for i in range(shard_count)])

    def chip_swap(value):
        return lax.ppermute(value, "mp", [(i, i ^ 2) for i in range(shard_count)])

    def after(value, *others):
        return lax.optimization_barrier((value, *others))[0]

    def along(value, bit):
        return lax.ppermute(value, "dp", [(i, i ^ bit) for i in range(groups)])

    group = lax.axis_index("dp")

    slice_rows = up_weight.shape[0] // groups
    slices = [
        lax.dynamic_slice_in_dim(weight, group * slice_rows, slice_rows, 0)
        for weight in (up_weight, down_weight)
    ]
    slice_two = chip_swap(jnp.stack(slices)[None])
    bias_pack = jnp.concatenate([up_bias, input_bias[0], input_bias[1]]).reshape(-1, LANES)
    bias_two = chip_swap(bias_pack)
    wi_two = chip_swap(after(input_weight, *slices))
    cot_t = core_swap(out_grad)
    normed1 = first_norm(tokens, first_gain, first_shift)
    normed1_t = core_swap(normed1)
    item_counts, variable_mask, output_bias = after(
        (item_counts, variable_mask, output_bias), normed1
    )

    live = (lax.axis_index("mp") // 2 < item_counts[0]).astype(f32)
    dataset_hit = jnp.arange(variable_mask.shape[0], dtype=jnp.int32) == group_dataset[0]
    own_units = (
        item_counts[0] * jnp.sum(jnp.where(dataset_hit[:, None], variable_mask, 0))
    ).astype(f32)
    scal = jnp.stack([live, own_units, (group % 2).astype(f32)])
    zero = jnp.zeros((width,), f32)
    params = jnp.stack(
        [first_gain, first_shift, output_bias, second_gain, second_shift, down_bias, zero, zero]
    )

    qkv_one = project(normed1, input_weight, input_bias)
    wo_two = chip_swap(after(output_weight, qkv_one[0]))
    ff_weights_two = lax.all_gather(after(slice_two, qkv_one[0]), "dp", axis=0, tiled=True)
    qkv_one = project(normed1_t, input_weight, after(input_bias, qkv_one[0]), qkv_one)
    att_one, att_one_send, turned_one, stat_one = attend_forward(*qkv_one)
    att_one_t = core_swap(att_one_send)
    wo_one_t = core_swap(output_weight)
    bias_two = after(bias_two, att_one).reshape(-1)
    up_bias_one = up_bias.reshape(1, hidden)
    up_bias_two = bias_two[:hidden].reshape(1, hidden)
    in_bias_two = bias_two[hidden:].reshape(2, cols)
    qkv_two = project(after(normed1, att_one), wi_two, in_bias_two)
    qkv_two = project(normed1_t, wi_two, after(in_bias_two, att_one_t), qkv_two)
    att_two, att_two_send, turned_two, stat_two = attend_forward(*qkv_two)
    wo_two_t = core_swap(after(wo_two, qkv_two[0]))
    att_two_t = core_swap(att_two_send)
    middle, normed2 = output_own(
        tokens,
        [att_one, att_two, att_one_t, after(att_two_t, ff_weights_two)],
        [output_weight, wo_two, wo_one_t, wo_two_t],
        params,
    )
    normed2_t = core_swap(normed2)

    act_two, ng_two, keep_two, send_two, up_sum_two = feed_forward(
        normed2, normed2_t, out_grad, cot_t, up_bias_two, (ff_weights_two, 0), (ff_weights_two, 1), scal
    )
    two_received = along(send_two, 1)
    up_one, down_one = ((w.reshape(1, 1, -1, width), 0) for w in (up_weight, down_weight))
    act_one, ng_own, *ng_sends, keep_one, send_one, up_sum_one = feed_forward(
        normed2, normed2_t, out_grad, cot_t, up_bias_one, up_one, down_one, scal, ng_two
    )
    one_received = along(send_one, 1)
    ng_received = [core_swap(ng_send) for ng_send in ng_sends]
    middle_grad, middle_low, second_sums = second_back(
        middle, ng_own, ng_received, out_grad, params, scal
    )
    pair_two = add_terms(keep_two, after(two_received, middle_low))
    pair_received = chip_swap(pair_two)
    middle_low_t = core_swap(middle_low)
    middle_low = after(middle_low, pair_two)
    out_weights = [output_weight, wo_two]
    g_one, g_two, *wo_terms = output_back(
        middle_low, [att_one, att_two], out_weights, scal
    )
    g_one_t, g_two_t, wo_one_term, wo_two_term = output_back(
        middle_low_t, [att_one_send, att_two_send], out_weights, scal, wo_terms
    )

    def both(own, received, *last):
        return (own.astype(f32) + after(received, *last).astype(f32)).astype(bf16)

    back_two = [attend_backward(*qkv_two, g_two, g_two_t, turned_two, stat_two, 0, 1)]
    wait = back_two[0][0]
    acts = [act_two, act_one]
    downs = [(ff_weights_two, 1), down_one]
    result_send = result_other([after(act_two, wait), act_one], downs)
    result_received = core_swap(result_send)
    ff_both = add_terms(keep_one, one_received, after(pair_received, wait, result_send))
    ff_sum = lax.psum(
        ff_both, "dp", axis_index_groups=[list(range(k, groups, 2)) for k in range(2)]
    )
    back_two.append(
        attend_backward(
            *qkv_two, after(g_two, ff_both), g_two_t, turned_two, stat_two, 1, cols // LANES - 1
        )
    )
    grads_two = [back[0] for back in back_two]
    wi_two_term = input_term(normed1, normed1_t, grads_two, scal)[0]
    wo_received = chip_swap(after(wo_two_term, grads_two[1]))
    wi_received = chip_swap(wi_two_term)
    g_one = after(g_one, wi_two_term)
    back_one = [attend_backward(*qkv_one, g_one, g_one_t, turned_one, stat_one, 0, cols // LANES)]
    grads_one = [back[0] for back in back_one]

    bits = [1 << k for k in range(groups.bit_length() - 1)]
    orders = [bits, bits[1:2] + bits[:1] + bits[2:]]

    def upper(bit):
        return (group // bit) % 2

    def split(part, bit):
        half = part.shape[0] // 2
        return (
            lax.dynamic_slice_in_dim(part, upper(bit) * half, half, 0),
            lax.dynamic_slice_in_dim(part, (1 - upper(bit)) * half, half, 0),
        )

    place = jnp.stack([upper(order[0]) for order in orders]).astype(jnp.int32)
    keep_a, send_a, keep_b, send_b = input_term(
        normed1, normed1_t, grads_one, scal, wi_received, (wo_one_term, wo_received), place
    )
    keeps, sends = (keep_a, keep_b), (send_a, send_b)
    received = [along(sends[k], orders[k][0]) for k in range(2)]

    grads = grads_one + grads_two
    weights = [input_weight, wi_two]
    ng1_received = core_swap(norm1_other(grads, [input_weight, after(wi_two, *sends)]))
    parts = [both(keeps[k], received[k]) for k in range(2)]
    last = len(bits) - 1
    for turn in range(1, last + 1):
        keeps, sends = zip(*[split(parts[k], orders[k][turn]) for k in range(2)], strict=True)
        received = [along(sends[k], orders[k][turn]) for k in range(2)]
        wait = []
        if turn == 1:
            ff_sum_other = along(after(ff_sum, *sends), 1)
        if turn == last:
            token_grad, first_sums = norm1_own(
                grads, weights, ng1_received, after(tokens, *sends), middle_grad, params, scal
            )
            wait = [token_grad]
        parts = [both(keeps[k], received[k], *wait) for k in range(2)]
    first_sums = after(first_sums, *parts)
    for turn in reversed(range(len(bits))):
        if turn == min(1, last):
            parts = [after(part, ff_sum_other) for part in parts]
        received = [along(parts[k], orders[k][turn]) for k in range(2)]
        last_parts = list(parts)
        if turn == last:
            result = block_result(
                after(middle, *parts), acts, downs, result_received, params, scal
            )
            received = [after(value, result) for value in received]
        for k in range(2):
            is_upper = upper(orders[k][turn]) == 1
            parts[k] = jnp.concatenate(
                [jnp.where(is_upper, received[k], parts[k]), jnp.where(is_upper, parts[k], received[k])]
            )
    wi_rows = 3 * width
    tail_sum = jnp.concatenate(parts)
    wi_sum = tail_sum[:wi_rows].reshape(3, width, cols)
    wo_sum = tail_sum[wi_rows:].reshape(width // cols, cols, cols)
    wo_sum = jnp.concatenate([wo_sum[k] for k in range(width // cols)], 1)

    lower = group % 2 == 0
    up_sum = jnp.where(lower, ff_sum, ff_sum_other)
    down_sum = jnp.where(lower, ff_sum_other, ff_sum)

    def quarter_rows(parts, up_sums):
        sums_all = jnp.concatenate([part[1] for part in parts], 1)
        rest = jnp.full((1, width - 2 * cols), own_units)
        bias_row = jnp.concatenate([sums_all[0:1] * own_units, sums_all[1:2] * own_units, rest], 1)
        return up_sums + jnp.pad(bias_row, ((6, 1), (0, 0)))

    late = first_sums + second_sums
    late = late + core_swap(late)
    late_one = late + quarter_rows(back_one, up_sum_one)
    late = late_one + chip_swap(late + quarter_rows(back_two, up_sum_two))
    for bit in bits[1:] + bits[:1]:
        late = after(late, result) if bit > 1 else after(late, *last_parts)
        late = late + along(late, bit)
    share = 2.0 / late[6, -1]
    late = late * share

    return (
        result,
        token_grad,
        late[0],
        late[1],
        wi_sum.astype(f32) * share,
        late[6, : 2 * cols].reshape(2, cols),
        wo_sum.astype(f32) * share,
        late[4],
        late[2],
        late[3],
        up_sum.astype(f32) * share,
        late[7],
        down_sum.astype(f32) * share,
        late[5],
    )


def solution(mesh):
    in_specs = (
        P(("dp", "mp"), None),
        P(("dp", "mp"), None),
        P("dp"),
        P("dp"),
        P(),
        P(),
        P(),
        P(None, None, "mp"),
        P(None, "mp"),
        P("mp", None),
        P(),
        P(),
        P(),
        P(None, "mp"),
        P("mp"),
        P("mp", None),
        P(),
    )
    out_specs = (
        P(("dp", "mp"), None),
        P(("dp", "mp"), None),
        P(),
        P(),
        P(None, None, "mp"),
        P(None, "mp"),
        P("mp", None),
        P(),
        P(),
        P(),
        P(None, "mp"),
        P("mp"),
        P("mp", None),
        P(),
    )
    return jax.shard_map(body, mesh=mesh, in_specs=in_specs, out_specs=out_specs, check_vma=False)
```

```python
import jax
import jax.numpy as jnp
from jax import lax
from jax.experimental import pallas as pl
from jax.experimental.pallas import tpu as pltpu
from jax.sharding import PartitionSpec as P

HEAD_DIM = 64
LANES = 128
norm_eps = 1e-06
SCALE = HEAD_DIM**-0.5
LOG2E = 1.4426950408889634
RSQRT2 = 0.7071067811865476
RSQRT2PI = 0.3989422804014327

bf16 = jnp.bfloat16
f32 = jnp.float32
NN = (((1,), (0,)), ((), ()))
NT = (((1,), (1,)), ((), ()))
TN = (((0,), (0,)), ((), ()))
VMEM_BYTES = 60 << 20


def dot(left, right, dims=NN):
    return lax.dot_general(left, right, dims, preferred_element_type=f32)


def shape(dims, dtype):
    return jax.ShapeDtypeStruct(dims, dtype)


def whole(array):
    rank = len(array.shape)
    return pl.BlockSpec(array.shape, lambda *_: (0,) * rank, pipeline_mode=pl.Buffered(1))


def scalars():
    return pl.BlockSpec(memory_space=pltpu.SMEM)


def call(kernel, name, grid, in_specs, out_specs, out_shape, scratch=(), flops=0, nbytes=0, exps=0, weight=1e-6, aliases=None):
    return pl.pallas_call(
        kernel,
        name=name,
        grid=grid,
        in_specs=in_specs,
        out_specs=out_specs,
        out_shape=out_shape,
        scratch_shapes=list(scratch),
        input_output_aliases=aliases or {},
        compiler_params=pltpu.CompilerParams(vmem_limit_bytes=VMEM_BYTES),
        cost_estimate=pl.CostEstimate(
            flops=int(flops * weight), bytes_accessed=int(nbytes * weight), transcendentals=int(exps * weight)
        ),
    )


def split_two(values):
    high = values.astype(bf16)
    return high, (values - high.astype(f32)).astype(bf16)


def split_three(values):
    high = values.astype(bf16)
    rest = values - high.astype(f32)
    mid = rest.astype(bf16)
    return high, mid, (rest - mid.astype(f32)).astype(bf16)


def stat_rows(vector, rows):
    high, mid, rest = (part.astype(f32) for part in split_three(vector))
    row = lax.broadcasted_iota(jnp.int32, (rows, vector.shape[1]), 0)
    return jnp.where(
        row == 0, high, jnp.where(row == 1, mid, jnp.where(row == 2, rest, 0.0))
    ).astype(bf16)


def normalize(values):
    centered = values - jnp.mean(values, axis=-1, keepdims=True)
    variance = jnp.mean(centered * centered, axis=-1, keepdims=True)
    inverse = lax.rsqrt(variance + norm_eps)
    return centered * inverse, inverse


def norm_back(grad, gain, unit, inverse):
    scaled = grad * gain
    return inverse * (
        scaled
        - jnp.mean(scaled, axis=-1, keepdims=True)
        - unit * jnp.mean(scaled * unit, axis=-1, keepdims=True)
    )


def add_rows(ref, rows, first, start):
    @pl.when(first)
    def _():
        ref[...] = jnp.zeros_like(ref)

    for place, row in enumerate(rows):
        ref[start + place : start + place + 1, :] += row


def first_norm(tokens, gain, shift):
    rows, width = tokens.shape
    block = 256

    def kernel(tok_ref, gain_ref, shift_ref, norm_ref):
        unit, _ = normalize(tok_ref[...].astype(f32))
        gain_row = gain_ref[...].reshape(1, width)
        norm_ref[...] = (unit * gain_row + shift_ref[...].reshape(1, width)).astype(bf16)

    spec = pl.BlockSpec((block, width), lambda i: (i, 0))
    return call(
        kernel,
        "first_norm",
        (rows // block,),
        [spec, whole(gain), whole(shift)],
        spec,
        shape((rows, width), bf16),
        flops=20 * rows * width,
        nbytes=4 * rows * width,
    )(tokens, gain, shift)


def halves(block, width, count):
    own = pl.BlockSpec((block, width), lambda i, *_: (jnp.minimum(i, count - 1), 0))
    other = pl.BlockSpec((block, width), lambda i, *_: (jnp.maximum(i - count, 0), 0))
    return own, other


def pick(count, own_ref, other_ref):
    return jnp.where(pl.program_id(0) < count, own_ref[...], other_ref[...])


def project(norm, weight, bias, earlier=None):
    rows, width = norm.shape
    cols = weight.shape[2]
    block = 512
    start = 0 if earlier is None else rows // block
    skip = 0 if earlier is None else 3

    def kernel(x_ref, w_ref, b_ref, *refs):
        q_ref, k_ref, v_ref = refs[skip:]
        x = x_ref[...]
        q_ref[...] = (dot(x, w_ref[0]) + b_ref[0:1, :]).astype(bf16)
        k_ref[...] = dot(x, w_ref[1]).astype(bf16)
        v_ref[...] = (dot(x, w_ref[2]) + b_ref[1:2, :]).astype(bf16)

    out = pl.BlockSpec((block, cols), lambda i: (i + start, 0))
    return call(
        kernel,
        "project",
        (rows // block,),
        [pl.BlockSpec((block, width), lambda i: (i, 0)), whole(weight), whole(bias)]
        + [pl.BlockSpec(memory_space=pl.ANY)] * skip,
        [out] * 3,
        [shape((2 * rows, cols), bf16)] * 3,
        flops=6 * rows * width * cols,
        nbytes=2 * rows * width + 6 * width * cols + 6 * rows * cols,
        weight=1000,
        aliases={3 + k: k for k in range(skip)},
    )(norm, weight, bias, *(earlier or ()))


def project_both(norm_own, norm_other, weight, bias):
    rows, width = norm_own.shape
    cols = weight.shape[2]
    block = 512
    count = rows // block

    def kernel(own_ref, other_ref, w_ref, b_ref, q_ref, k_ref, v_ref):
        x = pick(count, own_ref, other_ref)
        q_ref[...] = (dot(x, w_ref[0]) + b_ref[0:1, :]).astype(bf16)
        k_ref[...] = dot(x, w_ref[1]).astype(bf16)
        v_ref[...] = (dot(x, w_ref[2]) + b_ref[1:2, :]).astype(bf16)

    out = pl.BlockSpec((block, cols), lambda i: (i, 0))
    return call(
        kernel,
        "project_both",
        (2 * count,),
        [*halves(block, width, count), whole(weight), whole(bias)],
        [out] * 3,
        [shape((2 * rows, cols), bf16)] * 3,
        flops=12 * rows * width * cols,
        nbytes=4 * rows * width + 6 * width * cols + 12 * rows * cols,
        weight=1000,
    )(norm_own, norm_other, weight, bias)


def attend_forward(queries, keys, values):
    rows, width = queries.shape
    chunk = min(512, rows)

    def kernel(q_ref, k_ref, v_ref, own_ref, other_ref, ot_ref, lse_ref):
        k = k_ref[...]
        lane = lax.broadcasted_iota(jnp.int32, k.shape, 1)
        rolled = pltpu.roll(k.astype(f32), HEAD_DIM, 1).astype(bf16)
        turned = v_ref[...].astype(f32).T
        ones = jnp.ones((HEAD_DIM, rows), bf16)
        q_turned = q_ref[...].astype(f32).T * (SCALE * LOG2E)
        outs = []
        for head in range(2):
            at = head * HEAD_DIM
            k_two = jnp.where(lane < HEAD_DIM, k, rolled) if head == 0 else jnp.where(lane < HEAD_DIM, rolled, k)
            own = turned[at : at + HEAD_DIM].astype(bf16)
            v_turned = jnp.concatenate([own, ones] if head == 0 else [ones, own], 0)
            q_two = jnp.concatenate(split_two(q_turned[at : at + HEAD_DIM]), 0)
            total = peak = None
            for j in range(rows // chunk):
                part = slice(j * chunk, (j + 1) * chunk)
                scores = dot(k_two[part], q_two)
                top = jnp.max(scores.reshape(chunk // 8, 8, rows).max(axis=0), axis=0, keepdims=True)
                higher = top if peak is None else jnp.maximum(peak, top)
                weights = jnp.exp2(scores - higher).astype(bf16)
                add = dot(v_turned[:, part], weights)
                total = add if total is None else total * jnp.exp2(peak - higher) + add
                peak = higher
            row_sum = total[HEAD_DIM - at : HEAD_DIM - at + 1]
            outs.append(total[at : at + HEAD_DIM] / row_sum)
            lse_ref[head : head + 1, :] = peak + jnp.log2(row_sum)
        attended = jnp.concatenate(outs, 0)
        ot_ref[...] = attended
        own_ref[...] = attended[:, : rows // 2].T.astype(bf16)
        other_ref[...] = attended[:, rows // 2 :].T.astype(bf16)

    by_pair = pl.BlockSpec((rows, LANES), lambda j: (0, j))
    by_half = pl.BlockSpec((rows // 2, LANES), lambda j: (0, j))
    pairs = width // LANES
    return call(
        kernel,
        "attend_forward",
        (pairs,),
        [by_pair] * 3,
        [
            by_half,
            by_half,
            pl.BlockSpec((LANES, rows), lambda j: (j, 0)),
            pl.BlockSpec((None, 8, rows), lambda j: (j, 0, 0)),
        ],
        [shape((rows // 2, width), bf16)] * 2
        + [shape((width, rows), f32), shape((pairs, 8, rows), f32)],
        flops=16 * rows * rows * width,
        nbytes=12 * rows * width,
        exps=rows * rows * width // HEAD_DIM,
        weight=1000,
    )(queries, keys, values)


def attend_backward(queries, keys, values, grad_own, grad_other, out_turned, stats, first, pairs):
    rows = queries.shape[0]
    width = LANES * pairs
    block = grad_own.shape[0]
    chunk = 256
    count = rows // block

    def kernel(
        q_ref, k_ref, v_ref, go_ref, gt_ref, ot_ref, lse_ref, d_ref, sum_ref,
        k_wide, k_turned, v_wide, dk_acc, dv_acc,
    ):
        i = pl.program_id(1)

        @pl.when(i == 0)
        def _():
            k = k_ref[...]
            v = v_ref[...]
            lane = lax.broadcasted_iota(jnp.int32, k.shape, 1)
            k_rolled = pltpu.roll(k.astype(f32), HEAD_DIM, 1).astype(bf16)
            v_rolled = pltpu.roll(v.astype(f32), HEAD_DIM, 1).astype(bf16)
            ones = jnp.where(lane < 3, 1.0, 0.0).astype(bf16)
            k_wide[0] = jnp.concatenate([jnp.where(lane < HEAD_DIM, k, k_rolled), ones], 1)
            k_wide[1] = jnp.concatenate([jnp.where(lane < HEAD_DIM, k_rolled, k), ones], 1)
            tail = jnp.where(lane < HEAD_DIM + 3, 1.0, 0.0).astype(bf16)
            v_wide[0] = jnp.where(lane < HEAD_DIM, v, tail)
            v_wide[1] = jnp.where(lane < HEAD_DIM, v_rolled, tail)
            k_turned[...] = k.astype(f32).T.astype(bf16)
            dk_acc[...] = jnp.zeros_like(dk_acc)
            dv_acc[...] = jnp.zeros_like(dv_acc)
            sum_ref[...] = jnp.zeros_like(sum_ref)

        q_turned = q_ref[...].astype(f32).T
        q_low = q_turned.astype(bf16)
        q_turned = q_turned * (SCALE * LOG2E)
        g_turned = jnp.where(i == 0, go_ref[...], gt_ref[...]).astype(f32).T
        g_low = g_turned.astype(bf16)
        dqs = []
        for head in range(2):
            part = slice(head * HEAD_DIM, (head + 1) * HEAD_DIM)
            q_wide = jnp.concatenate(
                [*split_two(q_turned[part]), stat_rows(-lse_ref[head : head + 1, :], LANES)], 0
            )
            row_dot = jnp.sum(g_turned[part] * ot_ref[part, :], axis=0, keepdims=True)
            g_wide = jnp.concatenate([g_low[part], stat_rows(-row_dot, HEAD_DIM)], 0)
            dq = None
            for j in range(rows // chunk):
                at = pl.ds(j * chunk, chunk)
                probabilities = jnp.exp2(dot(k_wide[head, at, :], q_wide))
                shifted = dot(v_wide[head, at, :], g_wide)
                probs_low = probabilities.astype(bf16)
                score_grad = (probabilities * shifted).astype(bf16)
                dv_acc[part, at] += dot(g_low[part], probs_low, NT)
                dk_acc[part, at] += dot(q_low[part], score_grad, NT)
                add = dot(k_turned[part, at], score_grad)
                dq = add if dq is None else dq + add
            dqs.append(dq)
        dq = (jnp.concatenate(dqs, 0) * SCALE).T
        d_ref[pl.ds(i * block, block), :LANES] = dq.astype(bf16)
        sum_ref[0:1, :] += jnp.sum(dq, axis=0, keepdims=True)

        @pl.when(i == count - 1)
        def _():
            d_ref[:, LANES : 2 * LANES] = (dk_acc[...] * SCALE).T.astype(bf16)
            dv = dv_acc[...].T
            d_ref[:, 2 * LANES :] = dv.astype(bf16)
            sum_ref[1:2, :] = jnp.sum(dv, axis=0, keepdims=True)

    by_query = pl.BlockSpec((block, LANES), lambda j, i: (i, j + first))
    by_key = pl.BlockSpec((rows, LANES), lambda j, i: (0, j + first))
    half = pl.BlockSpec((block, LANES), lambda j, i: (0, j + first))
    turned_spec = pl.BlockSpec((LANES, block), lambda j, i: (j + first, i))
    stat_spec = pl.BlockSpec((None, 8, block), lambda j, i: (j + first, 0, i))
    out_spec = pl.BlockSpec((None, rows, 3 * LANES), lambda j, i: (j, 0, 0))
    sum_spec = pl.BlockSpec((8, LANES), lambda j, i: (0, j))
    return call(
        kernel,
        "attend_backward",
        (pairs, count),
        [by_query, by_key, by_key, half, half, turned_spec, stat_spec],
        [out_spec, sum_spec],
        [shape((pairs, rows, 3 * LANES), bf16), shape((8, width), f32)],
        [
            pltpu.VMEM((2, rows, 2 * LANES), bf16),
            pltpu.VMEM((LANES, rows), bf16),
            pltpu.VMEM((2, rows, LANES), bf16),
            pltpu.VMEM((LANES, rows), f32),
            pltpu.VMEM((LANES, rows), f32),
        ],
        flops=40 * rows * rows * width,
        nbytes=20 * rows * width,
        exps=rows * rows * width // HEAD_DIM,
        weight=1000,
    )(queries, keys, values, grad_own, grad_other, out_turned, stats)


def output_own(tokens, attended, weights, params):
    rows, width = tokens.shape
    cols = weights[0].shape[0]
    block = 256
    many = len(attended)

    def kernel(t_ref, par_ref, *refs):
        total = None
        for a_ref, w_ref in zip(refs[:many], refs[many : 2 * many], strict=True):
            part = dot(a_ref[...], w_ref[...])
            total = part if total is None else total + part
        mid_ref, norm_ref = refs[2 * many :]
        middle = t_ref[...].astype(f32) + total + par_ref[2:3, :]
        mid_ref[...] = middle
        unit, _ = normalize(middle)
        norm_ref[...] = (unit * par_ref[3:4, :] + par_ref[4:5, :]).astype(bf16)

    spec = pl.BlockSpec((block, width), lambda i: (i, 0))
    thin = pl.BlockSpec((block, cols), lambda i: (i, 0))
    return call(
        kernel,
        "output_own",
        (rows // block,),
        [spec, whole(params)] + [thin] * many + [whole(w) for w in weights],
        [spec, spec],
        [shape((rows, width), f32), shape((rows, width), bf16)],
        flops=2 * rows * many * cols * width,
        nbytes=2 * rows * many * cols + 8 * rows * width,
    )(tokens, params, *attended, *weights)


def feed_forward(norm_own, norm_other, cot_own, cot_other, bias, up, down, scal, earlier=None):
    rows, width = norm_own.shape
    hidden = bias.shape[1]
    block = 512
    count = rows // block
    last = earlier is not None
    (up, up_place), (down, down_place) = up, down
    slices, depth = up.shape[0], up.shape[2]
    def kernel(scal_ref, no_ref, nt_ref, co_ref, ct_ref, b_ref, up_ref, dn_ref, *refs):
        if last:
            ng_in, act_ref, ngo_ref, nga_ref, ngb_ref, *refs = refs
        else:
            act_ref, ng_ref, *refs = refs
        keep, send, sum_ref, up_acc, down_acc = refs
        i = pl.program_id(0)

        @pl.when(i == 0)
        def _():
            up_acc[...] = jnp.zeros_like(up_acc)
            down_acc[...] = jnp.zeros_like(down_acc)
            sum_ref[...] = jnp.zeros_like(sum_ref)

        x = pick(count, no_ref, nt_ref)
        cot = (pick(count, co_ref, ct_ref).astype(f32) * scal_ref[0]).astype(bf16)
        up_now = up_ref[...].reshape(width, hidden)
        down_now = dn_ref[...].reshape(hidden, width)
        h = dot(x, up_now) + b_ref[0:1, :]
        cdf = 0.5 * (1.0 + lax.erf(h * RSQRT2))
        act = (h * cdf).astype(bf16)
        slope = cdf + h * (RSQRT2PI * jnp.exp(-0.5 * h * h))
        act_ref[...] = act
        grad = dot(cot, down_now, NT) * slope
        sum_ref[7:8, :] += jnp.sum(grad, axis=0, keepdims=True)
        low = grad.astype(bf16)
        ng = dot(low, up_now, NT)
        up_acc[...] += dot(x, low, TN)
        down_acc[...] += dot(act, cot, TN)
        if last:
            ng = ng + ng_in[...].astype(f32)

            @pl.when(i < count)
            def _():
                ngo_ref[...] = ng

            @pl.when((i >= count) & (i < count + count // 2))
            def _():
                nga_ref[...] = ng.astype(bf16)

            @pl.when(i >= count + count // 2)
            def _():
                ngb_ref[...] = ng.astype(bf16)
        else:
            ng_ref[...] = ng.astype(bf16)

        @pl.when(i == 2 * count - 1)
        def _():
            units = scal_ref[1]

            @pl.when(scal_ref[2] < 0.5)
            def _():
                keep[...] = (up_acc[...] * units).astype(bf16)
                send[...] = (down_acc[...] * units).astype(bf16)

            @pl.when(scal_ref[2] > 0.5)
            def _():
                keep[...] = (down_acc[...] * units).astype(bf16)
                send[...] = (up_acc[...] * units).astype(bf16)

            sum_ref[...] = sum_ref[...] * units

    own, other = halves(block, width, count)
    every = pl.BlockSpec((block, width), lambda i: (i, 0))
    up_spec, down_spec = (
        pl.BlockSpec(
            (slices, None, depth, width), lambda i, j=j: (0, j, 0, 0), pipeline_mode=pl.Buffered(1)
        )
        for j in (up_place, down_place)
    )
    ins = [scalars(), own, other, own, other, whole(bias), up_spec, down_spec]
    args = [scal, norm_own, norm_other, cot_own, cot_other, bias, up, down]
    outs = [every]
    shapes = [shape((2 * rows, hidden), bf16)]
    if last:
        ins += [every]
        args += [earlier]
        half = count // 2
        top = pl.BlockSpec((block, width), lambda i: (jnp.clip(i - count, 0, half - 1), 0))
        low = pl.BlockSpec((block, width), lambda i: (jnp.maximum(i - count - half, 0), 0))
        outs += [own, top, low]
        shapes += [shape((rows, width), f32)] + [shape((rows // 2, width), bf16)] * 2
    else:
        outs += [every]
        shapes += [shape((2 * rows, width), bf16)]
    assert width == hidden
    terms = [shape((width, hidden), bf16)] * 2
    sums = shape((8, hidden), f32)
    return call(
        kernel,
        "feed_forward",
        (2 * count,),
        ins,
        outs + [whole(terms[0]), whole(terms[1]), whole(sums)],
        shapes + terms + [sums],
        [pltpu.VMEM((width, hidden), f32), pltpu.VMEM((hidden, width), f32)],
        flops=20 * rows * width * hidden,
        nbytes=24 * rows * width + 12 * width * hidden,
        exps=4 * rows * hidden,
        weight=1000 if last else 1e-6,
    )(*args)


def second_back(middle, grad_own, grad_received, cot, params, scal):
    rows, width = middle.shape
    block = 256
    half = rows // block // 2
    last = rows // block - 1

    def kernel(scal_ref, mid_ref, go_ref, ga_ref, gb_ref, cot_ref, par_ref, out_ref, low_ref, sum_ref):
        i = pl.program_id(0)
        unit, inverse = normalize(mid_ref[...])
        grad = go_ref[...] + pick(half, ga_ref, gb_ref).astype(f32)
        cot = cot_ref[...].astype(f32) * scal_ref[0]
        out = cot + norm_back(grad, par_ref[3:4, :], unit, inverse)
        out_ref[...] = out
        low_ref[...] = out.astype(bf16)
        sums = [jnp.sum(v, axis=0, keepdims=True) for v in (grad * unit, grad, out, cot)]
        add_rows(sum_ref, sums, i == 0, 2)

        @pl.when(i == last)
        def _():
            sum_ref[...] = sum_ref[...] * scal_ref[1]

    spec = pl.BlockSpec((block, width), lambda i: (i, 0))
    sums = shape((8, width), f32)
    return call(
        kernel,
        "second_back",
        (rows // block,),
        [scalars(), spec, spec, *halves(block, width, half), spec, whole(params)],
        [spec, spec, whole(sums)],
        [shape((rows, width), f32), shape((rows, width), bf16), sums],
        flops=30 * rows * width,
        nbytes=18 * rows * width,
    )(scal, middle, grad_own, *grad_received, cot, params)


def output_back(low, attended, weights, scal, earlier=None):
    rows, width = low.shape
    cols = weights[0].shape[0]
    block = 512
    last = earlier is not None

    def kernel(scal_ref, low_ref, a_ref, b_ref, wa_ref, wb_ref, *refs):
        before = refs[:2] if last else (None, None)
        ga_ref, gb_ref, ta_ref, tb_ref, acc_a, acc_b = refs[2 if last else 0 :]
        i = pl.program_id(0)
        now = low_ref[...]
        ga_ref[...] = dot(now, wa_ref[...], NT).astype(bf16)
        gb_ref[...] = dot(now, wb_ref[...], NT).astype(bf16)
        for acc, rows_ref, old in ((acc_a, a_ref, before[0]), (acc_b, b_ref, before[1])):

            @pl.when(i == 0)
            def _():
                acc[...] = jnp.zeros_like(acc) if old is None else old[...]

            acc[...] += dot(rows_ref[...], now, TN)

        @pl.when(i == rows // block - 1)
        def _():
            factor = scal_ref[1] if last else 1.0
            ta_ref[...] = (acc_a[...] * factor).astype(ta_ref.dtype)
            tb_ref[...] = (acc_b[...] * factor).astype(tb_ref.dtype)

    thin = pl.BlockSpec((block, cols), lambda i: (i, 0))
    terms = [shape((cols, width), bf16 if last else f32)] * 2
    before = list(earlier or ())
    return call(
        kernel,
        "output_back",
        (rows // block,),
        [scalars(), pl.BlockSpec((block, width), lambda i: (i, 0)), thin, thin]
        + [whole(w) for w in weights]
        + [whole(t) for t in before],
        [thin, thin, whole(terms[0]), whole(terms[1])],
        [shape((rows, cols), bf16)] * 2 + terms,
        [pltpu.VMEM((cols, width), f32)] * 2,
        flops=8 * rows * width * cols,
        nbytes=2 * rows * width + 8 * rows * cols,
        weight=1e-6 if last else 1000,
    )(scal, low, *attended, *weights, *before)


def side_by_side(refs):
    return jnp.concatenate([ref[p] for ref in refs for p in range(ref.shape[0])], 1)


def pair_specs(grads, block, place):
    return [
        pl.BlockSpec((g.shape[0], block, g.shape[2]), lambda i: (0, place(i), 0)) for g in grads
    ]


def input_term(norm_own, norm_other, grads, scal, other=None, outputs=(), place=None):
    rows, width = norm_own.shape
    pairs = sum(g.shape[0] for g in grads)
    cols = pairs * LANES
    many = len(grads)
    more = [] if other is None else [other, *outputs]
    quarter = width

    def kernel(scal_ref, *refs):
        place_ref = refs[0] if more else None
        no_ref, nt_ref, *refs = refs[1 if more else 0 :]
        outs, acc = refs[many + len(more) : -1], refs[-1]
        i = pl.program_id(0)
        term = dot(pick(1, no_ref, nt_ref), side_by_side(refs[:many]), TN)

        @pl.when(i == 0)
        def _():
            acc[...] = term

        def total(j, p):
            at = (3 * p + j) * LANES
            return (acc[:, at : at + LANES] + term[:, at : at + LANES]) * scal_ref[1]

        def store(half, keep, send):
            for p in range(pairs):
                lanes = slice(p * LANES, (p + 1) * LANES)
                for out_ref, j in ((keep, 2 * half), (send, 2 * half + 1)):
                    if j < 3:
                        final = total(j, p) + refs[many][j * width : (j + 1) * width, lanes].astype(f32)
                        out_ref[:, lanes] = final.astype(bf16)
                        continue
                    for k in range(width // cols):
                        at = slice(k * cols + p * LANES, k * cols + (p + 1) * LANES)
                        final = refs[many + 1][:, at].astype(f32) + refs[many + 2][:, at].astype(f32)
                        out_ref[k * cols : (k + 1) * cols, lanes] = final.astype(bf16)

        @pl.when(i == 1)
        def _():
            if not more:
                for p in range(pairs):
                    for j in range(3):
                        at = (slice(j * width, (j + 1) * width), slice(p * LANES, (p + 1) * LANES))
                        outs[0][at] = total(j, p).astype(bf16)
            for half in range(2 if more else 0):
                keep, send = outs[2 * half], outs[2 * half + 1]

                @pl.when(place_ref[half] == 0)
                def _():
                    store(half, keep, send)

                @pl.when(place_ref[half] == 1)
                def _():
                    store(half, send, keep)

    out = [shape((quarter, cols), bf16)] * 4 if more else [shape((3 * width, cols), bf16)]
    return call(
        kernel,
        "input_term",
        (2,),
        [scalars()]
        + [scalars()] * (1 if more else 0)
        + [*halves(rows, width, 1)]
        + pair_specs(grads, rows, lambda i: i)
        + [whole(m) for m in more],
        [whole(o) for o in out],
        out,
        [pltpu.VMEM((width, 3 * cols), f32)],
        flops=12 * rows * width * cols,
        nbytes=4 * rows * width + 12 * rows * cols + 12 * width * cols,
    )(scal, *([place] if more else []), norm_own, norm_other, *grads, *more)


def join_weights(refs, joined):
    @pl.when(pl.program_id(0) == 0)
    def _():
        place = 0
        for ref in refs:
            for p in range(ref.shape[2] // LANES):
                for j in range(3):
                    joined[:, place : place + LANES] = ref[j, :, p * LANES : (p + 1) * LANES]
                    place += LANES


def norm1_other(grads, weights):
    rows = grads[0].shape[1] // 2
    width, cols = weights[0].shape[1:]
    block = 512
    count = rows // block
    many = len(grads)

    def kernel(*refs):
        out_ref, joined = refs[-2:]
        join_weights(refs[many:-2], joined)
        out_ref[...] = dot(side_by_side(refs[:many]), joined[...], NT).astype(bf16)

    return call(
        kernel,
        "first_other",
        (count,),
        pair_specs(grads, block, lambda i: i + count) + [whole(w) for w in weights],
        pl.BlockSpec((block, width), lambda i: (i, 0)),
        shape((rows, width), bf16),
        [pltpu.VMEM((width, 3 * cols * len(weights)), bf16)],
        flops=12 * rows * width * cols,
        nbytes=12 * rows * cols + 2 * rows * width + 12 * width * cols,
    )(*grads, *weights)


def norm1_own(grads, weights, received, tokens, middle_grad, params, scal):
    rows, width = tokens.shape
    cols = weights[0].shape[2]
    block = 256
    last = rows // block - 1
    many = len(grads)

    def kernel(scal_ref, *refs):
        rec_ref, tok_ref, mid_ref, par_ref, out_ref, sum_ref, joined = refs[many + len(weights) :]
        i = pl.program_id(0)
        join_weights(refs[many : many + len(weights)], joined)
        grad = dot(side_by_side(refs[:many]), joined[...], NT) + rec_ref[...].astype(f32)
        unit, inverse = normalize(tok_ref[...].astype(f32))
        out = mid_ref[...] + norm_back(grad, par_ref[0:1, :], unit, inverse)
        out_ref[...] = out.astype(bf16)
        sums = [jnp.sum(v, axis=0, keepdims=True) for v in (grad * unit, grad)]
        add_rows(sum_ref, sums, i == 0, 0)

        @pl.when(i == last)
        def _():
            sum_ref[...] = sum_ref[...] * scal_ref[1]

    spec = pl.BlockSpec((block, width), lambda i: (i, 0))
    sums = shape((8, width), f32)
    return call(
        kernel,
        "first_own",
        (rows // block,),
        [scalars()]
        + pair_specs(grads, block, lambda i: i)
        + [whole(w) for w in weights]
        + [spec] * 3
        + [whole(params)],
        [spec, whole(sums)],
        [shape((rows, width), bf16), sums],
        [pltpu.VMEM((width, 3 * cols * len(weights)), bf16)],
        flops=12 * rows * width * cols,
        nbytes=12 * rows * cols + 10 * rows * width + 12 * width * cols,
    )(scal, *grads, *weights, received, tokens, middle_grad, params)


def down_specs(weights):
    return [
        pl.BlockSpec(
            (w.shape[0], None, *w.shape[2:]), lambda i, j=j: (0, j, 0, 0), pipeline_mode=pl.Buffered(1)
        )
        for w, j in weights
    ]


def down_product(acts, weights):
    total = None
    for a_ref, w_ref in zip(acts, weights, strict=True):
        part = dot(a_ref[...], w_ref[...].reshape(a_ref.shape[1], w_ref.shape[-1]))
        total = part if total is None else total + part
    return total


def result_other(acts, weights):
    rows, hidden = acts[0].shape
    rows = rows // 2
    width = weights[0][0].shape[-1]
    block = 512
    start = rows // block
    many = len(acts)

    def kernel(*refs):
        refs[-1][...] = down_product(refs[:many], refs[many:-1]).astype(bf16)

    return call(
        kernel,
        "result_other",
        (rows // block,),
        [pl.BlockSpec((block, hidden), lambda i: (i + start, 0))] * many + down_specs(weights),
        pl.BlockSpec((block, width), lambda i: (i, 0)),
        shape((rows, width), bf16),
        flops=2 * many * rows * hidden * width,
        nbytes=2 * many * rows * hidden,
    )(*acts, *[w for w, _ in weights])


def block_result(middle, acts, weights, received, params, scal):
    rows, width = middle.shape
    hidden = acts[0].shape[1]
    block = 256
    many = len(acts)

    def kernel(scal_ref, mid_ref, rec_ref, par_ref, *refs):
        total = mid_ref[...] + down_product(refs[:many], refs[many:-1])
        total = total + rec_ref[...].astype(f32) + par_ref[5:6, :]
        refs[-1][...] = (total * scal_ref[0]).astype(bf16)

    spec = pl.BlockSpec((block, width), lambda i: (i, 0))
    return call(
        kernel,
        "block_result",
        (rows // block,),
        [scalars(), spec, spec, whole(params)]
        + [pl.BlockSpec((block, hidden), lambda i: (i, 0))] * many
        + down_specs(weights),
        spec,
        shape((rows, width), bf16),
        flops=2 * many * rows * hidden * width,
        nbytes=12 * rows * width,
        weight=1000,
    )(scal, middle, received, params, *acts, *[w for w, _ in weights])


def add_terms(*terms):
    rows, width = terms[0].shape
    block = 256

    def kernel(*refs):
        total = refs[0][...].astype(f32)
        for ref in refs[1:-1]:
            total = total + ref[...].astype(f32)
        refs[-1][...] = total.astype(bf16)

    spec = pl.BlockSpec((block, width), lambda i: (i, 0))
    return call(
        kernel,
        "add_terms",
        (rows // block,),
        [spec] * len(terms),
        spec,
        shape((rows, width), bf16),
        flops=len(terms) * rows * width,
        nbytes=2 * (len(terms) + 1) * rows * width,
    )(*terms)


def body(
    tokens,
    out_grad,
    item_counts,
    group_dataset,
    variable_mask,
    first_gain,
    first_shift,
    input_weight,
    input_bias,
    output_weight,
    output_bias,
    second_gain,
    second_shift,
    up_weight,
    up_bias,
    down_weight,
    down_bias,
):
    shard_count = lax.axis_size("mp")
    groups = lax.axis_size("dp")
    rows, width = tokens.shape
    cols = input_weight.shape[2]
    hidden = up_weight.shape[1]

    def core_swap(value):
        return lax.ppermute(value, "mp", [(i, i ^ 1) for i in range(shard_count)])

    def chip_swap(value):
        return lax.ppermute(value, "mp", [(i, i ^ 2) for i in range(shard_count)])

    def after(value, *others):
        return lax.optimization_barrier((value, *others))[0]

    def along(value, bit):
        return lax.ppermute(value, "dp", [(i, i ^ bit) for i in range(groups)])

    group = lax.axis_index("dp")

    slice_rows = up_weight.shape[0] // groups
    slices = [
        lax.dynamic_slice_in_dim(weight, group * slice_rows, slice_rows, 0)
        for weight in (up_weight, down_weight)
    ]
    slice_two = chip_swap(jnp.stack(slices)[None])
    bias_pack = jnp.concatenate([up_bias, input_bias[0], input_bias[1]]).reshape(-1, LANES)
    bias_two = chip_swap(bias_pack)
    wi_two = chip_swap(after(input_weight, *slices))
    cot_t = core_swap(out_grad)
    normed1 = first_norm(tokens, first_gain, first_shift)
    normed1_t = core_swap(normed1)
    item_counts, variable_mask, output_bias = after(
        (item_counts, variable_mask, output_bias), normed1
    )

    live = (lax.axis_index("mp") // 2 < item_counts[0]).astype(f32)
    dataset_hit = jnp.arange(variable_mask.shape[0], dtype=jnp.int32) == group_dataset[0]
    own_units = (
        item_counts[0] * jnp.sum(jnp.where(dataset_hit[:, None], variable_mask, 0))
    ).astype(f32)
    scal = jnp.stack([live, own_units, (group % 2).astype(f32)])
    zero = jnp.zeros((width,), f32)
    params = jnp.stack(
        [first_gain, first_shift, output_bias, second_gain, second_shift, down_bias, zero, zero]
    )

    qkv_one = project(normed1, input_weight, input_bias)
    wo_two = chip_swap(after(output_weight, qkv_one[0]))
    ff_weights_two = lax.all_gather(after(slice_two, qkv_one[0]), "dp", axis=0, tiled=True)
    qkv_one = project(normed1_t, input_weight, after(input_bias, qkv_one[0]), qkv_one)
    att_one, att_one_send, turned_one, stat_one = attend_forward(*qkv_one)
    att_one_t = core_swap(att_one_send)
    wo_one_t = core_swap(output_weight)
    bias_two = after(bias_two, att_one).reshape(-1)
    up_bias_one = up_bias.reshape(1, hidden)
    up_bias_two = bias_two[:hidden].reshape(1, hidden)
    in_bias_two = bias_two[hidden:].reshape(2, cols)
    qkv_two = project_both(
        after(normed1, att_one), normed1_t, wi_two, after(in_bias_two, up_bias_two)
    )
    qkv_two = after(tuple(qkv_two), att_one_t)
    att_two, att_two_send, turned_two, stat_two = attend_forward(*qkv_two)
    wo_two_t = core_swap(after(wo_two, att_two))
    att_two_t = core_swap(att_two_send)
    middle, normed2 = output_own(
        tokens,
        [att_one, att_two, att_one_t, att_two_t],
        [output_weight, wo_two, wo_one_t, wo_two_t],
        params,
    )
    normed2_t = core_swap(normed2)

    act_two, ng_two, keep_two, send_two, up_sum_two = feed_forward(
        normed2, normed2_t, out_grad, cot_t, up_bias_two, (ff_weights_two, 0), (ff_weights_two, 1), scal
    )
    two_received = along(send_two, 1)
    up_one, down_one = ((w.reshape(1, 1, -1, width), 0) for w in (up_weight, down_weight))
    act_one, ng_own, *ng_sends, keep_one, send_one, up_sum_one = feed_forward(
        normed2, normed2_t, out_grad, cot_t, up_bias_one, up_one, down_one, scal, ng_two
    )
    one_received = along(send_one, 1)
    ng_received = [core_swap(ng_send) for ng_send in ng_sends]
    middle_grad, middle_low, second_sums = second_back(
        middle, ng_own, ng_received, out_grad, params, scal
    )
    pair_two = add_terms(keep_two, after(two_received, middle_low))
    pair_received = chip_swap(pair_two)
    middle_low_t = core_swap(middle_low)
    middle_low = after(middle_low, pair_two)
    out_weights = [output_weight, wo_two]
    g_one, g_two, *wo_terms = output_back(
        middle_low, [att_one, att_two], out_weights, scal
    )
    g_one_t, g_two_t, wo_one_term, wo_two_term = output_back(
        middle_low_t, [att_one_send, att_two_send], out_weights, scal, wo_terms
    )

    def both(own, received, *last):
        return (own.astype(f32) + after(received, *last).astype(f32)).astype(bf16)

    back_two = [attend_backward(*qkv_two, g_two, g_two_t, turned_two, stat_two, 0, 1)]
    wait = back_two[0][0]
    acts = [act_two, act_one]
    downs = [(ff_weights_two, 1), down_one]
    result_send = result_other([after(act_two, wait), act_one], downs)
    result_received = core_swap(result_send)
    ff_both = add_terms(keep_one, one_received, after(pair_received, wait, result_send))
    ff_sum = lax.psum(
        ff_both, "dp", axis_index_groups=[list(range(k, groups, 2)) for k in range(2)]
    )
    back_two.append(
        attend_backward(
            *qkv_two, after(g_two, ff_both), g_two_t, turned_two, stat_two, 1, cols // LANES - 1
        )
    )
    grads_two = [back[0] for back in back_two]
    wi_two_term = input_term(normed1, normed1_t, grads_two, scal)[0]
    wo_received = chip_swap(after(wo_two_term, grads_two[1]))
    wi_received = chip_swap(wi_two_term)
    g_one = after(g_one, wi_two_term)
    back_one = [attend_backward(*qkv_one, g_one, g_one_t, turned_one, stat_one, 0, cols // LANES)]
    grads_one = [back[0] for back in back_one]

    bits = [1 << k for k in range(groups.bit_length() - 1)]
    orders = [bits, bits[1:2] + bits[:1] + bits[2:]]

    def upper(bit):
        return (group // bit) % 2

    def split(part, bit):
        half = part.shape[0] // 2
        return (
            lax.dynamic_slice_in_dim(part, upper(bit) * half, half, 0),
            lax.dynamic_slice_in_dim(part, (1 - upper(bit)) * half, half, 0),
        )

    place = jnp.stack([upper(order[0]) for order in orders]).astype(jnp.int32)
    keep_a, send_a, keep_b, send_b = input_term(
        normed1, normed1_t, grads_one, scal, wi_received, (wo_one_term, wo_received), place
    )
    keeps, sends = (keep_a, keep_b), (send_a, send_b)
    received = [along(sends[k], orders[k][0]) for k in range(2)]

    grads = grads_one + grads_two
    weights = [input_weight, wi_two]
    ng1_received = core_swap(norm1_other(grads, [input_weight, after(wi_two, *sends)]))
    parts = [both(keeps[k], received[k]) for k in range(2)]
    last = len(bits) - 1
    for turn in range(1, last + 1):
        keeps, sends = zip(*[split(parts[k], orders[k][turn]) for k in range(2)], strict=True)
        received = [along(sends[k], orders[k][turn]) for k in range(2)]
        wait = []
        if turn == 1:
            ff_sum_other = along(after(ff_sum, *sends), 1)
            result = block_result(
                after(middle, *sends), acts, downs, result_received, params, scal
            )
            wait = [result]
        if turn == last:
            token_grad, first_sums = norm1_own(
                grads, weights, ng1_received, after(tokens, *sends), middle_grad, params, scal
            )
            wait = [token_grad]
        parts = [both(keeps[k], received[k], *wait) for k in range(2)]
    first_sums = after(first_sums, *parts)
    for turn in reversed(range(len(bits))):
        if turn == min(1, last):
            parts[1] = after(parts[1], ff_sum_other)
        received = [along(parts[k], orders[k][turn]) for k in range(2)]
        last_parts = list(parts)
        ahead = last_parts if turn >= last - 1 else ahead
        for k in range(2):
            is_upper = upper(orders[k][turn]) == 1
            parts[k] = jnp.concatenate(
                [jnp.where(is_upper, received[k], parts[k]), jnp.where(is_upper, parts[k], received[k])]
            )
    wi_rows = 3 * width
    tail_sum = jnp.concatenate(parts)
    wi_sum = tail_sum[:wi_rows].reshape(3, width, cols)
    wo_sum = tail_sum[wi_rows:].reshape(width // cols, cols, cols)
    wo_sum = jnp.concatenate([wo_sum[k] for k in range(width // cols)], 1)

    lower = group % 2 == 0
    up_sum = jnp.where(lower, ff_sum, ff_sum_other)
    down_sum = jnp.where(lower, ff_sum_other, ff_sum)

    def quarter_rows(parts, up_sums):
        sums_all = jnp.concatenate([part[1] for part in parts], 1)
        rest = jnp.full((1, width - 2 * cols), own_units)
        bias_row = jnp.concatenate([sums_all[0:1] * own_units, sums_all[1:2] * own_units, rest], 1)
        return up_sums + jnp.pad(bias_row, ((6, 1), (0, 0)))

    late = first_sums + second_sums
    late = late + core_swap(late)
    late_one = late + quarter_rows(back_one, up_sum_one)
    late = late_one + chip_swap(late + quarter_rows(back_two, up_sum_two))
    for bit in bits[1:] + bits[:1]:
        late = after(late, *(ahead if bit > 1 else last_parts))
        late = late + along(late, bit)
    share = 2.0 / late[6, -1]
    late = late * share

    return (
        result,
        token_grad,
        late[0],
        late[1],
        wi_sum.astype(f32) * share,
        late[6, : 2 * cols].reshape(2, cols),
        wo_sum.astype(f32) * share,
        late[4],
        late[2],
        late[3],
        up_sum.astype(f32) * share,
        late[7],
        down_sum.astype(f32) * share,
        late[5],
    )


def solution(mesh):
    in_specs = (
        P(("dp", "mp"), None),
        P(("dp", "mp"), None),
        P("dp"),
        P("dp"),
        P(),
        P(),
        P(),
        P(None, None, "mp"),
        P(None, "mp"),
        P("mp", None),
        P(),
        P(),
        P(),
        P(None, "mp"),
        P("mp"),
        P("mp", None),
        P(),
    )
    out_specs = (
        P(("dp", "mp"), None),
        P(("dp", "mp"), None),
        P(),
        P(),
        P(None, None, "mp"),
        P(None, "mp"),
        P("mp", None),
        P(),
        P(),
        P(),
        P(None, "mp"),
        P("mp"),
        P("mp", None),
        P(),
    )
    return jax.shard_map(body, mesh=mesh, in_specs=in_specs, out_specs=out_specs, check_vma=False)
```

```python
import jax
import jax.numpy as jnp
from jax import lax
from jax.experimental import pallas as pl
from jax.experimental.pallas import tpu as pltpu
from jax.sharding import PartitionSpec as P

HEAD_DIM = 64
LANES = 128
norm_eps = 1e-06
SCALE = HEAD_DIM**-0.5
LOG2E = 1.4426950408889634
RSQRT2 = 0.7071067811865476
RSQRT2PI = 0.3989422804014327

bf16 = jnp.bfloat16
f32 = jnp.float32
NN = (((1,), (0,)), ((), ()))
NT = (((1,), (1,)), ((), ()))
TN = (((0,), (0,)), ((), ()))
VMEM_BYTES = 60 << 20


def dot(left, right, dims=NN):
    return lax.dot_general(left, right, dims, preferred_element_type=f32)


def shape(dims, dtype):
    return jax.ShapeDtypeStruct(dims, dtype)


def whole(array):
    rank = len(array.shape)
    return pl.BlockSpec(array.shape, lambda *_: (0,) * rank, pipeline_mode=pl.Buffered(1))


def scalars():
    return pl.BlockSpec(memory_space=pltpu.SMEM)


def call(kernel, name, grid, in_specs, out_specs, out_shape, scratch=(), flops=0, nbytes=0, exps=0, weight=1e-6, aliases=None):
    return pl.pallas_call(
        kernel,
        name=name,
        grid=grid,
        in_specs=in_specs,
        out_specs=out_specs,
        out_shape=out_shape,
        scratch_shapes=list(scratch),
        input_output_aliases=aliases or {},
        compiler_params=pltpu.CompilerParams(vmem_limit_bytes=VMEM_BYTES),
        cost_estimate=pl.CostEstimate(
            flops=int(flops * weight), bytes_accessed=int(nbytes * weight), transcendentals=int(exps * weight)
        ),
    )


def split_two(values):
    high = values.astype(bf16)
    return high, (values - high.astype(f32)).astype(bf16)


def split_three(values):
    high = values.astype(bf16)
    rest = values - high.astype(f32)
    mid = rest.astype(bf16)
    return high, mid, (rest - mid.astype(f32)).astype(bf16)


def stat_rows(vector, rows):
    high, mid, rest = (part.astype(f32) for part in split_three(vector))
    row = lax.broadcasted_iota(jnp.int32, (rows, vector.shape[1]), 0)
    return jnp.where(
        row == 0, high, jnp.where(row == 1, mid, jnp.where(row == 2, rest, 0.0))
    ).astype(bf16)


def normalize(values):
    centered = values - jnp.mean(values, axis=-1, keepdims=True)
    variance = jnp.mean(centered * centered, axis=-1, keepdims=True)
    inverse = lax.rsqrt(variance + norm_eps)
    return centered * inverse, inverse


def norm_back(grad, gain, unit, inverse):
    scaled = grad * gain
    return inverse * (
        scaled
        - jnp.mean(scaled, axis=-1, keepdims=True)
        - unit * jnp.mean(scaled * unit, axis=-1, keepdims=True)
    )


def add_rows(ref, rows, first, start):
    @pl.when(first)
    def _():
        ref[...] = jnp.zeros_like(ref)

    for place, row in enumerate(rows):
        ref[start + place : start + place + 1, :] += row


def first_norm(tokens, gain, shift):
    rows, width = tokens.shape
    block = 256

    def kernel(tok_ref, gain_ref, shift_ref, norm_ref):
        unit, _ = normalize(tok_ref[...].astype(f32))
        gain_row = gain_ref[...].reshape(1, width)
        norm_ref[...] = (unit * gain_row + shift_ref[...].reshape(1, width)).astype(bf16)

    spec = pl.BlockSpec((block, width), lambda i: (i, 0))
    return call(
        kernel,
        "first_norm",
        (rows // block,),
        [spec, whole(gain), whole(shift)],
        spec,
        shape((rows, width), bf16),
        flops=20 * rows * width,
        nbytes=4 * rows * width,
    )(tokens, gain, shift)


def halves(block, width, count):
    own = pl.BlockSpec((block, width), lambda i, *_: (jnp.minimum(i, count - 1), 0))
    other = pl.BlockSpec((block, width), lambda i, *_: (jnp.maximum(i - count, 0), 0))
    return own, other


def pick(count, own_ref, other_ref):
    return jnp.where(pl.program_id(0) < count, own_ref[...], other_ref[...])


def project(norm, weight, bias, earlier=None):
    rows, width = norm.shape
    cols = weight.shape[2]
    block = 512
    start = 0 if earlier is None else rows // block
    skip = 0 if earlier is None else 3

    def kernel(x_ref, w_ref, b_ref, *refs):
        q_ref, k_ref, v_ref = refs[skip:]
        x = x_ref[...]
        q_ref[...] = (dot(x, w_ref[0]) + b_ref[0:1, :]).astype(bf16)
        k_ref[...] = dot(x, w_ref[1]).astype(bf16)
        v_ref[...] = (dot(x, w_ref[2]) + b_ref[1:2, :]).astype(bf16)

    out = pl.BlockSpec((block, cols), lambda i: (i + start, 0))
    return call(
        kernel,
        "project",
        (rows // block,),
        [pl.BlockSpec((block, width), lambda i: (i, 0)), whole(weight), whole(bias)]
        + [pl.BlockSpec(memory_space=pl.ANY)] * skip,
        [out] * 3,
        [shape((2 * rows, cols), bf16)] * 3,
        flops=6 * rows * width * cols,
        nbytes=2 * rows * width + 6 * width * cols + 6 * rows * cols,
        weight=1000,
        aliases={3 + k: k for k in range(skip)},
    )(norm, weight, bias, *(earlier or ()))


def project_both(norm_own, norm_other, weight, bias):
    rows, width = norm_own.shape
    cols = weight.shape[2]
    block = 512
    count = rows // block

    def kernel(own_ref, other_ref, w_ref, b_ref, q_ref, k_ref, v_ref):
        x = pick(count, own_ref, other_ref)
        q_ref[...] = (dot(x, w_ref[0]) + b_ref[0:1, :]).astype(bf16)
        k_ref[...] = dot(x, w_ref[1]).astype(bf16)
        v_ref[...] = (dot(x, w_ref[2]) + b_ref[1:2, :]).astype(bf16)

    out = pl.BlockSpec((block, cols), lambda i: (i, 0))
    return call(
        kernel,
        "project_both",
        (2 * count,),
        [*halves(block, width, count), whole(weight), whole(bias)],
        [out] * 3,
        [shape((2 * rows, cols), bf16)] * 3,
        flops=12 * rows * width * cols,
        nbytes=4 * rows * width + 6 * width * cols + 12 * rows * cols,
        weight=1000,
    )(norm_own, norm_other, weight, bias)


def attend_forward(queries, keys, values):
    rows, width = queries.shape
    chunk = min(512, rows)

    def kernel(q_ref, k_ref, v_ref, own_ref, other_ref, ot_ref, lse_ref):
        k = k_ref[...]
        lane = lax.broadcasted_iota(jnp.int32, k.shape, 1)
        rolled = pltpu.roll(k.astype(f32), HEAD_DIM, 1).astype(bf16)
        turned = v_ref[...].astype(f32).T
        ones = jnp.ones((HEAD_DIM, rows), bf16)
        q_turned = q_ref[...].astype(f32).T * (SCALE * LOG2E)
        outs = []
        for head in range(2):
            at = head * HEAD_DIM
            k_two = jnp.where(lane < HEAD_DIM, k, rolled) if head == 0 else jnp.where(lane < HEAD_DIM, rolled, k)
            own = turned[at : at + HEAD_DIM].astype(bf16)
            v_turned = jnp.concatenate([own, ones] if head == 0 else [ones, own], 0)
            q_two = jnp.concatenate(split_two(q_turned[at : at + HEAD_DIM]), 0)
            total = peak = None
            for j in range(rows // chunk):
                part = slice(j * chunk, (j + 1) * chunk)
                scores = dot(k_two[part], q_two)
                top = jnp.max(scores.reshape(chunk // 8, 8, rows).max(axis=0), axis=0, keepdims=True)
                higher = top if peak is None else jnp.maximum(peak, top)
                weights = jnp.exp2(scores - higher).astype(bf16)
                add = dot(v_turned[:, part], weights)
                total = add if total is None else total * jnp.exp2(peak - higher) + add
                peak = higher
            row_sum = total[HEAD_DIM - at : HEAD_DIM - at + 1]
            outs.append(total[at : at + HEAD_DIM] / row_sum)
            lse_ref[head : head + 1, :] = peak + jnp.log2(row_sum)
        attended = jnp.concatenate(outs, 0)
        ot_ref[...] = attended
        own_ref[...] = attended[:, : rows // 2].T.astype(bf16)
        other_ref[...] = attended[:, rows // 2 :].T.astype(bf16)

    by_pair = pl.BlockSpec((rows, LANES), lambda j: (0, j))
    by_half = pl.BlockSpec((rows // 2, LANES), lambda j: (0, j))
    pairs = width // LANES
    return call(
        kernel,
        "attend_forward",
        (pairs,),
        [by_pair] * 3,
        [
            by_half,
            by_half,
            pl.BlockSpec((LANES, rows), lambda j: (j, 0)),
            pl.BlockSpec((None, 8, rows), lambda j: (j, 0, 0)),
        ],
        [shape((rows // 2, width), bf16)] * 2
        + [shape((width, rows), f32), shape((pairs, 8, rows), f32)],
        flops=16 * rows * rows * width,
        nbytes=12 * rows * width,
        exps=rows * rows * width // HEAD_DIM,
        weight=1000,
    )(queries, keys, values)


def attend_backward(queries, keys, values, grad_own, grad_other, out_turned, stats, first, pairs):
    rows = queries.shape[0]
    width = LANES * pairs
    block = grad_own.shape[0]
    chunk = 256
    count = rows // block

    def kernel(
        q_ref, k_ref, v_ref, go_ref, gt_ref, ot_ref, lse_ref, d_ref, sum_ref,
        k_wide, k_turned, v_wide, dk_acc, dv_acc,
    ):
        i = pl.program_id(1)

        @pl.when(i == 0)
        def _():
            k = k_ref[...]
            v = v_ref[...]
            lane = lax.broadcasted_iota(jnp.int32, k.shape, 1)
            k_rolled = pltpu.roll(k.astype(f32), HEAD_DIM, 1).astype(bf16)
            v_rolled = pltpu.roll(v.astype(f32), HEAD_DIM, 1).astype(bf16)
            ones = jnp.where(lane < 3, 1.0, 0.0).astype(bf16)
            k_wide[0] = jnp.concatenate([jnp.where(lane < HEAD_DIM, k, k_rolled), ones], 1)
            k_wide[1] = jnp.concatenate([jnp.where(lane < HEAD_DIM, k_rolled, k), ones], 1)
            tail = jnp.where(lane < HEAD_DIM + 3, 1.0, 0.0).astype(bf16)
            v_wide[0] = jnp.where(lane < HEAD_DIM, v, tail)
            v_wide[1] = jnp.where(lane < HEAD_DIM, v_rolled, tail)
            k_turned[...] = k.astype(f32).T.astype(bf16)
            dk_acc[...] = jnp.zeros_like(dk_acc)
            dv_acc[...] = jnp.zeros_like(dv_acc)
            sum_ref[...] = jnp.zeros_like(sum_ref)

        q_turned = q_ref[...].astype(f32).T
        q_low = q_turned.astype(bf16)
        q_turned = q_turned * (SCALE * LOG2E)
        g_turned = jnp.where(i == 0, go_ref[...], gt_ref[...]).astype(f32).T
        g_low = g_turned.astype(bf16)
        dqs = []
        for head in range(2):
            part = slice(head * HEAD_DIM, (head + 1) * HEAD_DIM)
            q_wide = jnp.concatenate(
                [*split_two(q_turned[part]), stat_rows(-lse_ref[head : head + 1, :], LANES)], 0
            )
            row_dot = jnp.sum(g_turned[part] * ot_ref[part, :], axis=0, keepdims=True)
            g_wide = jnp.concatenate([g_low[part], stat_rows(-row_dot, HEAD_DIM)], 0)
            dq = None
            for j in range(rows // chunk):
                at = pl.ds(j * chunk, chunk)
                probabilities = jnp.exp2(dot(k_wide[head, at, :], q_wide))
                shifted = dot(v_wide[head, at, :], g_wide)
                probs_low = probabilities.astype(bf16)
                score_grad = (probabilities * shifted).astype(bf16)
                dv_acc[part, at] += dot(g_low[part], probs_low, NT)
                dk_acc[part, at] += dot(q_low[part], score_grad, NT)
                add = dot(k_turned[part, at], score_grad)
                dq = add if dq is None else dq + add
            dqs.append(dq)
        dq = (jnp.concatenate(dqs, 0) * SCALE).T
        d_ref[pl.ds(i * block, block), :LANES] = dq.astype(bf16)
        sum_ref[0:1, :] += jnp.sum(dq, axis=0, keepdims=True)

        @pl.when(i == count - 1)
        def _():
            d_ref[:, LANES : 2 * LANES] = (dk_acc[...] * SCALE).T.astype(bf16)
            dv = dv_acc[...].T
            d_ref[:, 2 * LANES :] = dv.astype(bf16)
            sum_ref[1:2, :] = jnp.sum(dv, axis=0, keepdims=True)

    by_query = pl.BlockSpec((block, LANES), lambda j, i: (i, j + first))
    by_key = pl.BlockSpec((rows, LANES), lambda j, i: (0, j + first))
    half = pl.BlockSpec((block, LANES), lambda j, i: (0, j + first))
    turned_spec = pl.BlockSpec((LANES, block), lambda j, i: (j + first, i))
    stat_spec = pl.BlockSpec((None, 8, block), lambda j, i: (j + first, 0, i))
    out_spec = pl.BlockSpec((None, rows, 3 * LANES), lambda j, i: (j, 0, 0))
    sum_spec = pl.BlockSpec((8, LANES), lambda j, i: (0, j))
    return call(
        kernel,
        "attend_backward",
        (pairs, count),
        [by_query, by_key, by_key, half, half, turned_spec, stat_spec],
        [out_spec, sum_spec],
        [shape((pairs, rows, 3 * LANES), bf16), shape((8, width), f32)],
        [
            pltpu.VMEM((2, rows, 2 * LANES), bf16),
            pltpu.VMEM((LANES, rows), bf16),
            pltpu.VMEM((2, rows, LANES), bf16),
            pltpu.VMEM((LANES, rows), f32),
            pltpu.VMEM((LANES, rows), f32),
        ],
        flops=40 * rows * rows * width,
        nbytes=20 * rows * width,
        exps=rows * rows * width // HEAD_DIM,
        weight=1000,
    )(queries, keys, values, grad_own, grad_other, out_turned, stats)


def output_own(tokens, attended, weights, params):
    rows, width = tokens.shape
    cols = weights[0].shape[0]
    block = 256
    many = len(attended)

    def kernel(t_ref, par_ref, *refs):
        total = None
        for a_ref, w_ref in zip(refs[:many], refs[many : 2 * many], strict=True):
            part = dot(a_ref[...], w_ref[...])
            total = part if total is None else total + part
        mid_ref, norm_ref = refs[2 * many :]
        middle = t_ref[...].astype(f32) + total + par_ref[2:3, :]
        mid_ref[...] = middle
        unit, _ = normalize(middle)
        norm_ref[...] = (unit * par_ref[3:4, :] + par_ref[4:5, :]).astype(bf16)

    spec = pl.BlockSpec((block, width), lambda i: (i, 0))
    thin = pl.BlockSpec((block, cols), lambda i: (i, 0))
    return call(
        kernel,
        "output_own",
        (rows // block,),
        [spec, whole(params)] + [thin] * many + [whole(w) for w in weights],
        [spec, spec],
        [shape((rows, width), f32), shape((rows, width), bf16)],
        flops=2 * rows * many * cols * width,
        nbytes=2 * rows * many * cols + 8 * rows * width,
    )(tokens, params, *attended, *weights)


def feed_forward(norm_own, norm_other, cot_own, cot_other, bias, up, down, scal, earlier=None):
    rows, width = norm_own.shape
    hidden = bias.shape[1]
    block = 512
    count = rows // block
    last = earlier is not None
    (up, up_place), (down, down_place) = up, down
    slices, depth = up.shape[0], up.shape[2]
    def kernel(scal_ref, no_ref, nt_ref, co_ref, ct_ref, b_ref, up_ref, dn_ref, *refs):
        if last:
            ng_in, act_ref, ngo_ref, nga_ref, ngb_ref, *refs = refs
        else:
            act_ref, ng_ref, *refs = refs
        keep, send, sum_ref, up_acc, down_acc = refs
        i = pl.program_id(0)

        @pl.when(i == 0)
        def _():
            up_acc[...] = jnp.zeros_like(up_acc)
            down_acc[...] = jnp.zeros_like(down_acc)
            sum_ref[...] = jnp.zeros_like(sum_ref)

        x = pick(count, no_ref, nt_ref)
        cot = (pick(count, co_ref, ct_ref).astype(f32) * scal_ref[0]).astype(bf16)
        up_now = up_ref[...].reshape(width, hidden)
        down_now = dn_ref[...].reshape(hidden, width)
        h = dot(x, up_now) + b_ref[0:1, :]
        cdf = 0.5 * (1.0 + lax.erf(h * RSQRT2))
        act = (h * cdf).astype(bf16)
        slope = cdf + h * (RSQRT2PI * jnp.exp(-0.5 * h * h))
        act_ref[...] = act
        grad = dot(cot, down_now, NT) * slope
        sum_ref[7:8, :] += jnp.sum(grad, axis=0, keepdims=True)
        low = grad.astype(bf16)
        ng = dot(low, up_now, NT)
        up_acc[...] += dot(x, low, TN)
        down_acc[...] += dot(act, cot, TN)
        if last:
            ng = ng + ng_in[...].astype(f32)

            @pl.when(i < count)
            def _():
                ngo_ref[...] = ng

            @pl.when((i >= count) & (i < count + count // 2))
            def _():
                nga_ref[...] = ng.astype(bf16)

            @pl.when(i >= count + count // 2)
            def _():
                ngb_ref[...] = ng.astype(bf16)
        else:
            ng_ref[...] = ng.astype(bf16)

        @pl.when(i == 2 * count - 1)
        def _():
            units = scal_ref[1]

            @pl.when(scal_ref[2] < 0.5)
            def _():
                keep[...] = (up_acc[...] * units).astype(bf16)
                send[...] = (down_acc[...] * units).astype(bf16)

            @pl.when(scal_ref[2] > 0.5)
            def _():
                keep[...] = (down_acc[...] * units).astype(bf16)
                send[...] = (up_acc[...] * units).astype(bf16)

            sum_ref[...] = sum_ref[...] * units

    own, other = halves(block, width, count)
    every = pl.BlockSpec((block, width), lambda i: (i, 0))
    up_spec, down_spec = (
        pl.BlockSpec(
            (slices, None, depth, width), lambda i, j=j: (0, j, 0, 0), pipeline_mode=pl.Buffered(1)
        )
        for j in (up_place, down_place)
    )
    ins = [scalars(), own, other, own, other, whole(bias), up_spec, down_spec]
    args = [scal, norm_own, norm_other, cot_own, cot_other, bias, up, down]
    outs = [every]
    shapes = [shape((2 * rows, hidden), bf16)]
    if last:
        ins += [every]
        args += [earlier]
        half = count // 2
        top = pl.BlockSpec((block, width), lambda i: (jnp.clip(i - count, 0, half - 1), 0))
        low = pl.BlockSpec((block, width), lambda i: (jnp.maximum(i - count - half, 0), 0))
        outs += [own, top, low]
        shapes += [shape((rows, width), f32)] + [shape((rows // 2, width), bf16)] * 2
    else:
        outs += [every]
        shapes += [shape((2 * rows, width), bf16)]
    assert width == hidden
    terms = [shape((width, hidden), bf16)] * 2
    sums = shape((8, hidden), f32)
    return call(
        kernel,
        "feed_forward",
        (2 * count,),
        ins,
        outs + [whole(terms[0]), whole(terms[1]), whole(sums)],
        shapes + terms + [sums],
        [pltpu.VMEM((width, hidden), f32), pltpu.VMEM((hidden, width), f32)],
        flops=20 * rows * width * hidden,
        nbytes=24 * rows * width + 12 * width * hidden,
        exps=4 * rows * hidden,
        weight=1000 if last else 1e-6,
    )(*args)


def second_back(middle, grad_own, grad_received, cot, params, scal):
    rows, width = middle.shape
    block = 256
    half = rows // block // 2
    last = rows // block - 1

    def kernel(scal_ref, mid_ref, go_ref, ga_ref, gb_ref, cot_ref, par_ref, out_ref, low_ref, sum_ref):
        i = pl.program_id(0)
        unit, inverse = normalize(mid_ref[...])
        grad = go_ref[...] + pick(half, ga_ref, gb_ref).astype(f32)
        cot = cot_ref[...].astype(f32) * scal_ref[0]
        out = cot + norm_back(grad, par_ref[3:4, :], unit, inverse)
        out_ref[...] = out
        low_ref[...] = out.astype(bf16)
        sums = [jnp.sum(v, axis=0, keepdims=True) for v in (grad * unit, grad, out, cot)]
        add_rows(sum_ref, sums, i == 0, 2)

        @pl.when(i == last)
        def _():
            sum_ref[...] = sum_ref[...] * scal_ref[1]

    spec = pl.BlockSpec((block, width), lambda i: (i, 0))
    sums = shape((8, width), f32)
    return call(
        kernel,
        "second_back",
        (rows // block,),
        [scalars(), spec, spec, *halves(block, width, half), spec, whole(params)],
        [spec, spec, whole(sums)],
        [shape((rows, width), f32), shape((rows, width), bf16), sums],
        flops=30 * rows * width,
        nbytes=18 * rows * width,
    )(scal, middle, grad_own, *grad_received, cot, params)


def output_back(low, attended, weights, scal, earlier=None):
    rows, width = low.shape
    cols = weights[0].shape[0]
    block = 512
    last = earlier is not None

    def kernel(scal_ref, low_ref, a_ref, b_ref, wa_ref, wb_ref, *refs):
        before = refs[:2] if last else (None, None)
        ga_ref, gb_ref, ta_ref, tb_ref, acc_a, acc_b = refs[2 if last else 0 :]
        i = pl.program_id(0)
        now = low_ref[...]
        ga_ref[...] = dot(now, wa_ref[...], NT).astype(bf16)
        gb_ref[...] = dot(now, wb_ref[...], NT).astype(bf16)
        for acc, rows_ref, old in ((acc_a, a_ref, before[0]), (acc_b, b_ref, before[1])):

            @pl.when(i == 0)
            def _():
                acc[...] = jnp.zeros_like(acc) if old is None else old[...]

            acc[...] += dot(rows_ref[...], now, TN)

        @pl.when(i == rows // block - 1)
        def _():
            factor = scal_ref[1] if last else 1.0
            ta_ref[...] = (acc_a[...] * factor).astype(ta_ref.dtype)
            tb_ref[...] = (acc_b[...] * factor).astype(tb_ref.dtype)

    thin = pl.BlockSpec((block, cols), lambda i: (i, 0))
    terms = [shape((cols, width), bf16 if last else f32)] * 2
    before = list(earlier or ())
    return call(
        kernel,
        "output_back",
        (rows // block,),
        [scalars(), pl.BlockSpec((block, width), lambda i: (i, 0)), thin, thin]
        + [whole(w) for w in weights]
        + [whole(t) for t in before],
        [thin, thin, whole(terms[0]), whole(terms[1])],
        [shape((rows, cols), bf16)] * 2 + terms,
        [pltpu.VMEM((cols, width), f32)] * 2,
        flops=8 * rows * width * cols,
        nbytes=2 * rows * width + 8 * rows * cols,
        weight=1e-6 if last else 1000,
    )(scal, low, *attended, *weights, *before)


def side_by_side(refs):
    return jnp.concatenate([ref[p] for ref in refs for p in range(ref.shape[0])], 1)


def pair_specs(grads, block, place):
    return [
        pl.BlockSpec((g.shape[0], block, g.shape[2]), lambda i: (0, place(i), 0)) for g in grads
    ]


def input_term(norm_own, norm_other, grads, scal, other=None, outputs=(), place=None):
    rows, width = norm_own.shape
    pairs = sum(g.shape[0] for g in grads)
    cols = pairs * LANES
    many = len(grads)
    more = [] if other is None else [other, *outputs]
    quarter = width

    def kernel(scal_ref, *refs):
        place_ref = refs[0] if more else None
        no_ref, nt_ref, *refs = refs[1 if more else 0 :]
        outs, acc = refs[many + len(more) : -1], refs[-1]
        i = pl.program_id(0)
        term = dot(pick(1, no_ref, nt_ref), side_by_side(refs[:many]), TN)

        @pl.when(i == 0)
        def _():
            acc[...] = term

        def total(j, p):
            at = (3 * p + j) * LANES
            return (acc[:, at : at + LANES] + term[:, at : at + LANES]) * scal_ref[1]

        def store(half, keep, send):
            for p in range(pairs):
                lanes = slice(p * LANES, (p + 1) * LANES)
                for out_ref, j in ((keep, 2 * half), (send, 2 * half + 1)):
                    if j < 3:
                        final = total(j, p) + refs[many][j * width : (j + 1) * width, lanes].astype(f32)
                        out_ref[:, lanes] = final.astype(bf16)
                        continue
                    for k in range(width // cols):
                        at = slice(k * cols + p * LANES, k * cols + (p + 1) * LANES)
                        final = refs[many + 1][:, at].astype(f32) + refs[many + 2][:, at].astype(f32)
                        out_ref[k * cols : (k + 1) * cols, lanes] = final.astype(bf16)

        @pl.when(i == 1)
        def _():
            if not more:
                for p in range(pairs):
                    for j in range(3):
                        at = (slice(j * width, (j + 1) * width), slice(p * LANES, (p + 1) * LANES))
                        outs[0][at] = total(j, p).astype(bf16)
            for half in range(2 if more else 0):
                keep, send = outs[2 * half], outs[2 * half + 1]

                @pl.when(place_ref[half] == 0)
                def _():
                    store(half, keep, send)

                @pl.when(place_ref[half] == 1)
                def _():
                    store(half, send, keep)

    out = [shape((quarter, cols), bf16)] * 4 if more else [shape((3 * width, cols), bf16)]
    return call(
        kernel,
        "input_term",
        (2,),
        [scalars()]
        + [scalars()] * (1 if more else 0)
        + [*halves(rows, width, 1)]
        + pair_specs(grads, rows, lambda i: i)
        + [whole(m) for m in more],
        [whole(o) for o in out],
        out,
        [pltpu.VMEM((width, 3 * cols), f32)],
        flops=12 * rows * width * cols,
        nbytes=4 * rows * width + 12 * rows * cols + 12 * width * cols,
    )(scal, *([place] if more else []), norm_own, norm_other, *grads, *more)


def join_weights(refs, joined):
    @pl.when(pl.program_id(0) == 0)
    def _():
        place = 0
        for ref in refs:
            for p in range(ref.shape[2] // LANES):
                for j in range(3):
                    joined[:, place : place + LANES] = ref[j, :, p * LANES : (p + 1) * LANES]
                    place += LANES


def norm1_other(grads, weights):
    rows = grads[0].shape[1] // 2
    width, cols = weights[0].shape[1:]
    block = 512
    count = rows // block
    many = len(grads)

    def kernel(*refs):
        out_ref, joined = refs[-2:]
        join_weights(refs[many:-2], joined)
        out_ref[...] = dot(side_by_side(refs[:many]), joined[...], NT).astype(bf16)

    return call(
        kernel,
        "first_other",
        (count,),
        pair_specs(grads, block, lambda i: i + count) + [whole(w) for w in weights],
        pl.BlockSpec((block, width), lambda i: (i, 0)),
        shape((rows, width), bf16),
        [pltpu.VMEM((width, 3 * cols * len(weights)), bf16)],
        flops=12 * rows * width * cols,
        nbytes=12 * rows * cols + 2 * rows * width + 12 * width * cols,
    )(*grads, *weights)


def norm1_own(grads, weights, received, tokens, middle_grad, params, scal):
    rows, width = tokens.shape
    cols = weights[0].shape[2]
    block = 256
    last = rows // block - 1
    many = len(grads)

    def kernel(scal_ref, *refs):
        rec_ref, tok_ref, mid_ref, par_ref, out_ref, sum_ref, joined = refs[many + len(weights) :]
        i = pl.program_id(0)
        join_weights(refs[many : many + len(weights)], joined)
        grad = dot(side_by_side(refs[:many]), joined[...], NT) + rec_ref[...].astype(f32)
        unit, inverse = normalize(tok_ref[...].astype(f32))
        out = mid_ref[...] + norm_back(grad, par_ref[0:1, :], unit, inverse)
        out_ref[...] = out.astype(bf16)
        sums = [jnp.sum(v, axis=0, keepdims=True) for v in (grad * unit, grad)]
        add_rows(sum_ref, sums, i == 0, 0)

        @pl.when(i == last)
        def _():
            sum_ref[...] = sum_ref[...] * scal_ref[1]

    spec = pl.BlockSpec((block, width), lambda i: (i, 0))
    sums = shape((8, width), f32)
    return call(
        kernel,
        "first_own",
        (rows // block,),
        [scalars()]
        + pair_specs(grads, block, lambda i: i)
        + [whole(w) for w in weights]
        + [spec] * 3
        + [whole(params)],
        [spec, whole(sums)],
        [shape((rows, width), bf16), sums],
        [pltpu.VMEM((width, 3 * cols * len(weights)), bf16)],
        flops=12 * rows * width * cols,
        nbytes=12 * rows * cols + 10 * rows * width + 12 * width * cols,
    )(scal, *grads, *weights, received, tokens, middle_grad, params)


def down_specs(weights):
    return [
        pl.BlockSpec(
            (w.shape[0], None, *w.shape[2:]), lambda i, j=j: (0, j, 0, 0), pipeline_mode=pl.Buffered(1)
        )
        for w, j in weights
    ]


def down_product(acts, weights):
    total = None
    for a_ref, w_ref in zip(acts, weights, strict=True):
        part = dot(a_ref[...], w_ref[...].reshape(a_ref.shape[1], w_ref.shape[-1]))
        total = part if total is None else total + part
    return total


def result_other(acts, weights):
    rows, hidden = acts[0].shape
    rows = rows // 2
    width = weights[0][0].shape[-1]
    block = 512
    start = rows // block
    many = len(acts)

    def kernel(*refs):
        refs[-1][...] = down_product(refs[:many], refs[many:-1]).astype(bf16)

    return call(
        kernel,
        "result_other",
        (rows // block,),
        [pl.BlockSpec((block, hidden), lambda i: (i + start, 0))] * many + down_specs(weights),
        pl.BlockSpec((block, width), lambda i: (i, 0)),
        shape((rows, width), bf16),
        flops=2 * many * rows * hidden * width,
        nbytes=2 * many * rows * hidden,
    )(*acts, *[w for w, _ in weights])


def block_result(middle, acts, weights, received, params, scal):
    rows, width = middle.shape
    hidden = acts[0].shape[1]
    block = 256
    many = len(acts)

    def kernel(scal_ref, mid_ref, rec_ref, par_ref, *refs):
        total = mid_ref[...] + down_product(refs[:many], refs[many:-1])
        total = total + rec_ref[...].astype(f32) + par_ref[5:6, :]
        refs[-1][...] = (total * scal_ref[0]).astype(bf16)

    spec = pl.BlockSpec((block, width), lambda i: (i, 0))
    return call(
        kernel,
        "block_result",
        (rows // block,),
        [scalars(), spec, spec, whole(params)]
        + [pl.BlockSpec((block, hidden), lambda i: (i, 0))] * many
        + down_specs(weights),
        spec,
        shape((rows, width), bf16),
        flops=2 * many * rows * hidden * width,
        nbytes=12 * rows * width,
        weight=1000,
    )(scal, middle, received, params, *acts, *[w for w, _ in weights])


def add_terms(*terms):
    rows, width = terms[0].shape
    block = 512

    def kernel(*refs):
        total = refs[0][...].astype(f32)
        for ref in refs[1:-1]:
            total = total + ref[...].astype(f32)
        refs[-1][...] = total.astype(bf16)

    spec = pl.BlockSpec((block, width), lambda i: (i, 0))
    return call(
        kernel,
        "add_terms",
        (rows // block,),
        [spec] * len(terms),
        spec,
        shape((rows, width), bf16),
        flops=len(terms) * rows * width,
        nbytes=2 * (len(terms) + 1) * rows * width,
    )(*terms)


def last_doubling(owns, others, flags):
    rows, cols = owns[0].shape
    blocks = rows // cols

    def kernel(flag_ref, own_a, own_b, other_a, other_b, wi_ref, wo_ref):
        factor = flag_ref[2]

        def ordered(k, own_ref, other_ref):
            is_upper = flag_ref[k] > 0.5
            own = own_ref[...].astype(f32) * factor
            other = other_ref[...].astype(f32) * factor
            return jnp.where(is_upper, other, own), jnp.where(is_upper, own, other)

        wi_ref[0], wi_ref[1] = ordered(0, own_a, other_a)
        wi_ref[2], below = ordered(1, own_b, other_b)
        for k in range(blocks):
            wo_ref[:, k * cols : (k + 1) * cols] = below[k * cols : (k + 1) * cols, :]

    outs = [shape((3, rows, cols), f32), shape((cols, rows), f32)]
    return call(
        kernel,
        "last_doubling",
        (1,),
        [scalars()] + [whole(value) for value in (*owns, *others)],
        [whole(out) for out in outs],
        outs,
        flops=8 * rows * cols,
        nbytes=24 * rows * cols,
    )(flags, *owns, *others)


def body(
    tokens,
    out_grad,
    item_counts,
    group_dataset,
    variable_mask,
    first_gain,
    first_shift,
    input_weight,
    input_bias,
    output_weight,
    output_bias,
    second_gain,
    second_shift,
    up_weight,
    up_bias,
    down_weight,
    down_bias,
):
    shard_count = lax.axis_size("mp")
    groups = lax.axis_size("dp")
    rows, width = tokens.shape
    cols = input_weight.shape[2]
    hidden = up_weight.shape[1]

    def core_swap(value):
        return lax.ppermute(value, "mp", [(i, i ^ 1) for i in range(shard_count)])

    def chip_swap(value):
        return lax.ppermute(value, "mp", [(i, i ^ 2) for i in range(shard_count)])

    def after(value, *others):
        return lax.optimization_barrier((value, *others))[0]

    def along(value, bit):
        return lax.ppermute(value, "dp", [(i, i ^ bit) for i in range(groups)])

    group = lax.axis_index("dp")

    slice_rows = up_weight.shape[0] // groups
    slices = [
        lax.dynamic_slice_in_dim(weight, group * slice_rows, slice_rows, 0)
        for weight in (up_weight, down_weight)
    ]
    slice_two = chip_swap(jnp.stack(slices)[None])
    bias_pack = jnp.concatenate([up_bias, input_bias[0], input_bias[1]]).reshape(-1, LANES)
    bias_two = chip_swap(bias_pack)
    wi_two = chip_swap(after(input_weight, *slices))
    cot_t = core_swap(out_grad)
    normed1 = first_norm(tokens, first_gain, first_shift)
    normed1_t = core_swap(normed1)
    item_counts, variable_mask, output_bias = after(
        (item_counts, variable_mask, output_bias), normed1
    )

    live = (lax.axis_index("mp") // 2 < item_counts[0]).astype(f32)
    dataset_hit = jnp.arange(variable_mask.shape[0], dtype=jnp.int32) == group_dataset[0]
    own_units = (
        item_counts[0] * jnp.sum(jnp.where(dataset_hit[:, None], variable_mask, 0))
    ).astype(f32)
    scal = jnp.stack([live, own_units, (group % 2).astype(f32)])
    zero = jnp.zeros((width,), f32)
    params = jnp.stack(
        [first_gain, first_shift, output_bias, second_gain, second_shift, down_bias, zero, zero]
    )

    qkv_one = project(normed1, input_weight, input_bias)
    wo_two = chip_swap(after(output_weight, qkv_one[0]))
    ff_weights_two = lax.all_gather(after(slice_two, qkv_one[0]), "dp", axis=0, tiled=True)
    qkv_one = project(normed1_t, input_weight, after(input_bias, qkv_one[0]), qkv_one)
    att_one, att_one_send, turned_one, stat_one = attend_forward(*qkv_one)
    att_one_t = core_swap(att_one_send)
    wo_one_t = core_swap(output_weight)
    bias_two = after(bias_two, att_one).reshape(-1)
    up_bias_one = up_bias.reshape(1, hidden)
    up_bias_two = bias_two[:hidden].reshape(1, hidden)
    in_bias_two = bias_two[hidden:].reshape(2, cols)
    qkv_two = project_both(
        after(normed1, att_one), normed1_t, wi_two, after(in_bias_two, up_bias_two)
    )
    qkv_two = after(tuple(qkv_two), att_one_t)
    att_two, att_two_send, turned_two, stat_two = attend_forward(*qkv_two)
    wo_two_t = core_swap(after(wo_two, att_two))
    att_two_t = core_swap(att_two_send)
    middle, normed2 = output_own(
        tokens,
        [att_one, att_two, att_one_t, att_two_t],
        [output_weight, wo_two, wo_one_t, wo_two_t],
        params,
    )
    normed2_t = core_swap(normed2)

    act_two, ng_two, keep_two, send_two, up_sum_two = feed_forward(
        normed2, normed2_t, out_grad, cot_t, up_bias_two, (ff_weights_two, 0), (ff_weights_two, 1), scal
    )
    two_received = along(send_two, 1)
    up_one, down_one = ((w.reshape(1, 1, -1, width), 0) for w in (up_weight, down_weight))
    act_one, ng_own, *ng_sends, keep_one, send_one, up_sum_one = feed_forward(
        normed2, normed2_t, out_grad, cot_t, up_bias_one, up_one, down_one, scal, ng_two
    )
    one_received = along(send_one, 1)
    ng_received = [core_swap(ng_send) for ng_send in ng_sends]
    middle_grad, middle_low, second_sums = second_back(
        middle, ng_own, ng_received, out_grad, params, scal
    )
    pair_two = add_terms(keep_two, after(two_received, middle_low))
    pair_received = chip_swap(pair_two)
    middle_low_t = core_swap(middle_low)
    middle_low = after(middle_low, pair_two)
    out_weights = [output_weight, wo_two]
    g_one, g_two, *wo_terms = output_back(
        middle_low, [att_one, att_two], out_weights, scal
    )
    g_one_t, g_two_t, wo_one_term, wo_two_term = output_back(
        middle_low_t, [att_one_send, att_two_send], out_weights, scal, wo_terms
    )

    def both(own, received, *last):
        return (own.astype(f32) + after(received, *last).astype(f32)).astype(bf16)

    back_two = [attend_backward(*qkv_two, g_two, g_two_t, turned_two, stat_two, 0, 1)]
    wait = back_two[0][0]
    acts = [act_two, act_one]
    downs = [(ff_weights_two, 1), down_one]
    result_send = result_other([after(act_two, wait), act_one], downs)
    result_received = core_swap(result_send)
    ff_both = add_terms(keep_one, one_received, after(pair_received, wait, result_send))
    ff_sum = lax.psum(
        ff_both, "dp", axis_index_groups=[list(range(k, groups, 2)) for k in range(2)]
    )
    back_two.append(
        attend_backward(
            *qkv_two, after(g_two, ff_both), g_two_t, turned_two, stat_two, 1, cols // LANES - 1
        )
    )
    grads_two = [back[0] for back in back_two]
    wi_two_term = input_term(normed1, normed1_t, grads_two, scal)[0]
    wo_received = chip_swap(after(wo_two_term, grads_two[1]))
    wi_received = chip_swap(wi_two_term)
    g_one = after(g_one, wi_two_term)
    back_one = [attend_backward(*qkv_one, g_one, g_one_t, turned_one, stat_one, 0, cols // LANES)]
    grads_one = [back[0] for back in back_one]

    bits = [1 << k for k in range(groups.bit_length() - 1)]
    orders = [bits, bits[1:2] + bits[:1] + bits[2:]]

    def upper(bit):
        return (group // bit) % 2

    def split(part, bit, axis=0):
        half = part.shape[axis] // 2
        return (
            lax.dynamic_slice_in_dim(part, upper(bit) * half, half, axis),
            lax.dynamic_slice_in_dim(part, (1 - upper(bit)) * half, half, axis),
        )

    place = jnp.stack([upper(order[0]) for order in orders]).astype(jnp.int32)
    keep_a, send_a, keep_b, send_b = input_term(
        normed1, normed1_t, grads_one, scal, wi_received, (wo_one_term, wo_received), place
    )
    keeps, sends = (keep_a, keep_b), (send_a, send_b)
    received = [along(sends[k], orders[k][0]) for k in range(2)]

    grads = grads_one + grads_two
    weights = [input_weight, wi_two]
    ng1_received = core_swap(norm1_other(grads, [input_weight, after(wi_two, *sends)]))
    parts = [both(keeps[k], received[k]) for k in range(2)]
    keeps, sends = zip(*[split(parts[k], orders[k][1]) for k in range(2)], strict=True)
    received = [along(sends[k], orders[k][1]) for k in range(2)]
    ff_sum_other = along(after(ff_sum, *sends), 1)
    result = block_result(after(middle, *sends), acts, downs, result_received, params, scal)
    merged = jnp.stack([both(keeps[k], received[k], result) for k in range(2)])
    later = bits[2:]
    for bit in later:
        keep, send = split(merged, bit, 1)
        received = along(send, bit)
        wait = []
        if bit == later[-1]:
            token_grad, first_sums = norm1_own(
                grads, weights, ng1_received, after(tokens, send), middle_grad, params, scal
            )
            wait = [token_grad]
        merged = both(keep, received, *wait)
    first_sums = after(first_sums, merged)

    def double(part, received, bit, axis):
        is_upper = upper(bit) == 1
        pair = [jnp.where(is_upper, received, part), jnp.where(is_upper, part, received)]
        return jnp.concatenate(pair, axis)

    for bit in reversed(later):
        merged = double(merged, along(merged, bit), bit, 1)
    parts = [merged[0], merged[1]]
    parts[1] = after(parts[1], ff_sum_other)
    ahead = parts
    parts = [double(parts[k], along(parts[k], orders[k][1]), orders[k][1], 0) for k in range(2)]
    last_parts = parts
    last_received = [along(parts[k], orders[k][0]) for k in range(2)]

    lower = group % 2 == 0
    up_sum = jnp.where(lower, ff_sum, ff_sum_other)
    down_sum = jnp.where(lower, ff_sum_other, ff_sum)

    def quarter_rows(parts, up_sums):
        sums_all = jnp.concatenate([part[1] for part in parts], 1)
        rest = jnp.full((1, width - 2 * cols), own_units)
        bias_row = jnp.concatenate([sums_all[0:1] * own_units, sums_all[1:2] * own_units, rest], 1)
        return up_sums + jnp.pad(bias_row, ((6, 1), (0, 0)))

    late = first_sums + second_sums
    late = late + core_swap(late)
    late_one = late + quarter_rows(back_one, up_sum_one)
    late = late_one + chip_swap(late + quarter_rows(back_two, up_sum_two))
    for bit in bits[1:] + bits[:1]:
        late = after(late, *(ahead if bit > 1 else last_parts))
        late = late + along(late, bit)
    share = 2.0 / late[6, -1]
    late = late * share

    flags = jnp.stack([*(upper(order[0]).astype(f32) for order in orders), share])
    wi_grad, wo_grad = last_doubling(last_parts, last_received, flags)

    return (
        result,
        token_grad,
        late[0],
        late[1],
        wi_grad,
        late[6, : 2 * cols].reshape(2, cols),
        wo_grad,
        late[4],
        late[2],
        late[3],
        up_sum.astype(f32) * share,
        late[7],
        down_sum.astype(f32) * share,
        late[5],
    )


def solution(mesh):
    in_specs = (
        P(("dp", "mp"), None),
        P(("dp", "mp"), None),
        P("dp"),
        P("dp"),
        P(),
        P(),
        P(),
        P(None, None, "mp"),
        P(None, "mp"),
        P("mp", None),
        P(),
        P(),
        P(),
        P(None, "mp"),
        P("mp"),
        P("mp", None),
        P(),
    )
    out_specs = (
        P(("dp", "mp"), None),
        P(("dp", "mp"), None),
        P(),
        P(),
        P(None, None, "mp"),
        P(None, "mp"),
        P("mp", None),
        P(),
        P(),
        P(),
        P(None, "mp"),
        P("mp"),
        P("mp", None),
        P(),
    )
    return jax.shard_map(body, mesh=mesh, in_specs=in_specs, out_specs=out_specs, check_vma=False)
```

```python
import jax
import jax.numpy as jnp
from jax import lax
from jax.experimental import pallas as pl
from jax.experimental.pallas import tpu as pltpu
from jax.sharding import PartitionSpec as P

HEAD_DIM = 64
LANES = 128
norm_eps = 1e-06
SCALE = HEAD_DIM**-0.5
LOG2E = 1.4426950408889634
RSQRT2 = 0.7071067811865476
RSQRT2PI = 0.3989422804014327

bf16 = jnp.bfloat16
f32 = jnp.float32
NN = (((1,), (0,)), ((), ()))
NT = (((1,), (1,)), ((), ()))
TN = (((0,), (0,)), ((), ()))
VMEM_BYTES = 60 << 20


def dot(left, right, dims=NN):
    return lax.dot_general(left, right, dims, preferred_element_type=f32)


def shape(dims, dtype):
    return jax.ShapeDtypeStruct(dims, dtype)


def whole(array):
    rank = len(array.shape)
    return pl.BlockSpec(array.shape, lambda *_: (0,) * rank, pipeline_mode=pl.Buffered(1))


def scalars():
    return pl.BlockSpec(memory_space=pltpu.SMEM)


def call(kernel, name, grid, in_specs, out_specs, out_shape, scratch=(), flops=0, nbytes=0, exps=0, weight=1e-6, aliases=None):
    return pl.pallas_call(
        kernel,
        name=name,
        grid=grid,
        in_specs=in_specs,
        out_specs=out_specs,
        out_shape=out_shape,
        scratch_shapes=list(scratch),
        input_output_aliases=aliases or {},
        compiler_params=pltpu.CompilerParams(vmem_limit_bytes=VMEM_BYTES),
        cost_estimate=pl.CostEstimate(
            flops=int(flops * weight), bytes_accessed=int(nbytes * weight), transcendentals=int(exps * weight)
        ),
    )


def split_two(values):
    high = values.astype(bf16)
    return high, (values - high.astype(f32)).astype(bf16)


def split_three(values):
    high = values.astype(bf16)
    rest = values - high.astype(f32)
    mid = rest.astype(bf16)
    return high, mid, (rest - mid.astype(f32)).astype(bf16)


def stat_rows(vector, rows):
    high, mid, rest = (part.astype(f32) for part in split_three(vector))
    row = lax.broadcasted_iota(jnp.int32, (rows, vector.shape[1]), 0)
    return jnp.where(
        row == 0, high, jnp.where(row == 1, mid, jnp.where(row == 2, rest, 0.0))
    ).astype(bf16)


def normalize(values):
    centered = values - jnp.mean(values, axis=-1, keepdims=True)
    variance = jnp.mean(centered * centered, axis=-1, keepdims=True)
    inverse = lax.rsqrt(variance + norm_eps)
    return centered * inverse, inverse


def norm_back(grad, gain, unit, inverse):
    scaled = grad * gain
    return inverse * (
        scaled
        - jnp.mean(scaled, axis=-1, keepdims=True)
        - unit * jnp.mean(scaled * unit, axis=-1, keepdims=True)
    )


def add_rows(ref, rows, first, start):
    @pl.when(first)
    def _():
        ref[...] = jnp.zeros_like(ref)

    for place, row in enumerate(rows):
        ref[start + place : start + place + 1, :] += row


def first_norm(tokens, gain, shift):
    rows, width = tokens.shape
    block = 256

    def kernel(tok_ref, gain_ref, shift_ref, norm_ref):
        unit, _ = normalize(tok_ref[...].astype(f32))
        gain_row = gain_ref[...].reshape(1, width)
        norm_ref[...] = (unit * gain_row + shift_ref[...].reshape(1, width)).astype(bf16)

    spec = pl.BlockSpec((block, width), lambda i: (i, 0))
    return call(
        kernel,
        "first_norm",
        (rows // block,),
        [spec, whole(gain), whole(shift)],
        spec,
        shape((rows, width), bf16),
        flops=20 * rows * width,
        nbytes=4 * rows * width,
    )(tokens, gain, shift)


def halves(block, width, count):
    own = pl.BlockSpec((block, width), lambda i, *_: (jnp.minimum(i, count - 1), 0))
    other = pl.BlockSpec((block, width), lambda i, *_: (jnp.maximum(i - count, 0), 0))
    return own, other


def pick(count, own_ref, other_ref):
    return jnp.where(pl.program_id(0) < count, own_ref[...], other_ref[...])


def project(norm, weight, bias, earlier=None):
    rows, width = norm.shape
    cols = weight.shape[2]
    block = 512
    start = 0 if earlier is None else rows // block
    skip = 0 if earlier is None else 3

    def kernel(x_ref, w_ref, b_ref, *refs):
        q_ref, k_ref, v_ref = refs[skip:]
        x = x_ref[...]
        q_ref[...] = (dot(x, w_ref[0]) + b_ref[0:1, :]).astype(bf16)
        k_ref[...] = dot(x, w_ref[1]).astype(bf16)
        v_ref[...] = (dot(x, w_ref[2]) + b_ref[1:2, :]).astype(bf16)

    out = pl.BlockSpec((block, cols), lambda i: (i + start, 0))
    return call(
        kernel,
        "project",
        (rows // block,),
        [pl.BlockSpec((block, width), lambda i: (i, 0)), whole(weight), whole(bias)]
        + [pl.BlockSpec(memory_space=pl.ANY)] * skip,
        [out] * 3,
        [shape((2 * rows, cols), bf16)] * 3,
        flops=6 * rows * width * cols,
        nbytes=2 * rows * width + 6 * width * cols + 6 * rows * cols,
        weight=1000,
        aliases={3 + k: k for k in range(skip)},
    )(norm, weight, bias, *(earlier or ()))


def project_both(norm_own, norm_other, weight, bias):
    rows, width = norm_own.shape
    cols = weight.shape[2]
    block = 512
    count = rows // block

    def kernel(own_ref, other_ref, w_ref, b_ref, q_ref, k_ref, v_ref):
        x = pick(count, own_ref, other_ref)
        q_ref[...] = (dot(x, w_ref[0]) + b_ref[0:1, :]).astype(bf16)
        k_ref[...] = dot(x, w_ref[1]).astype(bf16)
        v_ref[...] = (dot(x, w_ref[2]) + b_ref[1:2, :]).astype(bf16)

    out = pl.BlockSpec((block, cols), lambda i: (i, 0))
    return call(
        kernel,
        "project_both",
        (2 * count,),
        [*halves(block, width, count), whole(weight), whole(bias)],
        [out] * 3,
        [shape((2 * rows, cols), bf16)] * 3,
        flops=12 * rows * width * cols,
        nbytes=4 * rows * width + 6 * width * cols + 12 * rows * cols,
        weight=1000,
    )(norm_own, norm_other, weight, bias)


def attend_forward(queries, keys, values):
    rows, width = queries.shape
    chunk = min(512, rows)

    def kernel(q_ref, k_ref, v_ref, own_ref, other_ref, ot_ref, lse_ref):
        k = k_ref[...]
        lane = lax.broadcasted_iota(jnp.int32, k.shape, 1)
        rolled = pltpu.roll(k.astype(f32), HEAD_DIM, 1).astype(bf16)
        turned = v_ref[...].astype(f32).T
        ones = jnp.ones((HEAD_DIM, rows), bf16)
        q_turned = q_ref[...].astype(f32).T * (SCALE * LOG2E)
        outs = []
        for head in range(2):
            at = head * HEAD_DIM
            k_two = jnp.where(lane < HEAD_DIM, k, rolled) if head == 0 else jnp.where(lane < HEAD_DIM, rolled, k)
            own = turned[at : at + HEAD_DIM].astype(bf16)
            v_turned = jnp.concatenate([own, ones] if head == 0 else [ones, own], 0)
            q_two = jnp.concatenate(split_two(q_turned[at : at + HEAD_DIM]), 0)
            total = peak = None
            for j in range(rows // chunk):
                part = slice(j * chunk, (j + 1) * chunk)
                scores = dot(k_two[part], q_two)
                top = jnp.max(scores.reshape(chunk // 8, 8, rows).max(axis=0), axis=0, keepdims=True)
                higher = top if peak is None else jnp.maximum(peak, top)
                weights = jnp.exp2(scores - higher).astype(bf16)
                add = dot(v_turned[:, part], weights)
                total = add if total is None else total * jnp.exp2(peak - higher) + add
                peak = higher
            row_sum = total[HEAD_DIM - at : HEAD_DIM - at + 1]
            outs.append(total[at : at + HEAD_DIM] / row_sum)
            lse_ref[head : head + 1, :] = peak + jnp.log2(row_sum)
        attended = jnp.concatenate(outs, 0)
        ot_ref[...] = attended
        own_ref[...] = attended[:, : rows // 2].T.astype(bf16)
        other_ref[...] = attended[:, rows // 2 :].T.astype(bf16)

    by_pair = pl.BlockSpec((rows, LANES), lambda j: (0, j))
    by_half = pl.BlockSpec((rows // 2, LANES), lambda j: (0, j))
    pairs = width // LANES
    return call(
        kernel,
        "attend_forward",
        (pairs,),
        [by_pair] * 3,
        [
            by_half,
            by_half,
            pl.BlockSpec((LANES, rows), lambda j: (j, 0)),
            pl.BlockSpec((None, 8, rows), lambda j: (j, 0, 0)),
        ],
        [shape((rows // 2, width), bf16)] * 2
        + [shape((width, rows), f32), shape((pairs, 8, rows), f32)],
        flops=16 * rows * rows * width,
        nbytes=12 * rows * width,
        exps=rows * rows * width // HEAD_DIM,
        weight=1000,
    )(queries, keys, values)


def attend_backward(queries, keys, values, grad_own, grad_other, out_turned, stats, first, pairs):
    rows = queries.shape[0]
    width = LANES * pairs
    block = grad_own.shape[0]
    chunk = 256
    count = rows // block

    def kernel(
        q_ref, k_ref, v_ref, go_ref, gt_ref, ot_ref, lse_ref, d_ref, sum_ref,
        k_wide, k_turned, v_wide, dk_acc, dv_acc,
    ):
        i = pl.program_id(1)

        @pl.when(i == 0)
        def _():
            k = k_ref[...]
            v = v_ref[...]
            lane = lax.broadcasted_iota(jnp.int32, k.shape, 1)
            k_rolled = pltpu.roll(k.astype(f32), HEAD_DIM, 1).astype(bf16)
            v_rolled = pltpu.roll(v.astype(f32), HEAD_DIM, 1).astype(bf16)
            ones = jnp.where(lane < 3, 1.0, 0.0).astype(bf16)
            k_wide[0] = jnp.concatenate([jnp.where(lane < HEAD_DIM, k, k_rolled), ones], 1)
            k_wide[1] = jnp.concatenate([jnp.where(lane < HEAD_DIM, k_rolled, k), ones], 1)
            tail = jnp.where(lane < HEAD_DIM + 3, 1.0, 0.0).astype(bf16)
            v_wide[0] = jnp.where(lane < HEAD_DIM, v, tail)
            v_wide[1] = jnp.where(lane < HEAD_DIM, v_rolled, tail)
            k_turned[...] = k.astype(f32).T.astype(bf16)
            dk_acc[...] = jnp.zeros_like(dk_acc)
            dv_acc[...] = jnp.zeros_like(dv_acc)
            sum_ref[...] = jnp.zeros_like(sum_ref)

        q_turned = q_ref[...].astype(f32).T
        q_low = q_turned.astype(bf16)
        q_turned = q_turned * (SCALE * LOG2E)
        g_turned = jnp.where(i == 0, go_ref[...], gt_ref[...]).astype(f32).T
        g_low = g_turned.astype(bf16)
        dqs = []
        for head in range(2):
            part = slice(head * HEAD_DIM, (head + 1) * HEAD_DIM)
            q_wide = jnp.concatenate(
                [*split_two(q_turned[part]), stat_rows(-lse_ref[head : head + 1, :], LANES)], 0
            )
            row_dot = jnp.sum(g_turned[part] * ot_ref[part, :], axis=0, keepdims=True)
            g_wide = jnp.concatenate([g_low[part], stat_rows(-row_dot, HEAD_DIM)], 0)
            dq = None
            for j in range(rows // chunk):
                at = pl.ds(j * chunk, chunk)
                probabilities = jnp.exp2(dot(k_wide[head, at, :], q_wide))
                shifted = dot(v_wide[head, at, :], g_wide)
                probs_low = probabilities.astype(bf16)
                score_grad = (probabilities * shifted).astype(bf16)
                dv_acc[part, at] += dot(g_low[part], probs_low, NT)
                dk_acc[part, at] += dot(q_low[part], score_grad, NT)
                add = dot(k_turned[part, at], score_grad)
                dq = add if dq is None else dq + add
            dqs.append(dq)
        dq = (jnp.concatenate(dqs, 0) * SCALE).T
        d_ref[pl.ds(i * block, block), :LANES] = dq.astype(bf16)
        sum_ref[0:1, :] += jnp.sum(dq, axis=0, keepdims=True)

        @pl.when(i == count - 1)
        def _():
            d_ref[:, LANES : 2 * LANES] = (dk_acc[...] * SCALE).T.astype(bf16)
            dv = dv_acc[...].T
            d_ref[:, 2 * LANES :] = dv.astype(bf16)
            sum_ref[1:2, :] = jnp.sum(dv, axis=0, keepdims=True)

    by_query = pl.BlockSpec((block, LANES), lambda j, i: (i, j + first))
    by_key = pl.BlockSpec((rows, LANES), lambda j, i: (0, j + first))
    half = pl.BlockSpec((block, LANES), lambda j, i: (0, j + first))
    turned_spec = pl.BlockSpec((LANES, block), lambda j, i: (j + first, i))
    stat_spec = pl.BlockSpec((None, 8, block), lambda j, i: (j + first, 0, i))
    out_spec = pl.BlockSpec((None, rows, 3 * LANES), lambda j, i: (j, 0, 0))
    sum_spec = pl.BlockSpec((8, LANES), lambda j, i: (0, j))
    return call(
        kernel,
        "attend_backward",
        (pairs, count),
        [by_query, by_key, by_key, half, half, turned_spec, stat_spec],
        [out_spec, sum_spec],
        [shape((pairs, rows, 3 * LANES), bf16), shape((8, width), f32)],
        [
            pltpu.VMEM((2, rows, 2 * LANES), bf16),
            pltpu.VMEM((LANES, rows), bf16),
            pltpu.VMEM((2, rows, LANES), bf16),
            pltpu.VMEM((LANES, rows), f32),
            pltpu.VMEM((LANES, rows), f32),
        ],
        flops=40 * rows * rows * width,
        nbytes=20 * rows * width,
        exps=rows * rows * width // HEAD_DIM,
        weight=1000,
    )(queries, keys, values, grad_own, grad_other, out_turned, stats)


def output_own(tokens, attended, weights, params):
    rows, width = tokens.shape
    cols = weights[0].shape[0]
    block = 256
    many = len(attended)

    def kernel(t_ref, par_ref, *refs):
        total = None
        for a_ref, w_ref in zip(refs[:many], refs[many : 2 * many], strict=True):
            part = dot(a_ref[...], w_ref[...])
            total = part if total is None else total + part
        mid_ref, norm_ref = refs[2 * many :]
        middle = t_ref[...].astype(f32) + total + par_ref[2:3, :]
        mid_ref[...] = middle
        unit, _ = normalize(middle)
        norm_ref[...] = (unit * par_ref[3:4, :] + par_ref[4:5, :]).astype(bf16)

    spec = pl.BlockSpec((block, width), lambda i: (i, 0))
    thin = pl.BlockSpec((block, cols), lambda i: (i, 0))
    return call(
        kernel,
        "output_own",
        (rows // block,),
        [spec, whole(params)] + [thin] * many + [whole(w) for w in weights],
        [spec, spec],
        [shape((rows, width), f32), shape((rows, width), bf16)],
        flops=2 * rows * many * cols * width,
        nbytes=2 * rows * many * cols + 8 * rows * width,
    )(tokens, params, *attended, *weights)


def feed_forward(norm_own, norm_other, cot_own, cot_other, bias, up, down, scal, earlier=None):
    rows, width = norm_own.shape
    hidden = bias.shape[1]
    block = 512
    count = rows // block
    last = earlier is not None
    (up, up_place), (down, down_place) = up, down
    slices, depth = up.shape[0], up.shape[2]
    def kernel(scal_ref, no_ref, nt_ref, co_ref, ct_ref, b_ref, up_ref, dn_ref, *refs):
        if last:
            ng_in, act_ref, ngo_ref, nga_ref, ngb_ref, *refs = refs
        else:
            act_ref, ng_ref, *refs = refs
        keep, send, sum_ref, up_acc, down_acc = refs
        i = pl.program_id(0)

        @pl.when(i == 0)
        def _():
            up_acc[...] = jnp.zeros_like(up_acc)
            down_acc[...] = jnp.zeros_like(down_acc)
            sum_ref[...] = jnp.zeros_like(sum_ref)

        x = pick(count, no_ref, nt_ref)
        cot = (pick(count, co_ref, ct_ref).astype(f32) * scal_ref[0]).astype(bf16)
        up_now = up_ref[...].reshape(width, hidden)
        down_now = dn_ref[...].reshape(hidden, width)
        h = dot(x, up_now) + b_ref[0:1, :]
        cdf = 0.5 * (1.0 + lax.erf(h * RSQRT2))
        act = (h * cdf).astype(bf16)
        slope = cdf + h * (RSQRT2PI * jnp.exp(-0.5 * h * h))
        act_ref[...] = act
        grad = dot(cot, down_now, NT) * slope
        sum_ref[7:8, :] += jnp.sum(grad, axis=0, keepdims=True)
        low = grad.astype(bf16)
        ng = dot(low, up_now, NT)
        up_acc[...] += dot(x, low, TN)
        down_acc[...] += dot(act, cot, TN)
        if last:
            ng = ng + ng_in[...].astype(f32)

            @pl.when(i < count)
            def _():
                ngo_ref[...] = ng.astype(bf16)

            @pl.when((i >= count) & (i < count + count // 2))
            def _():
                nga_ref[...] = ng.astype(bf16)

            @pl.when(i >= count + count // 2)
            def _():
                ngb_ref[...] = ng.astype(bf16)
        else:
            ng_ref[...] = ng.astype(bf16)

        @pl.when(i == 2 * count - 1)
        def _():
            units = scal_ref[1]

            @pl.when(scal_ref[2] < 0.5)
            def _():
                keep[...] = (up_acc[...] * units).astype(bf16)
                send[...] = (down_acc[...] * units).astype(bf16)

            @pl.when(scal_ref[2] > 0.5)
            def _():
                keep[...] = (down_acc[...] * units).astype(bf16)
                send[...] = (up_acc[...] * units).astype(bf16)

            sum_ref[...] = sum_ref[...] * units

    own, other = halves(block, width, count)
    every = pl.BlockSpec((block, width), lambda i: (i, 0))
    up_spec, down_spec = (
        pl.BlockSpec(
            (slices, None, depth, width), lambda i, j=j: (0, j, 0, 0), pipeline_mode=pl.Buffered(1)
        )
        for j in (up_place, down_place)
    )
    ins = [scalars(), own, other, own, other, whole(bias), up_spec, down_spec]
    args = [scal, norm_own, norm_other, cot_own, cot_other, bias, up, down]
    outs = [every]
    shapes = [shape((2 * rows, hidden), bf16)]
    if last:
        ins += [every]
        args += [earlier]
        half = count // 2
        top = pl.BlockSpec((block, width), lambda i: (jnp.clip(i - count, 0, half - 1), 0))
        low = pl.BlockSpec((block, width), lambda i: (jnp.maximum(i - count - half, 0), 0))
        outs += [own, top, low]
        shapes += [shape((rows, width), bf16)] + [shape((rows // 2, width), bf16)] * 2
    else:
        outs += [every]
        shapes += [shape((2 * rows, width), bf16)]
    assert width == hidden
    terms = [shape((width, hidden), bf16)] * 2
    sums = shape((8, hidden), f32)
    return call(
        kernel,
        "feed_forward",
        (2 * count,),
        ins,
        outs + [whole(terms[0]), whole(terms[1]), whole(sums)],
        shapes + terms + [sums],
        [pltpu.VMEM((width, hidden), f32), pltpu.VMEM((hidden, width), f32)],
        flops=20 * rows * width * hidden,
        nbytes=24 * rows * width + 12 * width * hidden,
        exps=4 * rows * hidden,
        weight=1000 if last else 1e-6,
    )(*args)


def second_back(middle, grad_own, grad_received, cot, params, scal):
    rows, width = middle.shape
    block = 256
    half = rows // block // 2
    last = rows // block - 1

    def kernel(scal_ref, mid_ref, go_ref, ga_ref, gb_ref, cot_ref, par_ref, low_ref, sum_ref):
        i = pl.program_id(0)
        unit, inverse = normalize(mid_ref[...])
        grad = go_ref[...].astype(f32) + pick(half, ga_ref, gb_ref).astype(f32)
        cot = cot_ref[...].astype(f32) * scal_ref[0]
        out = cot + norm_back(grad, par_ref[3:4, :], unit, inverse)
        low_ref[...] = out.astype(bf16)
        sums = [jnp.sum(v, axis=0, keepdims=True) for v in (grad * unit, grad, out, cot)]
        add_rows(sum_ref, sums, i == 0, 2)

        @pl.when(i == last)
        def _():
            sum_ref[...] = sum_ref[...] * scal_ref[1]

    spec = pl.BlockSpec((block, width), lambda i: (i, 0))
    sums = shape((8, width), f32)
    return call(
        kernel,
        "second_back",
        (rows // block,),
        [scalars(), spec, spec, *halves(block, width, half), spec, whole(params)],
        [spec, whole(sums)],
        [shape((rows, width), bf16), sums],
        flops=30 * rows * width,
        nbytes=18 * rows * width,
    )(scal, middle, grad_own, *grad_received, cot, params)


def output_back(low, attended, weights, scal, earlier=None):
    rows, width = low.shape
    cols = weights[0].shape[0]
    block = 512
    last = earlier is not None

    def kernel(scal_ref, low_ref, a_ref, b_ref, wa_ref, wb_ref, *refs):
        before = refs[:2] if last else (None, None)
        ga_ref, gb_ref, ta_ref, tb_ref, acc_a, acc_b = refs[2 if last else 0 :]
        i = pl.program_id(0)
        now = low_ref[...]
        ga_ref[...] = dot(now, wa_ref[...], NT).astype(bf16)
        gb_ref[...] = dot(now, wb_ref[...], NT).astype(bf16)
        for acc, rows_ref, old in ((acc_a, a_ref, before[0]), (acc_b, b_ref, before[1])):

            @pl.when(i == 0)
            def _():
                acc[...] = jnp.zeros_like(acc) if old is None else old[...]

            acc[...] += dot(rows_ref[...], now, TN)

        @pl.when(i == rows // block - 1)
        def _():
            factor = scal_ref[1] if last else 1.0
            ta_ref[...] = (acc_a[...] * factor).astype(ta_ref.dtype)
            tb_ref[...] = (acc_b[...] * factor).astype(tb_ref.dtype)

    thin = pl.BlockSpec((block, cols), lambda i: (i, 0))
    terms = [shape((cols, width), bf16 if last else f32)] * 2
    before = list(earlier or ())
    return call(
        kernel,
        "output_back",
        (rows // block,),
        [scalars(), pl.BlockSpec((block, width), lambda i: (i, 0)), thin, thin]
        + [whole(w) for w in weights]
        + [whole(t) for t in before],
        [thin, thin, whole(terms[0]), whole(terms[1])],
        [shape((rows, cols), bf16)] * 2 + terms,
        [pltpu.VMEM((cols, width), f32)] * 2,
        flops=8 * rows * width * cols,
        nbytes=2 * rows * width + 8 * rows * cols,
        weight=1e-6 if last else 1000,
    )(scal, low, *attended, *weights, *before)


def side_by_side(refs):
    return jnp.concatenate([ref[p] for ref in refs for p in range(ref.shape[0])], 1)


def pair_specs(grads, block, place):
    return [
        pl.BlockSpec((g.shape[0], block, g.shape[2]), lambda i: (0, place(i), 0)) for g in grads
    ]


def input_term(norm_own, norm_other, grads, scal, other=None, outputs=(), place=None):
    rows, width = norm_own.shape
    pairs = sum(g.shape[0] for g in grads)
    cols = pairs * LANES
    many = len(grads)
    more = [] if other is None else [other, *outputs]
    quarter = width

    def kernel(scal_ref, *refs):
        place_ref = refs[0] if more else None
        no_ref, nt_ref, *refs = refs[1 if more else 0 :]
        outs, acc = refs[many + len(more) : -1], refs[-1]
        i = pl.program_id(0)
        term = dot(pick(1, no_ref, nt_ref), side_by_side(refs[:many]), TN)

        @pl.when(i == 0)
        def _():
            acc[...] = term

        def total(j, p):
            at = (3 * p + j) * LANES
            return (acc[:, at : at + LANES] + term[:, at : at + LANES]) * scal_ref[1]

        def store(half, keep, send):
            for p in range(pairs):
                lanes = slice(p * LANES, (p + 1) * LANES)
                for out_ref, j in ((keep, 2 * half), (send, 2 * half + 1)):
                    if j < 3:
                        final = total(j, p) + refs[many][j * width : (j + 1) * width, lanes].astype(f32)
                        out_ref[:, lanes] = final.astype(bf16)
                        continue
                    for k in range(width // cols):
                        at = slice(k * cols + p * LANES, k * cols + (p + 1) * LANES)
                        final = refs[many + 1][:, at].astype(f32) + refs[many + 2][:, at].astype(f32)
                        out_ref[k * cols : (k + 1) * cols, lanes] = final.astype(bf16)

        @pl.when(i == 1)
        def _():
            if not more:
                for p in range(pairs):
                    for j in range(3):
                        at = (slice(j * width, (j + 1) * width), slice(p * LANES, (p + 1) * LANES))
                        outs[0][at] = total(j, p).astype(bf16)
            for half in range(2 if more else 0):
                keep, send = outs[2 * half], outs[2 * half + 1]

                @pl.when(place_ref[half] == 0)
                def _():
                    store(half, keep, send)

                @pl.when(place_ref[half] == 1)
                def _():
                    store(half, send, keep)

    out = [shape((quarter, cols), bf16)] * 4 if more else [shape((3 * width, cols), bf16)]
    return call(
        kernel,
        "input_term",
        (2,),
        [scalars()]
        + [scalars()] * (1 if more else 0)
        + [*halves(rows, width, 1)]
        + pair_specs(grads, rows, lambda i: i)
        + [whole(m) for m in more],
        [whole(o) for o in out],
        out,
        [pltpu.VMEM((width, 3 * cols), f32)],
        flops=12 * rows * width * cols,
        nbytes=4 * rows * width + 12 * rows * cols + 12 * width * cols,
    )(scal, *([place] if more else []), norm_own, norm_other, *grads, *more)


def join_weights(refs, joined):
    @pl.when(pl.program_id(0) == 0)
    def _():
        place = 0
        for ref in refs:
            for p in range(ref.shape[2] // LANES):
                for j in range(3):
                    joined[:, place : place + LANES] = ref[j, :, p * LANES : (p + 1) * LANES]
                    place += LANES


def norm1_other(grads, weights):
    rows = grads[0].shape[1] // 2
    width, cols = weights[0].shape[1:]
    block = 512
    count = rows // block
    many = len(grads)

    def kernel(*refs):
        out_ref, joined = refs[-2:]
        join_weights(refs[many:-2], joined)
        out_ref[...] = dot(side_by_side(refs[:many]), joined[...], NT).astype(bf16)

    return call(
        kernel,
        "first_other",
        (count,),
        pair_specs(grads, block, lambda i: i + count) + [whole(w) for w in weights],
        pl.BlockSpec((block, width), lambda i: (i, 0)),
        shape((rows, width), bf16),
        [pltpu.VMEM((width, 3 * cols * len(weights)), bf16)],
        flops=12 * rows * width * cols,
        nbytes=12 * rows * cols + 2 * rows * width + 12 * width * cols,
    )(*grads, *weights)


def norm1_own(grads, weights, received, tokens, middle_grad, params, scal):
    rows, width = tokens.shape
    cols = weights[0].shape[2]
    block = 256
    last = rows // block - 1
    many = len(grads)

    def kernel(scal_ref, *refs):
        rec_ref, tok_ref, mid_ref, par_ref, out_ref, sum_ref, joined = refs[many + len(weights) :]
        i = pl.program_id(0)
        join_weights(refs[many : many + len(weights)], joined)
        grad = dot(side_by_side(refs[:many]), joined[...], NT) + rec_ref[...].astype(f32)
        unit, inverse = normalize(tok_ref[...].astype(f32))
        out = mid_ref[...].astype(f32) + norm_back(grad, par_ref[0:1, :], unit, inverse)
        out_ref[...] = out.astype(bf16)
        sums = [jnp.sum(v, axis=0, keepdims=True) for v in (grad * unit, grad)]
        add_rows(sum_ref, sums, i == 0, 0)

        @pl.when(i == last)
        def _():
            sum_ref[...] = sum_ref[...] * scal_ref[1]

    spec = pl.BlockSpec((block, width), lambda i: (i, 0))
    sums = shape((8, width), f32)
    return call(
        kernel,
        "first_own",
        (rows // block,),
        [scalars()]
        + pair_specs(grads, block, lambda i: i)
        + [whole(w) for w in weights]
        + [spec] * 3
        + [whole(params)],
        [spec, whole(sums)],
        [shape((rows, width), bf16), sums],
        [pltpu.VMEM((width, 3 * cols * len(weights)), bf16)],
        flops=12 * rows * width * cols,
        nbytes=12 * rows * cols + 10 * rows * width + 12 * width * cols,
    )(scal, *grads, *weights, received, tokens, middle_grad, params)


def down_specs(weights):
    return [
        pl.BlockSpec(
            (w.shape[0], None, *w.shape[2:]), lambda i, j=j: (0, j, 0, 0), pipeline_mode=pl.Buffered(1)
        )
        for w, j in weights
    ]


def down_product(acts, weights):
    total = None
    for a_ref, w_ref in zip(acts, weights, strict=True):
        part = dot(a_ref[...], w_ref[...].reshape(a_ref.shape[1], w_ref.shape[-1]))
        total = part if total is None else total + part
    return total


def result_other(acts, weights):
    rows, hidden = acts[0].shape
    rows = rows // 2
    width = weights[0][0].shape[-1]
    block = 512
    start = rows // block
    many = len(acts)

    def kernel(*refs):
        refs[-1][...] = down_product(refs[:many], refs[many:-1]).astype(bf16)

    return call(
        kernel,
        "result_other",
        (rows // block,),
        [pl.BlockSpec((block, hidden), lambda i: (i + start, 0))] * many + down_specs(weights),
        pl.BlockSpec((block, width), lambda i: (i, 0)),
        shape((rows, width), bf16),
        flops=2 * many * rows * hidden * width,
        nbytes=2 * many * rows * hidden,
    )(*acts, *[w for w, _ in weights])


def block_result(middle, acts, weights, received, params, scal):
    rows, width = middle.shape
    hidden = acts[0].shape[1]
    block = 256
    many = len(acts)

    def kernel(scal_ref, mid_ref, rec_ref, par_ref, *refs):
        total = mid_ref[...] + down_product(refs[:many], refs[many:-1])
        total = total + rec_ref[...].astype(f32) + par_ref[5:6, :]
        refs[-1][...] = (total * scal_ref[0]).astype(bf16)

    spec = pl.BlockSpec((block, width), lambda i: (i, 0))
    return call(
        kernel,
        "block_result",
        (rows // block,),
        [scalars(), spec, spec, whole(params)]
        + [pl.BlockSpec((block, hidden), lambda i: (i, 0))] * many
        + down_specs(weights),
        spec,
        shape((rows, width), bf16),
        flops=2 * many * rows * hidden * width,
        nbytes=12 * rows * width,
        weight=1000,
    )(scal, middle, received, params, *acts, *[w for w, _ in weights])


def add_terms(*terms):
    rows, width = terms[0].shape
    block = 512

    def kernel(*refs):
        total = refs[0][...].astype(f32)
        for ref in refs[1:-1]:
            total = total + ref[...].astype(f32)
        refs[-1][...] = total.astype(bf16)

    spec = pl.BlockSpec((block, width), lambda i: (i, 0))
    return call(
        kernel,
        "add_terms",
        (rows // block,),
        [spec] * len(terms),
        spec,
        shape((rows, width), bf16),
        flops=len(terms) * rows * width,
        nbytes=2 * (len(terms) + 1) * rows * width,
    )(*terms)


def last_doubling(owns, others, flags):
    rows, cols = owns[0].shape
    blocks = rows // cols

    def kernel(flag_ref, own_a, own_b, other_a, other_b, wi_ref, wo_ref):
        factor = flag_ref[2]

        def ordered(k, own_ref, other_ref):
            is_upper = flag_ref[k] > 0.5
            own = own_ref[...].astype(f32) * factor
            other = other_ref[...].astype(f32) * factor
            return jnp.where(is_upper, other, own), jnp.where(is_upper, own, other)

        wi_ref[0], wi_ref[1] = ordered(0, own_a, other_a)
        wi_ref[2], below = ordered(1, own_b, other_b)
        for k in range(blocks):
            wo_ref[:, k * cols : (k + 1) * cols] = below[k * cols : (k + 1) * cols, :]

    outs = [shape((3, rows, cols), f32), shape((cols, rows), f32)]
    return call(
        kernel,
        "last_doubling",
        (1,),
        [scalars()] + [whole(value) for value in (*owns, *others)],
        [whole(out) for out in outs],
        outs,
        flops=8 * rows * cols,
        nbytes=24 * rows * cols,
    )(flags, *owns, *others)


def body(
    tokens,
    out_grad,
    item_counts,
    group_dataset,
    variable_mask,
    first_gain,
    first_shift,
    input_weight,
    input_bias,
    output_weight,
    output_bias,
    second_gain,
    second_shift,
    up_weight,
    up_bias,
    down_weight,
    down_bias,
):
    shard_count = lax.axis_size("mp")
    groups = lax.axis_size("dp")
    rows, width = tokens.shape
    cols = input_weight.shape[2]
    hidden = up_weight.shape[1]

    def core_swap(value):
        return lax.ppermute(value, "mp", [(i, i ^ 1) for i in range(shard_count)])

    def chip_swap(value):
        return lax.ppermute(value, "mp", [(i, i ^ 2) for i in range(shard_count)])

    def after(value, *others):
        return lax.optimization_barrier((value, *others))[0]

    def along(value, bit):
        return lax.ppermute(value, "dp", [(i, i ^ bit) for i in range(groups)])

    group = lax.axis_index("dp")

    slice_rows = up_weight.shape[0] // groups
    slices = [
        lax.dynamic_slice_in_dim(weight, group * slice_rows, slice_rows, 0)
        for weight in (up_weight, down_weight)
    ]
    slice_two = chip_swap(jnp.stack(slices)[None])
    bias_pack = jnp.concatenate([up_bias, input_bias[0], input_bias[1]]).reshape(-1, LANES)
    bias_two = chip_swap(bias_pack)
    wi_two = chip_swap(after(input_weight, *slices))
    cot_t = core_swap(out_grad)
    normed1 = first_norm(tokens, first_gain, first_shift)
    normed1_t = core_swap(normed1)
    item_counts, variable_mask, output_bias = after(
        (item_counts, variable_mask, output_bias), normed1
    )

    live = (lax.axis_index("mp") // 2 < item_counts[0]).astype(f32)
    dataset_hit = jnp.arange(variable_mask.shape[0], dtype=jnp.int32) == group_dataset[0]
    own_units = (
        item_counts[0] * jnp.sum(jnp.where(dataset_hit[:, None], variable_mask, 0))
    ).astype(f32)
    scal = jnp.stack([live, own_units, (group % 2).astype(f32)])
    zero = jnp.zeros((width,), f32)
    params = jnp.stack(
        [first_gain, first_shift, output_bias, second_gain, second_shift, down_bias, zero, zero]
    )

    qkv_one = project(normed1, input_weight, input_bias)
    ff_weights_two = lax.all_gather(after(slice_two, qkv_one[0]), "dp", axis=0, tiled=True)
    qkv_one = project(normed1_t, input_weight, after(input_bias, qkv_one[0]), qkv_one)
    att_one, att_one_send, turned_one, stat_one = attend_forward(*qkv_one)
    att_one_t = core_swap(att_one_send)
    wo_two = chip_swap(after(output_weight, att_one))
    wo_two_t = lax.ppermute(
        after(output_weight, att_one), "mp", [(i, i ^ 3) for i in range(shard_count)]
    )
    wo_one_t = core_swap(output_weight)
    bias_two = after(bias_two, att_one).reshape(-1)
    up_bias_one = up_bias.reshape(1, hidden)
    up_bias_two = bias_two[:hidden].reshape(1, hidden)
    in_bias_two = bias_two[hidden:].reshape(2, cols)
    qkv_two = project_both(
        after(normed1, att_one), normed1_t, wi_two, after(in_bias_two, up_bias_two)
    )
    qkv_two = after(tuple(qkv_two), att_one_t, cot_t)
    att_two, att_two_send, turned_two, stat_two = attend_forward(*qkv_two)
    att_two_t = core_swap(att_two_send)
    middle, normed2 = output_own(
        tokens,
        [att_one, att_two, att_one_t, att_two_t],
        [output_weight, wo_two, wo_one_t, wo_two_t],
        params,
    )
    normed2_t = core_swap(normed2)

    act_two, ng_two, keep_two, send_two, up_sum_two = feed_forward(
        normed2, normed2_t, out_grad, cot_t, up_bias_two, (ff_weights_two, 0), (ff_weights_two, 1), scal
    )
    two_received = along(send_two, 1)
    up_one, down_one = ((w.reshape(1, 1, -1, width), 0) for w in (up_weight, down_weight))
    act_one, ng_own, *ng_sends, keep_one, send_one, up_sum_one = feed_forward(
        normed2, normed2_t, out_grad, cot_t, up_bias_one, up_one, down_one, scal, ng_two
    )
    one_received = along(send_one, 1)
    ng_received = [core_swap(ng_send) for ng_send in ng_sends]
    middle_low, second_sums = second_back(
        middle, ng_own, ng_received, out_grad, params, scal
    )
    pair_two = add_terms(keep_two, after(two_received, middle_low))
    pair_received = chip_swap(pair_two)
    middle_low_t = core_swap(middle_low)
    middle_low = after(middle_low, pair_two)
    out_weights = [output_weight, wo_two]
    g_one, g_two, *wo_terms = output_back(
        middle_low, [att_one, att_two], out_weights, scal
    )
    g_one_t, g_two_t, wo_one_term, wo_two_term = output_back(
        middle_low_t, [att_one_send, att_two_send], out_weights, scal, wo_terms
    )

    def both(own, received, *last):
        return (own.astype(f32) + after(received, *last).astype(f32)).astype(bf16)

    back_two = [attend_backward(*qkv_two, g_two, g_two_t, turned_two, stat_two, 0, 1)]
    wait = back_two[0][0]
    acts = [act_two, act_one]
    downs = [(ff_weights_two, 1), down_one]
    result_send = result_other([after(act_two, wait), act_one], downs)
    result_received = core_swap(result_send)
    ff_both = add_terms(keep_one, one_received, after(pair_received, wait, result_send))
    ff_sum = lax.psum(
        ff_both, "dp", axis_index_groups=[list(range(k, groups, 2)) for k in range(2)]
    )
    back_two.append(
        attend_backward(
            *qkv_two, after(g_two, ff_both), g_two_t, turned_two, stat_two, 1, cols // LANES - 1
        )
    )
    grads_two = [back[0] for back in back_two]
    wi_two_term = input_term(normed1, normed1_t, grads_two, scal)[0]
    wo_received = chip_swap(after(wo_two_term, grads_two[1]))
    wi_received = chip_swap(wi_two_term)
    g_one = after(g_one, wi_two_term)
    back_one = [attend_backward(*qkv_one, g_one, g_one_t, turned_one, stat_one, 0, cols // LANES)]
    grads_one = [back[0] for back in back_one]

    bits = [1 << k for k in range(groups.bit_length() - 1)]
    orders = [bits, bits[1:2] + bits[:1] + bits[2:]]

    def upper(bit):
        return (group // bit) % 2

    def split(part, bit, axis=0):
        half = part.shape[axis] // 2
        return (
            lax.dynamic_slice_in_dim(part, upper(bit) * half, half, axis),
            lax.dynamic_slice_in_dim(part, (1 - upper(bit)) * half, half, axis),
        )

    place = jnp.stack([upper(order[0]) for order in orders]).astype(jnp.int32)
    keep_a, send_a, keep_b, send_b = input_term(
        normed1, normed1_t, grads_one, scal, wi_received, (wo_one_term, wo_received), place
    )
    keeps, sends = (keep_a, keep_b), (send_a, send_b)
    received = [along(sends[k], orders[k][0]) for k in range(2)]

    grads = grads_one + grads_two
    weights = [input_weight, wi_two]
    ng1_received = core_swap(norm1_other(grads, [input_weight, after(wi_two, *sends)]))
    parts = [both(keeps[k], received[k]) for k in range(2)]
    keeps, sends = zip(*[split(parts[k], orders[k][1]) for k in range(2)], strict=True)
    received = [along(sends[k], orders[k][1]) for k in range(2)]
    ff_sum_other = along(after(ff_sum, *sends), 1)
    result = block_result(after(middle, *sends), acts, downs, result_received, params, scal)
    merged = jnp.stack([both(keeps[k], received[k], result) for k in range(2)])
    later = bits[2:]
    for bit in later:
        keep, send = split(merged, bit, 1)
        received = along(send, bit)
        wait = []
        if bit == later[-1]:
            token_grad, first_sums = norm1_own(
                grads, weights, ng1_received, after(tokens, send), middle_low, params, scal
            )
            wait = [token_grad]
        merged = both(keep, received, *wait)
    first_sums = after(first_sums, merged)

    def double(part, received, bit, axis):
        is_upper = upper(bit) == 1
        pair = [jnp.where(is_upper, received, part), jnp.where(is_upper, part, received)]
        return jnp.concatenate(pair, axis)

    for bit in reversed(later):
        merged = double(merged, along(merged, bit), bit, 1)
    parts = [merged[0], merged[1]]
    parts[1] = after(parts[1], ff_sum_other)
    ahead = parts
    parts = [double(parts[k], along(parts[k], orders[k][1]), orders[k][1], 0) for k in range(2)]
    last_parts = parts
    last_received = [along(parts[k], orders[k][0]) for k in range(2)]

    lower = group % 2 == 0
    up_sum = jnp.where(lower, ff_sum, ff_sum_other)
    down_sum = jnp.where(lower, ff_sum_other, ff_sum)

    def quarter_rows(parts, up_sums):
        sums_all = jnp.concatenate([part[1] for part in parts], 1)
        rest = jnp.full((1, width - 2 * cols), own_units)
        bias_row = jnp.concatenate([sums_all[0:1] * own_units, sums_all[1:2] * own_units, rest], 1)
        return up_sums + jnp.pad(bias_row, ((6, 1), (0, 0)))

    late = first_sums + second_sums
    late = late + core_swap(late)
    late_one = late + quarter_rows(back_one, up_sum_one)
    late = late_one + chip_swap(late + quarter_rows(back_two, up_sum_two))
    for bit in bits[1:] + bits[:1]:
        late = after(late, *(ahead if bit > 1 else last_parts))
        late = late + along(late, bit)
    share = 2.0 / late[6, -1]
    late = late * share

    flags = jnp.stack([*(upper(order[0]).astype(f32) for order in orders), share])
    wi_grad, wo_grad = last_doubling(last_parts, last_received, flags)

    return (
        result,
        token_grad,
        late[0],
        late[1],
        wi_grad,
        late[6, : 2 * cols].reshape(2, cols),
        wo_grad,
        late[4],
        late[2],
        late[3],
        up_sum.astype(f32) * share,
        late[7],
        down_sum.astype(f32) * share,
        late[5],
    )


def solution(mesh):
    in_specs = (
        P(("dp", "mp"), None),
        P(("dp", "mp"), None),
        P("dp"),
        P("dp"),
        P(),
        P(),
        P(),
        P(None, None, "mp"),
        P(None, "mp"),
        P("mp", None),
        P(),
        P(),
        P(),
        P(None, "mp"),
        P("mp"),
        P("mp", None),
        P(),
    )
    out_specs = (
        P(("dp", "mp"), None),
        P(("dp", "mp"), None),
        P(),
        P(),
        P(None, None, "mp"),
        P(None, "mp"),
        P("mp", None),
        P(),
        P(),
        P(),
        P(None, "mp"),
        P("mp"),
        P("mp", None),
        P(),
    )
    return jax.shard_map(body, mesh=mesh, in_specs=in_specs, out_specs=out_specs, check_vma=False)
```

```python
import jax
import jax.numpy as jnp
from jax import lax
from jax.experimental import pallas as pl
from jax.experimental.pallas import tpu as pltpu
from jax.sharding import PartitionSpec as P

HEAD_DIM = 64
LANES = 128
norm_eps = 1e-06
SCALE = HEAD_DIM**-0.5
LOG2E = 1.4426950408889634
RSQRT2 = 0.7071067811865476
RSQRT2PI = 0.3989422804014327

bf16 = jnp.bfloat16
f32 = jnp.float32
NN = (((1,), (0,)), ((), ()))
NT = (((1,), (1,)), ((), ()))
TN = (((0,), (0,)), ((), ()))
VMEM_BYTES = 63 << 20


def dot(left, right, dims=NN):
    return lax.dot_general(left, right, dims, preferred_element_type=f32)


def shape(dims, dtype):
    return jax.ShapeDtypeStruct(dims, dtype)


def whole(array):
    rank = len(array.shape)
    return pl.BlockSpec(array.shape, lambda *_: (0,) * rank, pipeline_mode=pl.Buffered(1))


def scalars():
    return pl.BlockSpec(memory_space=pltpu.SMEM)


def call(kernel, name, grid, in_specs, out_specs, out_shape, scratch=(), flops=0, nbytes=0, exps=0, weight=1e-6, aliases=None):
    return pl.pallas_call(
        kernel,
        name=name,
        grid=grid,
        in_specs=in_specs,
        out_specs=out_specs,
        out_shape=out_shape,
        scratch_shapes=list(scratch),
        input_output_aliases=aliases or {},
        compiler_params=pltpu.CompilerParams(vmem_limit_bytes=VMEM_BYTES),
        cost_estimate=pl.CostEstimate(
            flops=int(flops * weight), bytes_accessed=int(nbytes * weight), transcendentals=int(exps * weight)
        ),
    )


def split_two(values):
    high = values.astype(bf16)
    return high, (values - high.astype(f32)).astype(bf16)


def split_three(values):
    high = values.astype(bf16)
    rest = values - high.astype(f32)
    mid = rest.astype(bf16)
    return high, mid, (rest - mid.astype(f32)).astype(bf16)


def stat_rows(vector, rows):
    high, mid, rest = (part.astype(f32) for part in split_three(vector))
    row = lax.broadcasted_iota(jnp.int32, (rows, vector.shape[1]), 0)
    return jnp.where(
        row == 0, high, jnp.where(row == 1, mid, jnp.where(row == 2, rest, 0.0))
    ).astype(bf16)


def normalize(values):
    centered = values - jnp.mean(values, axis=-1, keepdims=True)
    variance = jnp.mean(centered * centered, axis=-1, keepdims=True)
    inverse = lax.rsqrt(variance + norm_eps)
    return centered * inverse, inverse


def norm_back(grad, gain, unit, inverse):
    scaled = grad * gain
    return inverse * (
        scaled
        - jnp.mean(scaled, axis=-1, keepdims=True)
        - unit * jnp.mean(scaled * unit, axis=-1, keepdims=True)
    )


def add_rows(ref, rows, first, start):
    @pl.when(first)
    def _():
        ref[...] = jnp.zeros_like(ref)

    for place, row in enumerate(rows):
        ref[start + place : start + place + 1, :] += row


def first_norm(tokens, gain, shift):
    rows, width = tokens.shape
    block = 256

    def kernel(tok_ref, gain_ref, shift_ref, norm_ref):
        unit, _ = normalize(tok_ref[...].astype(f32))
        gain_row = gain_ref[...].reshape(1, width)
        norm_ref[...] = (unit * gain_row + shift_ref[...].reshape(1, width)).astype(bf16)

    spec = pl.BlockSpec((block, width), lambda i: (i, 0))
    return call(
        kernel,
        "first_norm",
        (rows // block,),
        [spec, whole(gain), whole(shift)],
        spec,
        shape((rows, width), bf16),
        flops=20 * rows * width,
        nbytes=4 * rows * width,
    )(tokens, gain, shift)


def halves(block, width, count):
    own = pl.BlockSpec((block, width), lambda i, *_: (jnp.minimum(i, count - 1), 0))
    other = pl.BlockSpec((block, width), lambda i, *_: (jnp.maximum(i - count, 0), 0))
    return own, other


def pick(count, own_ref, other_ref):
    return jnp.where(pl.program_id(0) < count, own_ref[...], other_ref[...])


def project(norm, weight, bias, earlier=None):
    rows, width = norm.shape
    cols = weight.shape[2]
    block = 512
    start = 0 if earlier is None else rows // block
    skip = 0 if earlier is None else 3

    def kernel(x_ref, w_ref, b_ref, *refs):
        q_ref, k_ref, v_ref = refs[skip:]
        x = x_ref[...]
        q_ref[...] = (dot(x, w_ref[0]) + b_ref[0:1, :]).astype(bf16)
        k_ref[...] = dot(x, w_ref[1]).astype(bf16)
        v_ref[...] = (dot(x, w_ref[2]) + b_ref[1:2, :]).astype(bf16)

    out = pl.BlockSpec((block, cols), lambda i: (i + start, 0))
    return call(
        kernel,
        "project",
        (rows // block,),
        [pl.BlockSpec((block, width), lambda i: (i, 0)), whole(weight), whole(bias)]
        + [pl.BlockSpec(memory_space=pl.ANY)] * skip,
        [out] * 3,
        [shape((2 * rows, cols), bf16)] * 3,
        flops=6 * rows * width * cols,
        nbytes=2 * rows * width + 6 * width * cols + 6 * rows * cols,
        weight=1000,
        aliases={3 + k: k for k in range(skip)},
    )(norm, weight, bias, *(earlier or ()))


def project_both(norm_own, norm_other, weight, bias):
    rows, width = norm_own.shape
    cols = weight.shape[2]
    block = 512
    count = rows // block

    def kernel(own_ref, other_ref, w_ref, b_ref, q_ref, k_ref, v_ref):
        x = pick(count, own_ref, other_ref)
        q_ref[...] = (dot(x, w_ref[0]) + b_ref[0:1, :]).astype(bf16)
        k_ref[...] = dot(x, w_ref[1]).astype(bf16)
        v_ref[...] = (dot(x, w_ref[2]) + b_ref[1:2, :]).astype(bf16)

    out = pl.BlockSpec((block, cols), lambda i: (i, 0))
    return call(
        kernel,
        "project_both",
        (2 * count,),
        [*halves(block, width, count), whole(weight), whole(bias)],
        [out] * 3,
        [shape((2 * rows, cols), bf16)] * 3,
        flops=12 * rows * width * cols,
        nbytes=4 * rows * width + 6 * width * cols + 12 * rows * cols,
        weight=1000,
    )(norm_own, norm_other, weight, bias)


def attend_forward(queries, keys, values):
    rows, width = queries.shape
    chunk = min(512, rows)

    def kernel(q_ref, k_ref, v_ref, own_ref, other_ref, ot_ref, lse_ref):
        k = k_ref[...]
        lane = lax.broadcasted_iota(jnp.int32, k.shape, 1)
        rolled = pltpu.roll(k.astype(f32), HEAD_DIM, 1).astype(bf16)
        turned = v_ref[...].astype(f32).T
        ones = jnp.ones((HEAD_DIM, rows), bf16)
        q_turned = q_ref[...].astype(f32).T * (SCALE * LOG2E)
        outs = []
        for head in range(2):
            at = head * HEAD_DIM
            k_two = jnp.where(lane < HEAD_DIM, k, rolled) if head == 0 else jnp.where(lane < HEAD_DIM, rolled, k)
            own = turned[at : at + HEAD_DIM].astype(bf16)
            v_turned = jnp.concatenate([own, ones] if head == 0 else [ones, own], 0)
            q_two = jnp.concatenate(split_two(q_turned[at : at + HEAD_DIM]), 0)
            total = peak = None
            for j in range(rows // chunk):
                part = slice(j * chunk, (j + 1) * chunk)
                scores = dot(k_two[part], q_two)
                top = jnp.max(scores.reshape(chunk // 8, 8, rows).max(axis=0), axis=0, keepdims=True)
                higher = top if peak is None else jnp.maximum(peak, top)
                weights = jnp.exp2(scores - higher).astype(bf16)
                add = dot(v_turned[:, part], weights)
                total = add if total is None else total * jnp.exp2(peak - higher) + add
                peak = higher
            row_sum = total[HEAD_DIM - at : HEAD_DIM - at + 1]
            outs.append(total[at : at + HEAD_DIM] / row_sum)
            lse_ref[head : head + 1, :] = peak + jnp.log2(row_sum)
        attended = jnp.concatenate(outs, 0)
        ot_ref[...] = attended
        own_ref[...] = attended[:, : rows // 2].T.astype(bf16)
        other_ref[...] = attended[:, rows // 2 :].T.astype(bf16)

    by_pair = pl.BlockSpec((rows, LANES), lambda j: (0, j))
    by_half = pl.BlockSpec((rows // 2, LANES), lambda j: (0, j))
    pairs = width // LANES
    return call(
        kernel,
        "attend_forward",
        (pairs,),
        [by_pair] * 3,
        [
            by_half,
            by_half,
            pl.BlockSpec((LANES, rows), lambda j: (j, 0)),
            pl.BlockSpec((None, 8, rows), lambda j: (j, 0, 0)),
        ],
        [shape((rows // 2, width), bf16)] * 2
        + [shape((width, rows), f32), shape((pairs, 8, rows), f32)],
        flops=16 * rows * rows * width,
        nbytes=12 * rows * width,
        exps=rows * rows * width // HEAD_DIM,
        weight=1000,
    )(queries, keys, values)


def attend_backward(queries, keys, values, grad_own, grad_other, out_turned, stats, first, pairs):
    rows = queries.shape[0]
    width = LANES * pairs
    block = grad_own.shape[0]
    chunk = 256
    count = rows // block

    def kernel(
        q_ref, k_ref, v_ref, go_ref, gt_ref, ot_ref, lse_ref, d_ref, sum_ref,
        k_wide, k_turned, v_wide, dk_acc, dv_acc,
    ):
        i = pl.program_id(1)

        @pl.when(i == 0)
        def _():
            k = k_ref[...]
            v = v_ref[...]
            lane = lax.broadcasted_iota(jnp.int32, k.shape, 1)
            k_rolled = pltpu.roll(k.astype(f32), HEAD_DIM, 1).astype(bf16)
            v_rolled = pltpu.roll(v.astype(f32), HEAD_DIM, 1).astype(bf16)
            ones = jnp.where(lane < 3, 1.0, 0.0).astype(bf16)
            k_wide[0] = jnp.concatenate([jnp.where(lane < HEAD_DIM, k, k_rolled), ones], 1)
            k_wide[1] = jnp.concatenate([jnp.where(lane < HEAD_DIM, k_rolled, k), ones], 1)
            tail = jnp.where(lane < HEAD_DIM + 3, 1.0, 0.0).astype(bf16)
            v_wide[0] = jnp.where(lane < HEAD_DIM, v, tail)
            v_wide[1] = jnp.where(lane < HEAD_DIM, v_rolled, tail)
            k_turned[...] = k.astype(f32).T.astype(bf16)
            dk_acc[...] = jnp.zeros_like(dk_acc)
            dv_acc[...] = jnp.zeros_like(dv_acc)
            sum_ref[...] = jnp.zeros_like(sum_ref)

        q_turned = q_ref[...].astype(f32).T
        q_low = q_turned.astype(bf16)
        q_turned = q_turned * (SCALE * LOG2E)
        g_turned = jnp.where(i == 0, go_ref[...], gt_ref[...]).astype(f32).T
        g_low = g_turned.astype(bf16)
        dqs = []
        for head in range(2):
            part = slice(head * HEAD_DIM, (head + 1) * HEAD_DIM)
            q_wide = jnp.concatenate(
                [*split_two(q_turned[part]), stat_rows(-lse_ref[head : head + 1, :], LANES)], 0
            )
            row_dot = jnp.sum(g_turned[part] * ot_ref[part, :], axis=0, keepdims=True)
            g_wide = jnp.concatenate([g_low[part], stat_rows(-row_dot, HEAD_DIM)], 0)
            dq = None
            for j in range(rows // chunk):
                at = pl.ds(j * chunk, chunk)
                probabilities = jnp.exp2(dot(k_wide[head, at, :], q_wide))
                shifted = dot(v_wide[head, at, :], g_wide)
                probs_low = probabilities.astype(bf16)
                score_grad = (probabilities * shifted).astype(bf16)
                dv_acc[part, at] += dot(g_low[part], probs_low, NT)
                dk_acc[part, at] += dot(q_low[part], score_grad, NT)
                add = dot(k_turned[part, at], score_grad)
                dq = add if dq is None else dq + add
            dqs.append(dq)
        dq = (jnp.concatenate(dqs, 0) * SCALE).T
        d_ref[pl.ds(i * block, block), :LANES] = dq.astype(bf16)
        sum_ref[0:1, :] += jnp.sum(dq, axis=0, keepdims=True)

        @pl.when(i == count - 1)
        def _():
            d_ref[:, LANES : 2 * LANES] = (dk_acc[...] * SCALE).T.astype(bf16)
            dv = dv_acc[...].T
            d_ref[:, 2 * LANES :] = dv.astype(bf16)
            sum_ref[1:2, :] = jnp.sum(dv, axis=0, keepdims=True)

    by_query = pl.BlockSpec((block, LANES), lambda j, i: (i, j + first))
    by_key = pl.BlockSpec((rows, LANES), lambda j, i: (0, j + first))
    half = pl.BlockSpec((block, LANES), lambda j, i: (0, j + first))
    turned_spec = pl.BlockSpec((LANES, block), lambda j, i: (j + first, i))
    stat_spec = pl.BlockSpec((None, 8, block), lambda j, i: (j + first, 0, i))
    out_spec = pl.BlockSpec((None, rows, 3 * LANES), lambda j, i: (j, 0, 0))
    sum_spec = pl.BlockSpec((8, LANES), lambda j, i: (0, j))
    return call(
        kernel,
        "attend_backward",
        (pairs, count),
        [by_query, by_key, by_key, half, half, turned_spec, stat_spec],
        [out_spec, sum_spec],
        [shape((pairs, rows, 3 * LANES), bf16), shape((8, width), f32)],
        [
            pltpu.VMEM((2, rows, 2 * LANES), bf16),
            pltpu.VMEM((LANES, rows), bf16),
            pltpu.VMEM((2, rows, LANES), bf16),
            pltpu.VMEM((LANES, rows), f32),
            pltpu.VMEM((LANES, rows), f32),
        ],
        flops=40 * rows * rows * width,
        nbytes=20 * rows * width,
        exps=rows * rows * width // HEAD_DIM,
        weight=1000,
    )(queries, keys, values, grad_own, grad_other, out_turned, stats)


def output_own(tokens, attended, weights, params):
    rows, width = tokens.shape
    cols = weights[0].shape[0]
    block = 256
    many = len(attended)

    def kernel(t_ref, par_ref, *refs):
        total = None
        for a_ref, w_ref in zip(refs[:many], refs[many : 2 * many], strict=True):
            part = dot(a_ref[...], w_ref[...])
            total = part if total is None else total + part
        mid_ref, norm_ref = refs[2 * many :]
        middle = t_ref[...].astype(f32) + total + par_ref[2:3, :]
        mid_ref[...] = middle
        unit, _ = normalize(middle)
        norm_ref[...] = (unit * par_ref[3:4, :] + par_ref[4:5, :]).astype(bf16)

    spec = pl.BlockSpec((block, width), lambda i: (i, 0))
    thin = pl.BlockSpec((block, cols), lambda i: (i, 0))
    return call(
        kernel,
        "output_own",
        (rows // block,),
        [spec, whole(params)] + [thin] * many + [whole(w) for w in weights],
        [spec, spec],
        [shape((rows, width), f32), shape((rows, width), bf16)],
        flops=2 * rows * many * cols * width,
        nbytes=2 * rows * many * cols + 8 * rows * width,
    )(tokens, params, *attended, *weights)


def feed_forward(norm_own, norm_other, cot_own, cot_other, bias, up, down, scal, earlier=None):
    rows, width = norm_own.shape
    hidden = bias.shape[1]
    block = 512
    count = rows // block
    last = earlier is not None
    (up, up_place), (down, down_place) = up, down
    slices, depth = up.shape[0], up.shape[2]
    def kernel(scal_ref, no_ref, nt_ref, co_ref, ct_ref, b_ref, up_ref, dn_ref, *refs):
        if last:
            ng_in, act_ref, ngo_ref, nga_ref, ngb_ref, *refs = refs
        else:
            act_ref, ng_ref, *refs = refs
        keep, send, sum_ref, up_acc, down_acc = refs
        i = pl.program_id(0)

        @pl.when(i == 0)
        def _():
            up_acc[...] = jnp.zeros_like(up_acc)
            down_acc[...] = jnp.zeros_like(down_acc)
            sum_ref[...] = jnp.zeros_like(sum_ref)

        x = pick(count, no_ref, nt_ref)
        cot = (pick(count, co_ref, ct_ref).astype(f32) * scal_ref[0]).astype(bf16)
        up_now = up_ref[...].reshape(width, hidden)
        down_now = dn_ref[...].reshape(hidden, width)
        h = dot(x, up_now) + b_ref[0:1, :]
        cdf = 0.5 * (1.0 + lax.erf(h * RSQRT2))
        act = (h * cdf).astype(bf16)
        slope = cdf + h * (RSQRT2PI * jnp.exp(-0.5 * h * h))
        act_ref[...] = act
        grad = dot(cot, down_now, NT) * slope
        sum_ref[7:8, :] += jnp.sum(grad, axis=0, keepdims=True)
        low = grad.astype(bf16)
        ng = dot(low, up_now, NT)
        up_acc[...] += dot(x, low, TN)
        down_acc[...] += dot(act, cot, TN)
        if last:
            ng = ng + ng_in[...].astype(f32)

            @pl.when(i < count)
            def _():
                ngo_ref[...] = ng.astype(bf16)

            @pl.when((i >= count) & (i < count + count // 2))
            def _():
                nga_ref[...] = ng.astype(bf16)

            @pl.when(i >= count + count // 2)
            def _():
                ngb_ref[...] = ng.astype(bf16)
        else:
            ng_ref[...] = ng.astype(bf16)

        @pl.when(i == 2 * count - 1)
        def _():
            units = scal_ref[1]

            @pl.when(scal_ref[2] < 0.5)
            def _():
                keep[...] = (up_acc[...] * units).astype(bf16)
                send[...] = (down_acc[...] * units).astype(bf16)

            @pl.when(scal_ref[2] > 0.5)
            def _():
                keep[...] = (down_acc[...] * units).astype(bf16)
                send[...] = (up_acc[...] * units).astype(bf16)

            sum_ref[...] = sum_ref[...] * units

    own, other = halves(block, width, count)
    every = pl.BlockSpec((block, width), lambda i: (i, 0))
    up_spec, down_spec = (
        pl.BlockSpec(
            (slices, None, depth, width), lambda i, j=j: (0, j, 0, 0), pipeline_mode=pl.Buffered(1)
        )
        for j in (up_place, down_place)
    )
    ins = [scalars(), own, other, own, other, whole(bias), up_spec, down_spec]
    args = [scal, norm_own, norm_other, cot_own, cot_other, bias, up, down]
    outs = [every]
    shapes = [shape((2 * rows, hidden), bf16)]
    if last:
        ins += [every]
        args += [earlier]
        half = count // 2
        top = pl.BlockSpec((block, width), lambda i: (jnp.clip(i - count, 0, half - 1), 0))
        low = pl.BlockSpec((block, width), lambda i: (jnp.maximum(i - count - half, 0), 0))
        outs += [own, top, low]
        shapes += [shape((rows, width), bf16)] + [shape((rows // 2, width), bf16)] * 2
    else:
        outs += [every]
        shapes += [shape((2 * rows, width), bf16)]
    assert width == hidden
    terms = [shape((width, hidden), bf16)] * 2
    sums = shape((8, hidden), f32)
    return call(
        kernel,
        "feed_forward",
        (2 * count,),
        ins,
        outs + [whole(terms[0]), whole(terms[1]), whole(sums)],
        shapes + terms + [sums],
        [pltpu.VMEM((width, hidden), f32), pltpu.VMEM((hidden, width), f32)],
        flops=20 * rows * width * hidden,
        nbytes=24 * rows * width + 12 * width * hidden,
        exps=4 * rows * hidden,
        weight=1000 if last else 1e-6,
    )(*args)


def second_back(middle, grad_own, grad_received, cot, params, scal):
    rows, width = middle.shape
    block = 256
    half = rows // block // 2
    last = rows // block - 1

    def kernel(scal_ref, mid_ref, go_ref, ga_ref, gb_ref, cot_ref, par_ref, low_ref, sum_ref):
        i = pl.program_id(0)
        unit, inverse = normalize(mid_ref[...])
        grad = go_ref[...].astype(f32) + pick(half, ga_ref, gb_ref).astype(f32)
        cot = cot_ref[...].astype(f32) * scal_ref[0]
        out = cot + norm_back(grad, par_ref[3:4, :], unit, inverse)
        low_ref[...] = out.astype(bf16)
        sums = [jnp.sum(v, axis=0, keepdims=True) for v in (grad * unit, grad, out, cot)]
        add_rows(sum_ref, sums, i == 0, 2)

        @pl.when(i == last)
        def _():
            sum_ref[...] = sum_ref[...] * scal_ref[1]

    spec = pl.BlockSpec((block, width), lambda i: (i, 0))
    sums = shape((8, width), f32)
    return call(
        kernel,
        "second_back",
        (rows // block,),
        [scalars(), spec, spec, *halves(block, width, half), spec, whole(params)],
        [spec, whole(sums)],
        [shape((rows, width), bf16), sums],
        flops=30 * rows * width,
        nbytes=18 * rows * width,
    )(scal, middle, grad_own, *grad_received, cot, params)


def output_back(low, attended, weights, scal, earlier=None):
    rows, width = low.shape
    cols = weights[0].shape[0]
    block = 512
    last = earlier is not None

    def kernel(scal_ref, low_ref, a_ref, b_ref, wa_ref, wb_ref, *refs):
        before = refs[:2] if last else (None, None)
        ga_ref, gb_ref, ta_ref, tb_ref, acc_a, acc_b = refs[2 if last else 0 :]
        i = pl.program_id(0)
        now = low_ref[...]
        ga_ref[...] = dot(now, wa_ref[...], NT).astype(bf16)
        gb_ref[...] = dot(now, wb_ref[...], NT).astype(bf16)
        for acc, rows_ref, old in ((acc_a, a_ref, before[0]), (acc_b, b_ref, before[1])):

            @pl.when(i == 0)
            def _():
                acc[...] = jnp.zeros_like(acc) if old is None else old[...]

            acc[...] += dot(rows_ref[...], now, TN)

        @pl.when(i == rows // block - 1)
        def _():
            factor = scal_ref[1] if last else 1.0
            ta_ref[...] = (acc_a[...] * factor).astype(ta_ref.dtype)
            tb_ref[...] = (acc_b[...] * factor).astype(tb_ref.dtype)

    thin = pl.BlockSpec((block, cols), lambda i: (i, 0))
    terms = [shape((cols, width), bf16 if last else f32)] * 2
    before = list(earlier or ())
    return call(
        kernel,
        "output_back",
        (rows // block,),
        [scalars(), pl.BlockSpec((block, width), lambda i: (i, 0)), thin, thin]
        + [whole(w) for w in weights]
        + [whole(t) for t in before],
        [thin, thin, whole(terms[0]), whole(terms[1])],
        [shape((rows, cols), bf16)] * 2 + terms,
        [pltpu.VMEM((cols, width), f32)] * 2,
        flops=8 * rows * width * cols,
        nbytes=2 * rows * width + 8 * rows * cols,
        weight=1e-6 if last else 1000,
    )(scal, low, *attended, *weights, *before)


def side_by_side(refs):
    return jnp.concatenate([ref[p] for ref in refs for p in range(ref.shape[0])], 1)


def pair_specs(grads, block, place):
    return [
        pl.BlockSpec((g.shape[0], block, g.shape[2]), lambda i: (0, place(i), 0)) for g in grads
    ]


def input_term(norm_own, norm_other, grads, scal, other=None, outputs=(), place=None):
    rows, width = norm_own.shape
    pairs = sum(g.shape[0] for g in grads)
    cols = pairs * LANES
    many = len(grads)
    more = [] if other is None else [other, *outputs]
    quarter = width

    def kernel(scal_ref, *refs):
        place_ref = refs[0] if more else None
        no_ref, nt_ref, *refs = refs[1 if more else 0 :]
        outs, acc = refs[many + len(more) : -1], refs[-1]
        i = pl.program_id(0)
        term = dot(pick(1, no_ref, nt_ref), side_by_side(refs[:many]), TN)

        @pl.when(i == 0)
        def _():
            acc[...] = term

        def total(j, p):
            at = (3 * p + j) * LANES
            return (acc[:, at : at + LANES] + term[:, at : at + LANES]) * scal_ref[1]

        def store(half, keep, send):
            for p in range(pairs):
                lanes = slice(p * LANES, (p + 1) * LANES)
                for out_ref, j in ((keep, 2 * half), (send, 2 * half + 1)):
                    if j < 3:
                        final = total(j, p) + refs[many][j * width : (j + 1) * width, lanes].astype(f32)
                        out_ref[:, lanes] = final.astype(bf16)
                        continue
                    for k in range(width // cols):
                        at = slice(k * cols + p * LANES, k * cols + (p + 1) * LANES)
                        final = refs[many + 1][:, at].astype(f32) + refs[many + 2][:, at].astype(f32)
                        out_ref[k * cols : (k + 1) * cols, lanes] = final.astype(bf16)

        @pl.when(i == 1)
        def _():
            if not more:
                for p in range(pairs):
                    for j in range(3):
                        at = (slice(j * width, (j + 1) * width), slice(p * LANES, (p + 1) * LANES))
                        outs[0][at] = total(j, p).astype(bf16)
            for half in range(2 if more else 0):
                keep, send = outs[2 * half], outs[2 * half + 1]

                @pl.when(place_ref[half] == 0)
                def _():
                    store(half, keep, send)

                @pl.when(place_ref[half] == 1)
                def _():
                    store(half, send, keep)

    out = [shape((quarter, cols), bf16)] * 4 if more else [shape((3 * width, cols), bf16)]
    return call(
        kernel,
        "input_term",
        (2,),
        [scalars()]
        + [scalars()] * (1 if more else 0)
        + [*halves(rows, width, 1)]
        + pair_specs(grads, rows, lambda i: i)
        + [whole(m) for m in more],
        [whole(o) for o in out],
        out,
        [pltpu.VMEM((width, 3 * cols), f32)],
        flops=12 * rows * width * cols,
        nbytes=4 * rows * width + 12 * rows * cols + 12 * width * cols,
    )(scal, *([place] if more else []), norm_own, norm_other, *grads, *more)


def join_weights(refs, joined):
    @pl.when(pl.program_id(0) == 0)
    def _():
        place = 0
        for ref in refs:
            for p in range(ref.shape[2] // LANES):
                for j in range(3):
                    joined[:, place : place + LANES] = ref[j, :, p * LANES : (p + 1) * LANES]
                    place += LANES


def norm1_other(grads, weights):
    rows = grads[0].shape[1] // 2
    width, cols = weights[0].shape[1:]
    block = 512
    count = rows // block
    many = len(grads)

    def kernel(*refs):
        out_ref, joined = refs[-2:]
        join_weights(refs[many:-2], joined)
        out_ref[...] = dot(side_by_side(refs[:many]), joined[...], NT).astype(bf16)

    return call(
        kernel,
        "first_other",
        (count,),
        pair_specs(grads, block, lambda i: i + count) + [whole(w) for w in weights],
        pl.BlockSpec((block, width), lambda i: (i, 0)),
        shape((rows, width), bf16),
        [pltpu.VMEM((width, 3 * cols * len(weights)), bf16)],
        flops=12 * rows * width * cols,
        nbytes=12 * rows * cols + 2 * rows * width + 12 * width * cols,
    )(*grads, *weights)


def norm1_own(grads, weights, received, tokens, middle_grad, params, scal):
    rows, width = tokens.shape
    cols = weights[0].shape[2]
    block = 256
    last = rows // block - 1
    many = len(grads)

    def kernel(scal_ref, *refs):
        rec_ref, tok_ref, mid_ref, par_ref, out_ref, sum_ref, joined = refs[many + len(weights) :]
        i = pl.program_id(0)
        join_weights(refs[many : many + len(weights)], joined)
        grad = dot(side_by_side(refs[:many]), joined[...], NT) + rec_ref[...].astype(f32)
        unit, inverse = normalize(tok_ref[...].astype(f32))
        out = mid_ref[...].astype(f32) + norm_back(grad, par_ref[0:1, :], unit, inverse)
        out_ref[...] = out.astype(bf16)
        sums = [jnp.sum(v, axis=0, keepdims=True) for v in (grad * unit, grad)]
        add_rows(sum_ref, sums, i == 0, 0)

        @pl.when(i == last)
        def _():
            sum_ref[...] = sum_ref[...] * scal_ref[1]

    spec = pl.BlockSpec((block, width), lambda i: (i, 0))
    sums = shape((8, width), f32)
    return call(
        kernel,
        "first_own",
        (rows // block,),
        [scalars()]
        + pair_specs(grads, block, lambda i: i)
        + [whole(w) for w in weights]
        + [spec] * 3
        + [whole(params)],
        [spec, whole(sums)],
        [shape((rows, width), bf16), sums],
        [pltpu.VMEM((width, 3 * cols * len(weights)), bf16)],
        flops=12 * rows * width * cols,
        nbytes=12 * rows * cols + 10 * rows * width + 12 * width * cols,
    )(scal, *grads, *weights, received, tokens, middle_grad, params)


def down_specs(weights):
    return [
        pl.BlockSpec(
            (w.shape[0], None, *w.shape[2:]), lambda i, j=j: (0, j, 0, 0), pipeline_mode=pl.Buffered(1)
        )
        for w, j in weights
    ]


def down_product(acts, weights):
    total = None
    for a_ref, w_ref in zip(acts, weights, strict=True):
        part = dot(a_ref[...], w_ref[...].reshape(a_ref.shape[1], w_ref.shape[-1]))
        total = part if total is None else total + part
    return total


def result_other(acts, weights):
    rows, hidden = acts[0].shape
    rows = rows // 2
    width = weights[0][0].shape[-1]
    block = 512
    start = rows // block
    many = len(acts)

    def kernel(*refs):
        refs[-1][...] = down_product(refs[:many], refs[many:-1]).astype(bf16)

    return call(
        kernel,
        "result_other",
        (rows // block,),
        [pl.BlockSpec((block, hidden), lambda i: (i + start, 0))] * many + down_specs(weights),
        pl.BlockSpec((block, width), lambda i: (i, 0)),
        shape((rows, width), bf16),
        flops=2 * many * rows * hidden * width,
        nbytes=2 * many * rows * hidden,
    )(*acts, *[w for w, _ in weights])


def block_result(middle, acts, weights, received, params, scal):
    rows, width = middle.shape
    hidden = acts[0].shape[1]
    block = 256
    many = len(acts)

    def kernel(scal_ref, mid_ref, rec_ref, par_ref, *refs):
        total = mid_ref[...] + down_product(refs[:many], refs[many:-1])
        total = total + rec_ref[...].astype(f32) + par_ref[5:6, :]
        refs[-1][...] = (total * scal_ref[0]).astype(bf16)

    spec = pl.BlockSpec((block, width), lambda i: (i, 0))
    return call(
        kernel,
        "block_result",
        (rows // block,),
        [scalars(), spec, spec, whole(params)]
        + [pl.BlockSpec((block, hidden), lambda i: (i, 0))] * many
        + down_specs(weights),
        spec,
        shape((rows, width), bf16),
        flops=2 * many * rows * hidden * width,
        nbytes=12 * rows * width,
        weight=1000,
    )(scal, middle, received, params, *acts, *[w for w, _ in weights])


def add_terms(*terms):
    rows, width = terms[0].shape
    block = 512

    def kernel(*refs):
        total = refs[0][...].astype(f32)
        for ref in refs[1:-1]:
            total = total + ref[...].astype(f32)
        refs[-1][...] = total.astype(bf16)

    spec = pl.BlockSpec((block, width), lambda i: (i, 0))
    return call(
        kernel,
        "add_terms",
        (rows // block,),
        [spec] * len(terms),
        spec,
        shape((rows, width), bf16),
        flops=len(terms) * rows * width,
        nbytes=2 * (len(terms) + 1) * rows * width,
    )(*terms)


def last_doubling(owns, others, flags):
    rows, cols = owns[0].shape
    blocks = rows // cols

    def kernel(flag_ref, own_a, own_b, other_a, other_b, wi_ref, wo_ref):
        factor = flag_ref[2]

        def ordered(k, own_ref, other_ref):
            is_upper = flag_ref[k] > 0.5
            own = own_ref[...].astype(f32) * factor
            other = other_ref[...].astype(f32) * factor
            return jnp.where(is_upper, other, own), jnp.where(is_upper, own, other)

        wi_ref[0], wi_ref[1] = ordered(0, own_a, other_a)
        wi_ref[2], below = ordered(1, own_b, other_b)
        for k in range(blocks):
            wo_ref[:, k * cols : (k + 1) * cols] = below[k * cols : (k + 1) * cols, :]

    outs = [shape((3, rows, cols), f32), shape((cols, rows), f32)]
    return call(
        kernel,
        "last_doubling",
        (1,),
        [scalars()] + [whole(value) for value in (*owns, *others)],
        [whole(out) for out in outs],
        outs,
        flops=8 * rows * cols,
        nbytes=24 * rows * cols,
    )(flags, *owns, *others)


def body(
    tokens,
    out_grad,
    item_counts,
    group_dataset,
    variable_mask,
    first_gain,
    first_shift,
    input_weight,
    input_bias,
    output_weight,
    output_bias,
    second_gain,
    second_shift,
    up_weight,
    up_bias,
    down_weight,
    down_bias,
):
    shard_count = lax.axis_size("mp")
    groups = lax.axis_size("dp")
    rows, width = tokens.shape
    cols = input_weight.shape[2]
    hidden = up_weight.shape[1]

    def core_swap(value):
        return lax.ppermute(value, "mp", [(i, i ^ 1) for i in range(shard_count)])

    def chip_swap(value):
        return lax.ppermute(value, "mp", [(i, i ^ 2) for i in range(shard_count)])

    def after(value, *others):
        return lax.optimization_barrier((value, *others))[0]

    def along(value, bit):
        return lax.ppermute(value, "dp", [(i, i ^ bit) for i in range(groups)])

    group = lax.axis_index("dp")

    slice_rows = up_weight.shape[0] // groups
    slices = [
        lax.dynamic_slice_in_dim(weight, group * slice_rows, slice_rows, 0)
        for weight in (up_weight, down_weight)
    ]
    slice_two = chip_swap(jnp.stack(slices)[None])
    bias_pack = jnp.concatenate([up_bias, input_bias[0], input_bias[1]]).reshape(-1, LANES)
    bias_two = chip_swap(bias_pack)
    wi_two = chip_swap(after(input_weight, *slices))
    cot_t = core_swap(out_grad)
    normed1 = first_norm(tokens, first_gain, first_shift)
    normed1_t = core_swap(normed1)
    item_counts, variable_mask, output_bias = after(
        (item_counts, variable_mask, output_bias), normed1
    )

    live = (lax.axis_index("mp") // 2 < item_counts[0]).astype(f32)
    dataset_hit = jnp.arange(variable_mask.shape[0], dtype=jnp.int32) == group_dataset[0]
    own_units = (
        item_counts[0] * jnp.sum(jnp.where(dataset_hit[:, None], variable_mask, 0))
    ).astype(f32)
    scal = jnp.stack([live, own_units, (group % 2).astype(f32)])
    zero = jnp.zeros((width,), f32)
    params = jnp.stack(
        [first_gain, first_shift, output_bias, second_gain, second_shift, down_bias, zero, zero]
    )

    qkv_one = project(normed1, input_weight, input_bias)
    ff_weights_two = lax.all_gather(after(slice_two, qkv_one[0]), "dp", axis=0, tiled=True)
    qkv_one = project(normed1_t, input_weight, after(input_bias, qkv_one[0]), qkv_one)
    att_one, att_one_send, turned_one, stat_one = attend_forward(*qkv_one)
    att_one_t = core_swap(att_one_send)
    wo_two = chip_swap(after(output_weight, att_one))
    wo_two_t = lax.ppermute(
        after(output_weight, att_one), "mp", [(i, i ^ 3) for i in range(shard_count)]
    )
    wo_one_t = core_swap(output_weight)
    bias_two = after(bias_two, att_one).reshape(-1)
    up_bias_one = up_bias.reshape(1, hidden)
    up_bias_two = bias_two[:hidden].reshape(1, hidden)
    in_bias_two = bias_two[hidden:].reshape(2, cols)
    qkv_two = project_both(
        after(normed1, att_one), normed1_t, wi_two, after(in_bias_two, up_bias_two)
    )
    qkv_two = after(tuple(qkv_two), att_one_t, cot_t)
    att_two, att_two_send, turned_two, stat_two = attend_forward(*qkv_two)
    att_two_t = core_swap(att_two_send)
    middle, normed2 = output_own(
        tokens,
        [att_one, att_two, att_one_t, att_two_t],
        [output_weight, wo_two, wo_one_t, wo_two_t],
        params,
    )
    normed2_t = core_swap(normed2)

    act_two, ng_two, keep_two, send_two, up_sum_two = feed_forward(
        normed2, normed2_t, out_grad, cot_t, up_bias_two, (ff_weights_two, 0), (ff_weights_two, 1), scal
    )
    two_received = along(send_two, 1)
    up_one, down_one = ((w.reshape(1, 1, -1, width), 0) for w in (up_weight, down_weight))
    act_one, ng_own, *ng_sends, keep_one, send_one, up_sum_one = feed_forward(
        normed2, normed2_t, out_grad, cot_t, up_bias_one, up_one, down_one, scal, ng_two
    )
    one_received = along(send_one, 1)
    ng_received = [core_swap(ng_send) for ng_send in ng_sends]
    middle_low, second_sums = second_back(
        middle, ng_own, ng_received, out_grad, params, scal
    )
    pair_two = add_terms(keep_two, after(two_received, middle_low))
    pair_received = chip_swap(pair_two)
    middle_low_t = core_swap(middle_low)
    middle_low = after(middle_low, pair_two)
    out_weights = [output_weight, wo_two]
    g_one, g_two, *wo_terms = output_back(
        middle_low, [att_one, att_two], out_weights, scal
    )
    g_one_t, g_two_t, wo_one_term, wo_two_term = output_back(
        middle_low_t, [att_one_send, att_two_send], out_weights, scal, wo_terms
    )

    def both(own, received, *last):
        return (own.astype(f32) + after(received, *last).astype(f32)).astype(bf16)

    back_two = [attend_backward(*qkv_two, g_two, g_two_t, turned_two, stat_two, 0, 1)]
    wait = back_two[0][0]
    acts = [act_two, act_one]
    downs = [(ff_weights_two, 1), down_one]
    result_send = result_other([after(act_two, wait), act_one], downs)
    result_received = core_swap(result_send)
    ff_both = add_terms(keep_one, one_received, after(pair_received, wait, result_send))
    ff_sum = lax.psum(
        ff_both, "dp", axis_index_groups=[list(range(k, groups, 2)) for k in range(2)]
    )
    back_two.append(
        attend_backward(
            *qkv_two, after(g_two, ff_both), g_two_t, turned_two, stat_two, 1, cols // LANES - 1
        )
    )
    grads_two = [back[0] for back in back_two]
    wi_two_term = input_term(normed1, normed1_t, grads_two, scal)[0]
    wo_received = chip_swap(after(wo_two_term, grads_two[1]))
    wi_received = chip_swap(wi_two_term)
    g_one = after(g_one, wi_two_term)
    back_one = [attend_backward(*qkv_one, g_one, g_one_t, turned_one, stat_one, 0, cols // LANES)]
    grads_one = [back[0] for back in back_one]

    bits = [1 << k for k in range(groups.bit_length() - 1)]
    orders = [bits, bits[1:2] + bits[:1] + bits[2:]]

    def upper(bit):
        return (group // bit) % 2

    def split(part, bit, axis=0):
        half = part.shape[axis] // 2
        return (
            lax.dynamic_slice_in_dim(part, upper(bit) * half, half, axis),
            lax.dynamic_slice_in_dim(part, (1 - upper(bit)) * half, half, axis),
        )

    place = jnp.stack([upper(order[0]) for order in orders]).astype(jnp.int32)
    keep_a, send_a, keep_b, send_b = input_term(
        normed1, normed1_t, grads_one, scal, wi_received, (wo_one_term, wo_received), place
    )
    keeps, sends = (keep_a, keep_b), (send_a, send_b)
    received = [along(sends[k], orders[k][0]) for k in range(2)]

    grads = grads_one + grads_two
    weights = [input_weight, wi_two]
    ng1_received = core_swap(norm1_other(grads, [input_weight, after(wi_two, *sends)]))
    parts = [both(keeps[k], received[k]) for k in range(2)]
    keeps, sends = zip(*[split(parts[k], orders[k][1]) for k in range(2)], strict=True)
    received = [along(sends[k], orders[k][1]) for k in range(2)]
    ff_sum_other = along(after(ff_sum, *sends), 1)
    result = block_result(after(middle, *sends), acts, downs, result_received, params, scal)
    merged = jnp.stack([both(keeps[k], received[k], result) for k in range(2)])
    later = bits[2:]
    for bit in later:
        keep, send = split(merged, bit, 1)
        received = along(send, bit)
        wait = []
        if bit == later[-1]:
            token_grad, first_sums = norm1_own(
                grads, weights, ng1_received, after(tokens, send), middle_low, params, scal
            )
            wait = [token_grad]
        merged = both(keep, received, *wait)
    first_sums = after(first_sums, merged)

    def double(part, received, bit, axis):
        is_upper = upper(bit) == 1
        pair = [jnp.where(is_upper, received, part), jnp.where(is_upper, part, received)]
        return jnp.concatenate(pair, axis)

    for bit in reversed(later):
        merged = double(merged, along(merged, bit), bit, 1)
    parts = [merged[0], merged[1]]
    parts[1] = after(parts[1], ff_sum_other)
    ahead = parts
    parts = [double(parts[k], along(parts[k], orders[k][1]), orders[k][1], 0) for k in range(2)]
    last_parts = parts
    last_received = [along(parts[k], orders[k][0]) for k in range(2)]

    lower = group % 2 == 0
    up_sum = jnp.where(lower, ff_sum, ff_sum_other)
    down_sum = jnp.where(lower, ff_sum_other, ff_sum)

    def quarter_rows(parts, up_sums):
        sums_all = jnp.concatenate([part[1] for part in parts], 1)
        rest = jnp.full((1, width - 2 * cols), own_units)
        bias_row = jnp.concatenate([sums_all[0:1] * own_units, sums_all[1:2] * own_units, rest], 1)
        return up_sums + jnp.pad(bias_row, ((6, 1), (0, 0)))

    late = first_sums + second_sums
    late = late + core_swap(late)
    late_one = late + quarter_rows(back_one, up_sum_one)
    late = late_one + chip_swap(late + quarter_rows(back_two, up_sum_two))
    for bit in bits[1:] + bits[:1]:
        late = after(late, *(ahead if bit > 1 else last_parts))
        late = late + along(late, bit)
    share = 2.0 / late[6, -1]
    late = late * share

    flags = jnp.stack([*(upper(order[0]).astype(f32) for order in orders), share])
    wi_grad, wo_grad = last_doubling(last_parts, last_received, flags)

    return (
        result,
        token_grad,
        late[0],
        late[1],
        wi_grad,
        late[6, : 2 * cols].reshape(2, cols),
        wo_grad,
        late[4],
        late[2],
        late[3],
        up_sum.astype(f32) * share,
        late[7],
        down_sum.astype(f32) * share,
        late[5],
    )


def solution(mesh):
    in_specs = (
        P(("dp", "mp"), None),
        P(("dp", "mp"), None),
        P("dp"),
        P("dp"),
        P(),
        P(),
        P(),
        P(None, None, "mp"),
        P(None, "mp"),
        P("mp", None),
        P(),
        P(),
        P(),
        P(None, "mp"),
        P("mp"),
        P("mp", None),
        P(),
    )
    out_specs = (
        P(("dp", "mp"), None),
        P(("dp", "mp"), None),
        P(),
        P(),
        P(None, None, "mp"),
        P(None, "mp"),
        P("mp", None),
        P(),
        P(),
        P(),
        P(None, "mp"),
        P("mp"),
        P("mp", None),
        P(),
    )
    return jax.shard_map(body, mesh=mesh, in_specs=in_specs, out_specs=out_specs, check_vma=False)
```
